128 devices in a mesh: rep: 16 (over y, z), tp: 8 (over x, core).
Axes of the slice: x: 4, y: 4, z: 4, core: 2. Of those that a mesh axis runs over, the one named last changes fastest.
Arguments:
- hidden: bfloat16 [16384, 5120], P('rep', 'tp'), may hold values from -6 to 6
- ref_gain: float32 [5120], replicated, may hold values from 0.1 to 1.9
- ref_wq: bfloat16 [5120, 4096], P(None, 'tp'), may hold values from -2 to 2
- ref_wkv: bfloat16 [5120, 2, 1024], P(None, None, 'tp'), may hold values from -0.078125 to 0.078125
- ref_wo: bfloat16 [4096, 5120], P('tp'), may hold values from -0.09375 to 0.09375
- score_vec: float32 [5120], replicated, may hold values from -0.078125 to 0.078125
- lengths: int32 [16, 8], P('rep'), may hold values from 1 to 512, 1024 in all within a row
- advantage: float32 [16, 8], P('rep'), may hold values from -4 to 4
- dest: int32 [16384], P(('rep', 'tp')), may hold values from 0 to 127, as said below
- policy_norm_gain: float32 [5120], replicated, may hold values from 0.1 to 1.9
- pol_w: bfloat16 [5120, 512], P(('rep', 'tp')), may hold values from -0.078125 to 0.078125
- cotangent: bfloat16 [16384, 512], P(('rep', 'tp')), may hold values from -6 to 6
Outputs:
- policy_input_gradient: bfloat16 [16384, 5120], P(('rep', 'tp'))
- grad_weight: float32 [5120, 512], P(('rep', 'tp'))
- policy_gain_gradient: float32 [5120], P(('rep', 'tp'))
The draws below stay inside these ranges and needn't reach their ends.
Inputs may be any that keep to these rules, and one draw needn't show every extreme that they name: `dest`: each aligned block of 128 tokens is cut into 16 runs of 8 consecutive tokens with one destination each; the runs of one block go to distinct devices, and every device receives exactly 16 runs in all.
All inputs are finite; a program needn't handle non-finite values.
Results may differ from the reference program's by a relative error of at most 0.014.
The reference program's roundings to bfloat16 on the way count: a program that leaves them out, or rounds other values in their place, can miss the bound.
Values may be sent and summed in bfloat16 or wider, within the bound.
No kernel may reach another device: no remote copies, remote signals or barrier semaphores. Data moves between devices by JAX's collectives and lax.ppermute only.
A program may use at most 192 MiB of HBM per device.

```python
import math
import jax
import jax.numpy as jnp
import numpy as np
from jax import lax

D = 5120
QH = 32
KVH = 8
HD = 128
SEQS = 8
RUNS_DEV = 16
RUN = 8
REP_ROWS = 1024
TOKENS = 16384
LMAX = 512
E = 512
N_REP = 16
N_TP = 8


def draw_dest(key, part):
    key = jax.random.fold_in(key, 11)
    devices = N_REP * N_TP
    first, second, third = jax.random.split(key, 3)
    relabel = jax.random.permutation(first, devices).astype(jnp.int32)
    offsets = jax.random.permutation(second, devices)[:RUNS_DEV].astype(jnp.int32)
    run_keys = jax.random.split(third, devices)
    slots = jax.vmap(lambda k: jax.random.permutation(k, RUNS_DEV))(run_keys).astype(jnp.int32)
    senders = jnp.arange(devices, dtype=jnp.int32)[:, None]
    run_dest = relabel[(senders + offsets[slots]) % devices]
    return jnp.repeat(run_dest, RUN, axis=1).reshape(-1).astype(jnp.int32)


def draw_ref_wq(key, part):
    key = jax.random.fold_in(key, 5)
    base = jax.random.normal(key, (D, QH * HD), jnp.float32) / jnp.sqrt(jnp.float32(D))
    return base.astype(jnp.bfloat16)


def level_of(own_key, shape, cuts, smallest, high):
    factor_of = 1.0
    for dim, blocks in cuts:
        draws = jax.random.uniform(jax.random.fold_in(jax.random.fold_in(own_key, 6), dim), (blocks,), jnp.float32, smallest / len(cuts), high / len(cuts))
        factor_of = factor_of * jnp.repeat(jnp.exp(draws), shape[dim] // blocks).reshape((-1,) + (1,) * (len(shape) - 1 - dim))
    return factor_of


def length_profile(amount, total, most, slope):
    weights = [(1 << 20) // math.isqrt(rank ** slope) + 1 for rank in range(2, amount + 1)]
    surplus, holding = total - most - (amount - 1), [1] * (amount - 1)
    while surplus > 0:
        movable = [i for i in range(amount - 1) if holding[i] < most]
        whole, budget = sum([weights[i] for i in movable]), surplus
        for i in movable:
            more = min(most - holding[i], max(1, budget * weights[i] // whole), surplus)
            holding[i] = holding[i] + more
            surplus = surplus - more
    return np.array([most] + holding)


def ragged(own_key, number_of, total, reach, slope):
    if number_of == 2:
        one = jax.random.randint(own_key, (), max(1, total - reach), min(reach, total - 1) + 1)
        return jnp.stack([one, total - one])
    tallies = jnp.asarray(length_profile(number_of, total, reach, slope), jnp.int32)
    couples = (number_of - 1) // 2
    donor, sink = tallies[1:1 + 2 * couples:2], tallies[2:2 + 2 * couples:2]
    margin = jnp.minimum(donor - 1, reach - sink)
    moved = jax.random.randint(jax.random.fold_in(own_key, 1), (couples,), 0, 1 << 20) % (margin + 1)
    tallies = tallies.at[1:1 + 2 * couples:2].set(donor - moved).at[2:2 + 2 * couples:2].set(sink + moved)
    return tallies[jax.random.permutation(jax.random.fold_in(own_key, 2), number_of)]


def bell_draw(stream_key, shape, width, limit, pieces=(), kind=jnp.bfloat16):
    gain = level_of(stream_key, shape, pieces, -0.22, 0.18) if pieces else 1.0
    values = jax.random.normal(stream_key, shape, jnp.float32) * width * gain
    return jnp.minimum(jnp.maximum(values, -limit), limit).astype(kind)


def setup_inputs(seed: int = 0) -> dict:
    key_of = jax.random.split(jax.random.key(seed), 13)
    return {
        "hidden": bell_draw(key_of[0], (TOKENS, D), 1.0, 6.0, ((0, 16), (1, 8))),
        "ref_gain": jnp.clip(1.0 + 0.18 * jax.random.normal(key_of[1], (D,), jnp.float32), 0.1, 1.9),
        "ref_wq": draw_ref_wq(jax.random.fold_in(key_of[12], 71), 0),
        "ref_wkv": bell_draw(key_of[3], (D, 2, KVH * HD), D ** -0.5, 0.078125, ((2, 8),)),
        "ref_wo": bell_draw(key_of[4], (QH * HD, D), (QH * HD) ** -0.5, 0.09375, ((0, 8),)),
        "score_vec": bell_draw(key_of[5], (D,), D ** -0.5, 0.078125, (), jnp.float32),
        "lengths": jax.vmap(lambda own: ragged(own, SEQS, REP_ROWS, LMAX, 2))(jax.random.split(key_of[6], N_REP)).reshape((N_REP, SEQS)).astype(jnp.int32),
        "advantage": bell_draw(key_of[7], (N_REP, SEQS), 1.0, 4.0, ((0, 16),), jnp.float32),
        "dest": draw_dest(jax.random.fold_in(key_of[12], 71), 0),
        "policy_norm_gain": jnp.clip(1.0 + 0.18 * jax.random.normal(key_of[9], (D,), jnp.float32), 0.1, 1.9),
        "pol_w": bell_draw(key_of[10], (D, E), D ** -0.5, 0.078125, ((0, 128),)),
        "cotangent": bell_draw(key_of[11], (TOKENS, E), 1.0, 6.0, ((0, 128),)),
    }


def rms_scale(v):
    return lax.rsqrt(lax.optimization_barrier(jnp.mean(v * v, axis=-1, keepdims=True)) + 1e-06)

def replica_weights(x_rep, lens, adv, ref_gain, ref_wq, ref_wkv, ref_wo, score_vec):
    rows = x_rep.shape[0]
    input_float = x_rep.astype(jnp.float32)
    xn = (input_float * rms_scale(input_float) * ref_gain).astype(jnp.bfloat16)
    q = jnp.dot(xn, ref_wq, preferred_element_type=jnp.float32).astype(jnp.bfloat16)
    kv = jnp.dot(xn, ref_wkv.reshape(D, 2 * KVH * HD), preferred_element_type=jnp.float32).astype(jnp.bfloat16)
    keys = kv[:, :KVH * HD].reshape(rows, KVH, HD)
    values = kv[:, KVH * HD:].reshape(rows, KVH, HD)
    group = QH // KVH
    queries = q.reshape(rows, KVH, group, HD)
    ends = jnp.cumsum(lens)
    pos = jnp.arange(rows, dtype=jnp.int32)
    seg = lax.optimization_barrier(jnp.sum((pos[:, None] >= ends[None, :]).astype(jnp.int32), axis=1))
    allowed = (seg[:, None] == seg[None, :]) & (pos[:, None] >= pos[None, :])

    def one_head(head):
        qh = queries[:, head].astype(jnp.float32)
        kh = keys[:, head].astype(jnp.float32)
        vh = values[:, head].astype(jnp.float32)
        scores = jnp.einsum('rgd,sd->grs', qh, kh) / jnp.sqrt(jnp.float32(HD))
        scores = jnp.where(allowed[None], scores, jnp.float32(-1e+30))
        top = lax.optimization_barrier(jnp.max(scores, axis=-1, keepdims=True))
        expd = jnp.exp(scores - top)
        probs = (expd / lax.optimization_barrier(jnp.sum(expd, axis=-1, keepdims=True))).astype(jnp.bfloat16)
        return jnp.einsum('grs,sd->rgd', probs.astype(jnp.float32), vh).astype(jnp.bfloat16)
    heads = lax.map(one_head, jnp.arange(KVH))
    attn = jnp.transpose(heads, (1, 0, 2, 3)).reshape(rows, QH * HD)
    cols = QH * HD // N_TP
    total = jnp.zeros((rows, D), jnp.float32)
    for part in range(N_TP):
        piece = jnp.dot(attn[:, part * cols:(part + 1) * cols], ref_wo[part * cols:(part + 1) * cols], preferred_element_type=jnp.float32)
        piece = lax.optimization_barrier(piece.astype(jnp.bfloat16))
        total = total + piece.astype(jnp.float32)
    ref_out = input_float + total
    score = lax.optimization_barrier(jnp.sum(ref_out * rms_scale(ref_out) * score_vec, axis=-1))
    onehot = seg[:, None] == jnp.arange(SEQS, dtype=jnp.int32)[None, :]
    adv_tok = lax.optimization_barrier(jnp.sum(jnp.where(onehot, adv[None, :], jnp.float32(0.0)), axis=1))
    return (adv_tok - score).astype(jnp.bfloat16)

def reference(hidden, ref_gain, ref_wq, ref_wkv, ref_wo, score_vec, lengths, advantage, dest, policy_norm_gain, pol_w, cotangent):
    blocks = hidden.reshape(N_REP, REP_ROWS, D)

    def per_replica(items):
        return replica_weights(items[0], items[1], items[2], ref_gain, ref_wq, ref_wkv, ref_wo, score_vec)
    tok_weight = lax.map(per_replica, (blocks, lengths, advantage)).reshape(TOKENS)
    order = jnp.argsort(dest, stable=True).astype(jnp.int32)
    x_pol = hidden[order]
    w_pol = tok_weight[order]
    input_float = x_pol.astype(jnp.float32)
    inverse_root_mean = rms_scale(input_float)
    normalized_input = input_float * inverse_root_mean
    policy_normed = (normalized_input * policy_norm_gain).astype(jnp.bfloat16)
    y = jnp.dot(policy_normed, pol_w, preferred_element_type=jnp.float32)
    dy = (w_pol.astype(jnp.float32)[:, None] * cotangent.astype(jnp.float32) + 0.5 * y).astype(jnp.bfloat16)
    grad_weight = jnp.dot(policy_normed.T, dy, preferred_element_type=jnp.float32)
    normed_gradient = jnp.dot(dy, pol_w.T, preferred_element_type=jnp.float32)
    policy_gain_gradient = lax.optimization_barrier(jnp.sum(normed_gradient * normalized_input, axis=0))
    normalized_input_gradient = normed_gradient * policy_norm_gain
    policy_input_gradient = (inverse_root_mean * (normalized_input_gradient - normalized_input * lax.optimization_barrier(jnp.mean(normalized_input_gradient * normalized_input, axis=-1, keepdims=True)))).astype(jnp.bfloat16)
    return (policy_input_gradient, grad_weight, policy_gain_gradient)
```

```python
import functools

import jax
import jax.numpy as jnp
from jax import lax
from jax.experimental import pallas as pl
from jax.experimental.pallas import tpu as pltpu
from jax.sharding import PartitionSpec as P

HD = 128
RUN = 8
CAP = 24
BLOCK = 256
EPS = 1e-6
BF = jnp.bfloat16
F32 = jnp.float32
VMEM_LIMIT = 48 * 1024 * 1024
HIGH = lax.Precision.HIGHEST


def attention_kernel(heads, ends_ref, q_ref, kv_ref, out_ref):
    rows = q_ref.shape[0]
    for block in range(rows // BLOCK):
        low = max(0, block - 2) * BLOCK
        high = (block + 1) * BLOCK
        width = high - low
        row = lax.broadcasted_iota(jnp.int32, (BLOCK, 1), 0) + block * BLOCK
        start = jnp.zeros((BLOCK, 1), jnp.int32)
        for k in range(ends_ref.shape[0]):
            end = ends_ref[k]
            start = jnp.where(row >= end, end, start)
        col = lax.broadcasted_iota(jnp.int32, (BLOCK, width), 1) + low
        allowed = (col >= start) & (col <= row)
        keys = kv_ref[low:high, :HD]
        values = kv_ref[low:high, HD:]
        for head in range(heads):
            lanes = slice(head * HD, (head + 1) * HD)
            q = q_ref[block * BLOCK : high, lanes]
            s = lax.dot_general(q, keys, (((1,), (1,)), ((), ())), preferred_element_type=F32)
            s = jnp.where(allowed, s * F32(HD**-0.5), F32(-1e30))
            e = jnp.exp(s - jnp.max(s, axis=-1, keepdims=True))
            p = (e / jnp.sum(e, axis=-1, keepdims=True)).astype(BF)
            o = lax.dot_general(p, values, (((1,), (0,)), ((), ())), preferred_element_type=F32)
            out_ref[block * BLOCK : high, lanes] = o.astype(BF)


def attention(ends, q, kv):
    rows, width = q.shape
    return pl.pallas_call(
        functools.partial(attention_kernel, width // HD),
        out_shape=jax.ShapeDtypeStruct((rows, width), BF),
        in_specs=[
            pl.BlockSpec(memory_space=pltpu.SMEM),
            pl.BlockSpec(memory_space=pltpu.VMEM),
            pl.BlockSpec(memory_space=pltpu.VMEM),
        ],
        out_specs=pl.BlockSpec(memory_space=pltpu.VMEM),
        compiler_params=pltpu.CompilerParams(vmem_limit_bytes=VMEM_LIMIT),
        cost_estimate=pl.CostEstimate(flops=2 * 10**9, bytes_accessed=3 * 10**6, transcendentals=2 * 10**6),
        name="attention",
    )(ends, q, kv)


def readout_kernel(attn_ref, wo_ref, hid_ref, vec_ref, out_ref):
    total = hid_ref[...].astype(F32)
    for g in range(attn_ref.shape[0]):
        part = jnp.dot(attn_ref[g], wo_ref[g], preferred_element_type=F32)
        total = total + part.astype(BF).astype(F32)
    ones = jnp.ones((8, total.shape[1]), F32)
    dims = (((1,), (1,)), ((), ()))
    first = lax.dot_general(ones, total * vec_ref[...], dims, precision=HIGH, preferred_element_type=F32)
    second = lax.dot_general(ones, total * total, dims, precision=HIGH, preferred_element_type=F32)
    which = lax.broadcasted_iota(jnp.int32, first.shape, 0)
    out_ref[...] = jnp.where(which == 0, first, second)


def readout(attn, wo, hid, vec):
    groups, rows, depth = attn.shape
    width = wo.shape[2]
    return pl.pallas_call(
        readout_kernel,
        out_shape=jax.ShapeDtypeStruct((8, rows), F32),
        grid=(rows // BLOCK,),
        in_specs=[
            pl.BlockSpec((groups, BLOCK, depth), lambda i: (0, i, 0)),
            pl.BlockSpec((groups, depth, width), lambda i: (0, 0, 0)),
            pl.BlockSpec((BLOCK, width), lambda i: (i, 0)),
            pl.BlockSpec((1, width), lambda i: (0, 0)),
        ],
        out_specs=pl.BlockSpec((8, BLOCK), lambda i: (0, i)),
        compiler_params=pltpu.CompilerParams(vmem_limit_bytes=VMEM_LIMIT),
        cost_estimate=pl.CostEstimate(
            flops=2 * groups * rows * depth * width, bytes_accessed=15 * 10**6, transcendentals=0
        ),
        name="readout",
    )(attn, wo, hid, vec)


def policy_kernel(model, chunk, pad, w_ref, inv_ref, y_ref, cot_ref, x_ref, gain_ref, pw_ref, dx_ref, gw_ref, acc, gacc):
    i = pl.program_id(0)

    @pl.when(i == 0)
    def _():
        acc[...] = jnp.zeros_like(acc)
        gacc[...] = jnp.zeros_like(gacc)

    y = y_ref[...].astype(F32)
    dy = (w_ref[...] * cot_ref[...].astype(F32) + 0.5 * y).astype(BF)
    mean = jnp.sum(dy.astype(F32) * y, axis=-1, keepdims=True) * F32(1.0 / model)
    gain = gain_ref[...]
    inv = inv_ref[...]
    xhat = x_ref[...].astype(F32) * inv
    pn = (xhat * gain).astype(BF)
    acc[...] += lax.dot_general(pn, dy, (((0,), (0,)), ((), ())), preferred_element_type=F32)
    dpn = lax.dot_general(dy, pw_ref[...], (((1,), (1,)), ((), ())), preferred_element_type=F32)
    gacc[0:1, :] += jnp.sum(dpn * xhat, axis=0, keepdims=True)
    dx_ref[...] = (inv * (dpn * gain - xhat * mean)).astype(BF)

    @pl.when(i == pl.num_programs(0) - 1)
    def _():
        for k in range(gw_ref.shape[0]):
            gw_ref[k, :chunk, :] = acc[k * chunk : (k + 1) * chunk, :].astype(BF)
            gw_ref[k, chunk:, :] = jnp.zeros((pad - chunk, gw_ref.shape[2]), BF)
            piece = gacc[0:1, k * chunk : (k + 1) * chunk]
            hi = piece.astype(BF)
            gw_ref[k, chunk : chunk + 1, :chunk] = hi
            gw_ref[k, chunk + 1 : chunk + 2, :chunk] = (piece - hi.astype(F32)).astype(BF)


def policy(model, reps, w, inv, y, cot, x, gain, pw):
    rows, width = x.shape
    outs = y.shape[1]
    chunk = width // reps
    pad = -(-(chunk + 2) // 16) * 16
    row = lambda n: pl.BlockSpec((BLOCK, n), lambda i: (i, 0))
    return pl.pallas_call(
        functools.partial(policy_kernel, model, chunk, pad),
        out_shape=(
            jax.ShapeDtypeStruct((rows, width), BF),
            jax.ShapeDtypeStruct((reps, pad, outs), BF),
        ),
        grid=(rows // BLOCK,),
        in_specs=[
            row(1),
            row(1),
            row(outs),
            row(outs),
            row(width),
            pl.BlockSpec((1, width), lambda i: (0, 0)),
            pl.BlockSpec((width, outs), lambda i: (0, 0)),
        ],
        out_specs=(row(width), pl.BlockSpec((reps, pad, outs), lambda i: (0, 0, 0))),
        scratch_shapes=[pltpu.VMEM((width, outs), F32), pltpu.VMEM((8, width), F32)],
        compiler_params=pltpu.CompilerParams(vmem_limit_bytes=VMEM_LIMIT),
        cost_estimate=pl.CostEstimate(flops=4 * rows * width * outs, bytes_accessed=7 * 10**6, transcendentals=0),
        name="policy",
    )(w, inv, y, cot, x, gain, pw)


def spread(a, axis):
    n = lax.axis_size(axis)
    return lax.all_to_all(jnp.broadcast_to(a[None], (n,) + a.shape), axis, split_axis=0, concat_axis=0, tiled=True)


def ints(a, b):
    return jnp.dot(a.astype(BF), b.astype(BF), preferred_element_type=F32).astype(jnp.int32)


def relay_lists(run_dest, rep, reps, tps):
    devices, runs = run_dest.shape
    match = (run_dest[:, :, None] == jnp.arange(devices, dtype=jnp.int32)).astype(jnp.int32)
    sends = jnp.sum(match, axis=1)
    which = jnp.sum(match * jnp.arange(runs, dtype=jnp.int32)[None, :, None], axis=1)
    at = jnp.arange(devices, dtype=jnp.int32)
    rank = ints(at[None, :] < at[:, None], sends)
    pairs = tps * tps
    blocks = sends.reshape(reps, tps, reps, tps).transpose(0, 2, 1, 3).reshape(reps * reps, pairs)
    pair = jnp.arange(pairs, dtype=jnp.int32)
    slot = ints(blocks, pair[:, None] < pair[None, :])
    most = jnp.max(jnp.sum(blocks, axis=1))
    blocks = blocks.reshape(reps, reps, pairs)
    slot = slot.reshape(reps, reps, pairs)
    local_run = (
        (jnp.arange(devices, dtype=jnp.int32) % tps)[:, None] * runs + which
    ).reshape(reps, tps, reps, tps).transpose(0, 2, 1, 3).reshape(reps, reps, pairs)
    pick = lambda a: lax.dynamic_index_in_dim(a, rep, 0, keepdims=False)
    mine, my_slot, my_run = pick(blocks), pick(slot), pick(local_run)

    def sending(turn):
        want = jnp.arange(CAP, dtype=jnp.int32) + CAP * turn
        hit = (my_slot[:, None, :] == want[None, :, None]) & (mine[:, None, :] > 0)
        return jnp.sum(jnp.where(hit, my_run[:, None, :], 0), axis=2).reshape(-1)

    take = lambda a: lax.dynamic_slice_in_dim(a, rep * tps, tps, 1)
    to_me, my_rank, from_run = take(sends), take(rank), take(which)
    slot_in = lax.dynamic_index_in_dim(slot, rep, 1, keepdims=False).reshape(devices, tps)
    hit = (my_rank[:, :, None] == jnp.arange(runs, dtype=jnp.int32)) & (to_me[:, :, None] > 0)
    get = lambda a: jnp.sum(jnp.where(hit, a[:, :, None], 0), axis=0).reshape(-1)
    got_slot = get(slot_in)
    got_rep = get(jnp.broadcast_to((at // tps)[:, None], (devices, tps)))
    got_run = get(at[:, None] * runs + from_run)
    return sending, got_rep * CAP + got_slot % CAP, got_slot // CAP, got_run, most


def relay(a, chosen, place):
    got = lax.all_to_all(a[chosen], "rep", split_axis=0, concat_axis=0, tiled=True)
    return got[place]


def per_device(
    hidden,
    ref_gain,
    ref_wq,
    ref_wkv,
    ref_wo,
    score_vec,
    lengths,
    advantage,
    dest,
    policy_norm_gain,
    pol_w,
    cotangent,
):
    tps, reps = lax.axis_size("tp"), lax.axis_size("rep")
    tp, rep = lax.axis_index("tp"), lax.axis_index("rep")
    rows, width = hidden.shape
    model = width * tps
    outs = pol_w.shape[1]
    runs_dev = dest.shape[0] // RUN

    own = hidden.astype(F32)
    squares = jnp.sum(spread(jnp.sum(own * own, axis=1), "tp"), axis=0)
    inv = lax.rsqrt(squares / model + EPS)
    full = lax.all_gather(hidden, "tp", axis=1, tiled=True)

    run_dest = spread(dest.reshape(runs_dev, RUN)[:, 0], ("rep", "tp"))
    sending, place, turn_of, got_run, most = relay_lists(run_dest, rep, reps, tps)
    first = sending(0)
    x_runs = hidden.reshape(rows // RUN, RUN, width)
    x_pol = relay(x_runs, first, place)

    share = ref_wo.shape[0] // reps
    wo_part = lax.dynamic_slice_in_dim(ref_wo, rep * share, share, 0)
    wo_part = wo_part.reshape(share, tps, width).transpose(1, 0, 2)
    cols = outs // tps
    w_rows = pol_w.shape[0]
    w_part = pol_w.reshape(w_rows, tps, cols).transpose(1, 0, 2).reshape(tps, -1, width)
    mixed = lax.all_to_all(
        jnp.concatenate([wo_part, w_part], axis=1), "tp", split_axis=0, concat_axis=0, tiled=True
    )
    devices = reps * tps
    turned = lax.ppermute(
        pol_w, ("rep", "tp"), [(t * reps + k, k * tps + t) for t in range(tps) for k in range(reps)]
    )
    w_len = w_part.shape[1]
    packed = jnp.concatenate(
        [mixed.reshape(tps * (share + w_len), width), turned.reshape(-1, width)], axis=0
    )
    gathered = lax.all_gather(packed, "rep", axis=0, tiled=False)
    mixed_all = gathered[:, : tps * (share + w_len)].reshape(reps, tps, share + w_len, width)
    wo_cols = mixed_all[:, :, :share].transpose(1, 0, 2, 3).reshape(tps, reps * share, width)
    w_cols = mixed_all[:, :, share:].reshape(model, cols)
    w_slice = gathered[:, tps * (share + w_len) :].reshape(width, outs)

    normed = full.astype(F32) * inv[:, None]
    xn = (normed * ref_gain).astype(BF)
    q = jnp.dot(xn, ref_wq, preferred_element_type=F32).astype(BF)
    kv = jnp.dot(xn, ref_wkv.reshape(model, -1), preferred_element_type=F32).astype(BF)
    ends = jnp.cumsum(lengths[0])
    attn = attention(ends, q, kv)
    attn_all = lax.all_gather(attn, "tp", axis=0, tiled=False)

    pn_here = (normed * policy_norm_gain).astype(BF)
    y_here = jnp.dot(pn_here, w_cols, preferred_element_type=F32).astype(BF)
    inv_hi = inv.astype(BF)
    inv_lo = (inv - inv_hi.astype(F32)).astype(BF)
    stats = jnp.stack([inv_hi, inv_lo], axis=1)
    y_runs = jnp.pad(jnp.concatenate([y_here, stats], axis=1), ((0, 0), (0, 128 - cols - 2)))
    y_runs = y_runs.reshape(rows // RUN, RUN, 128)
    y_pol = relay(y_runs, first, place)

    def again(state):
        turn, x_now, y_now = state
        chosen = sending(turn)
        fresh = (turn_of == turn)[:, None, None]
        return (
            turn + 1,
            jnp.where(fresh, relay(x_runs, chosen, place), x_now),
            jnp.where(fresh, relay(y_runs, chosen, place), y_now),
        )

    _, x_pol, y_pol = lax.while_loop(lambda s: s[0] * CAP < most, again, (jnp.int32(1), x_pol, y_pol))
    x_pol = x_pol.reshape(rows, width)
    y_pol = y_pol.reshape(rows, 128)
    inv_pol = y_pol[:, cols : cols + 1].astype(F32) + y_pol[:, cols + 1 : cols + 2].astype(F32)
    y_all = lax.all_gather(y_pol[:, :cols], "tp", axis=1, tiled=True)
    cot_all = lax.all_gather(cotangent, "tp", axis=0, tiled=True)

    vec = lax.dynamic_slice_in_dim(score_vec, tp * width, width, 0)[None]
    sums = jnp.sum(spread(readout(attn_all, wo_cols, hidden, vec)[:2], "tp"), axis=0)
    score = sums[0] * lax.rsqrt(sums[1] / model + EPS)
    pos = jnp.arange(rows, dtype=jnp.int32)
    seg = jnp.sum((pos[:, None] >= ends[None, :]).astype(jnp.int32), axis=1)
    onehot = seg[:, None] == jnp.arange(lengths.shape[1], dtype=jnp.int32)[None, :]
    adv_tok = jnp.sum(jnp.where(onehot, advantage[0][None, :], F32(0.0)), axis=1)
    tok_weight = (adv_tok - score).astype(BF)
    w_all = spread(tok_weight, "rep").reshape(devices * runs_dev, RUN)
    w_pol = w_all[got_run].reshape(rows, 1).astype(F32)

    gain = lax.dynamic_slice_in_dim(policy_norm_gain, tp * width, width, 0)[None]
    dx, gw = policy(model, reps, w_pol, inv_pol, y_all, cot_all, x_pol, gain, w_slice)
    policy_input_gradient = lax.all_to_all(
        dx.reshape(tps, rows // tps, width), "tp", split_axis=0, concat_axis=2, tiled=True
    ).reshape(rows // tps, model)
    parts = lax.all_to_all(gw, "rep", split_axis=0, concat_axis=0, tiled=True)
    total = jnp.sum(parts.astype(F32), axis=0)
    back = [(k * tps + t, t * reps + k) for t in range(tps) for k in range(reps)]
    total = lax.ppermute(total, ("rep", "tp"), back)
    grad_weight = total[:w_rows]
    policy_gain_gradient = total[w_rows, :w_rows] + total[w_rows + 1, :w_rows]
    return (policy_input_gradient, grad_weight, policy_gain_gradient)


def solution(mesh):
    return jax.shard_map(
        per_device,
        mesh=mesh,
        in_specs=(
            P("rep", "tp"),
            P(),
            P(None, "tp"),
            P(None, None, "tp"),
            P("tp", None),
            P(),
            P("rep", None),
            P("rep", None),
            P(("rep", "tp")),
            P(),
            P(("rep", "tp"), None),
            P(("rep", "tp"), None),
        ),
        out_specs=(P(("rep", "tp"), None), P(("rep", "tp"), None), P(("rep", "tp"))),
        check_vma=False,
    )
```

```python
import functools

import jax
import jax.numpy as jnp
from jax import lax
from jax.experimental import pallas as pl
from jax.experimental.pallas import tpu as pltpu
from jax.sharding import PartitionSpec as P

HD = 128
RUN = 8
CAP = 22
BLOCK = 256
CHUNKS = 2
EPS = 1e-6
BF = jnp.bfloat16
F32 = jnp.float32
VMEM_LIMIT = 48 * 1024 * 1024
ANY = pl.ANY
VM = pltpu.VMEM


def pull(copies):
    for c in copies:
        c.start()


def qkv_kernel(pieces, *refs):
    order_ref, x_refs, (gain_ref, w_ref) = refs[0], refs[1 : 1 + pieces], refs[1 + pieces : 3 + pieces]
    q_ref, kv_ref, inv_ref, x, w, acc, x_sem, w_sem = refs[3 + pieces :]
    width = x.shape[2]
    model = F32(1.0 / (width * pieces))
    x_copies = [pltpu.make_async_copy(x_refs[j], x.at[j], x_sem.at[j]) for j in range(pieces)]
    w_copies = [
        pltpu.make_async_copy(
            w_ref.at[pl.ds(pl.multiple_of(order_ref[j] * width, width), width), :], w.at[j], w_sem.at[j]
        )
        for j in range(pieces)
    ]
    pull(x_copies)
    pull(w_copies)
    squares = jnp.zeros((x.shape[1], 1), F32)
    for j in range(pieces):
        x_copies[j].wait()
        v = x[j].astype(F32)
        squares = squares + jnp.sum(v * v, axis=-1, keepdims=True)
    inv = lax.rsqrt(squares * model + EPS)
    inv_ref[...] = inv
    for j in range(pieces):
        w_copies[j].wait()
        gain = gain_ref[order_ref[j]]
        xn = (x[j].astype(F32) * inv * gain).astype(BF)
        part = jnp.dot(xn, w[j], preferred_element_type=F32)
        if j == 0:
            acc[...] = part
        else:
            acc[...] += part
    q_ref[...] = acc[:, : q_ref.shape[1]].astype(BF)
    kv_ref[...] = acc[:, q_ref.shape[1] :].astype(BF)


def qkv(order, xs, gain, w, q_width):
    n, (rows, width) = len(xs), xs[0].shape
    outs = w.shape[1]
    return pl.pallas_call(
        functools.partial(qkv_kernel, n),
        out_shape=(
            jax.ShapeDtypeStruct((rows, q_width), BF),
            jax.ShapeDtypeStruct((rows, outs - q_width), BF),
            jax.ShapeDtypeStruct((rows, 1), F32),
        ),
        in_specs=[pl.BlockSpec(memory_space=pltpu.SMEM)]
        + [pl.BlockSpec(memory_space=ANY)] * n
        + [pl.BlockSpec(memory_space=VM), pl.BlockSpec(memory_space=ANY)],
        out_specs=(pl.BlockSpec(memory_space=VM),) * 3,
        scratch_shapes=[
            VM((n, rows, width), BF),
            VM((n, width, outs), BF),
            VM((rows, outs), F32),
            pltpu.SemaphoreType.DMA((n,)),
            pltpu.SemaphoreType.DMA((n,)),
        ],
        compiler_params=pltpu.CompilerParams(vmem_limit_bytes=VMEM_LIMIT),
        cost_estimate=pl.CostEstimate(
            flops=2 * n * rows * width * outs, bytes_accessed=14 * 10**6, transcendentals=0
        ),
        name="qkv",
    )(order, *xs, gain, w)


def project_kernel(pieces, cols, *refs):
    order_ref, x_refs = refs[0], refs[1 : 1 + pieces]
    gain_ref, w_ref, inv_ref, out_ref, x, x_sem = refs[1 + pieces :]
    width = x.shape[2]
    copies = [pltpu.make_async_copy(x_refs[j], x.at[j], x_sem.at[j]) for j in range(pieces)]
    pull(copies)
    inv = inv_ref[...]
    acc = jnp.zeros(out_ref.shape, F32)
    for j in range(pieces):
        copies[j].wait()
        at = order_ref[j]
        pn = (x[j].astype(F32) * inv * gain_ref[at]).astype(BF)
        w = w_ref[pl.ds(pl.multiple_of(at * width, width), width), :]
        acc = acc + jnp.dot(pn, w, preferred_element_type=F32)
    lane = lax.broadcasted_iota(jnp.int32, acc.shape, 1)
    hi = inv.astype(BF).astype(F32)
    acc = jnp.where(lane == cols, hi, acc)
    acc = jnp.where(lane == cols + 1, inv - hi, acc)
    out_ref[...] = acc.astype(BF)


def project(order, xs, gain, w, inv, cols):
    n, (rows, width) = len(xs), xs[0].shape
    return pl.pallas_call(
        functools.partial(project_kernel, n, cols),
        out_shape=jax.ShapeDtypeStruct((rows, w.shape[1]), BF),
        in_specs=[pl.BlockSpec(memory_space=pltpu.SMEM)]
        + [pl.BlockSpec(memory_space=ANY)] * n
        + [pl.BlockSpec(memory_space=VM)] * 3,
        out_specs=pl.BlockSpec(memory_space=VM),
        scratch_shapes=[VM((n, rows, width), BF), pltpu.SemaphoreType.DMA((n,))],
        compiler_params=pltpu.CompilerParams(vmem_limit_bytes=VMEM_LIMIT),
        cost_estimate=pl.CostEstimate(
            flops=4 * n * rows * width * w.shape[1], bytes_accessed=7 * 10**6, transcendentals=0
        ),
        name="project",
    )(order, *xs, gain, w, inv)


def attention_kernel(heads, first, ends_ref, q_ref, kv_ref, out_ref):
    rows = q_ref.shape[0]
    for block in range(rows // BLOCK):
        base = first + block * BLOCK
        low = max(0, base - 2 * BLOCK)
        high = base + BLOCK
        width = high - low
        row = lax.broadcasted_iota(jnp.int32, (BLOCK, 1), 0) + base
        start = jnp.zeros((BLOCK, 1), jnp.int32)
        for k in range(ends_ref.shape[0]):
            end = ends_ref[k]
            start = jnp.where(row >= end, end, start)
        col = lax.broadcasted_iota(jnp.int32, (BLOCK, width), 1) + low
        allowed = (col >= start) & (col <= row)
        keys = kv_ref[low:high, :HD]
        values = kv_ref[low:high, HD:]
        here = slice(block * BLOCK, (block + 1) * BLOCK)
        for head in range(heads):
            lanes = slice(head * HD, (head + 1) * HD)
            s = lax.dot_general(q_ref[here, lanes], keys, (((1,), (1,)), ((), ())), preferred_element_type=F32)
            s = jnp.where(allowed, s * F32(HD**-0.5), F32(-1e30))
            e = jnp.exp(s - jnp.max(s, axis=-1, keepdims=True))
            p = (e / jnp.sum(e, axis=-1, keepdims=True)).astype(BF)
            o = lax.dot_general(p, values, (((1,), (0,)), ((), ())), preferred_element_type=F32)
            out_ref[here, lanes] = o.astype(BF)


def attention(ends, q, kv, first):
    rows, width = q.shape
    return pl.pallas_call(
        functools.partial(attention_kernel, width // HD, first),
        out_shape=jax.ShapeDtypeStruct((rows, width), BF),
        in_specs=[
            pl.BlockSpec(memory_space=pltpu.SMEM),
            pl.BlockSpec(memory_space=VM),
            pl.BlockSpec(memory_space=VM),
        ],
        out_specs=pl.BlockSpec(memory_space=VM),
        compiler_params=pltpu.CompilerParams(vmem_limit_bytes=VMEM_LIMIT),
        cost_estimate=pl.CostEstimate(flops=2 * 10**9, bytes_accessed=3 * 10**6, transcendentals=2 * 10**6),
        name="attention",
    )(ends, q, kv)


def readout_kernel(pieces, *refs):
    order_ref, a_refs = refs[0], refs[1 : 1 + pieces]
    wo_ref, hid_ref, vec_ref, out_ref, a, wo, a_sem, wo_sem = refs[1 + pieces :]
    share = wo.shape[2]
    a_copies = [pltpu.make_async_copy(a_refs[j], a.at[j], a_sem.at[j]) for j in range(pieces)]
    wo_copies = [
        pltpu.make_async_copy(
            wo_ref.at[:, pl.ds(pl.multiple_of(order_ref[j] * share, share), share), :], wo.at[j], wo_sem.at[j]
        )
        for j in range(pieces)
    ]
    for j in range(pieces):
        pull((a_copies[j], wo_copies[j]))
    total = hid_ref[...].astype(F32)
    for j in range(pieces):
        a_copies[j].wait()
        wo_copies[j].wait()
        part = jnp.dot(a[j], wo[j].reshape(-1, wo.shape[3]), preferred_element_type=F32)
        total = total + part.astype(BF).astype(F32)
    first = jnp.sum(total * vec_ref[...], axis=-1, keepdims=True)
    second = jnp.sum(total * total, axis=-1, keepdims=True)
    lane = lax.broadcasted_iota(jnp.int32, (total.shape[0], 128), 1)
    both = jnp.where(lane == 0, first, second)
    out_ref[...] = jnp.transpose(both)[:8, :]


def readout(order, pieces, wo, hid, vec):
    n, (rows, depth) = len(pieces), pieces[0].shape
    reps, width = wo.shape[0], wo.shape[2]
    share = depth // reps
    return pl.pallas_call(
        functools.partial(readout_kernel, n),
        out_shape=jax.ShapeDtypeStruct((8, rows), F32),
        in_specs=[pl.BlockSpec(memory_space=pltpu.SMEM)]
        + [pl.BlockSpec(memory_space=ANY)] * (n + 1)
        + [pl.BlockSpec(memory_space=VM)] * 2,
        out_specs=pl.BlockSpec(memory_space=VM),
        scratch_shapes=[
            VM((n, rows, depth), BF),
            VM((n, reps, share, width), BF),
            pltpu.SemaphoreType.DMA((n,)),
            pltpu.SemaphoreType.DMA((n,)),
        ],
        compiler_params=pltpu.CompilerParams(vmem_limit_bytes=VMEM_LIMIT),
        cost_estimate=pl.CostEstimate(
            flops=2 * n * rows * depth * width, bytes_accessed=10 * 10**6, transcendentals=0
        ),
        name="readout",
    )(order, *pieces, wo, hid, vec)


def weight_kernel(model, w_ref, inv_ref, y_ref, cot_ref, x_ref, gain_ref, dy_ref, mean_ref, gw_ref, acc):
    i = pl.program_id(0)
    y = y_ref[...].astype(F32)
    dy = (w_ref[...] * cot_ref[...].astype(F32) + 0.5 * y).astype(BF)
    dy_ref[...] = dy
    mean_ref[...] = jnp.sum(dy.astype(F32) * y, axis=-1, keepdims=True) * F32(1.0 / model)
    pn = (x_ref[...].astype(F32) * inv_ref[...] * gain_ref[...]).astype(BF)
    part = lax.dot_general(pn, dy, (((0,), (0,)), ((), ())), preferred_element_type=F32)

    @pl.when(i == 0)
    def _():
        acc[...] = part

    @pl.when(i > 0)
    def _():
        acc[...] += part

    @pl.when(i == pl.num_programs(0) - 1)
    def _():
        gw_ref[...] = acc[...].astype(BF)


def input_kernel(inv_ref, mean_ref, dy_ref, x_ref, gain_ref, pw_ref, dx_ref):
    inv = inv_ref[...]
    xhat = x_ref[...].astype(F32) * inv
    dpn = lax.dot_general(dy_ref[...], pw_ref[...], (((1,), (1,)), ((), ())), preferred_element_type=F32)
    dx_ref[...] = (inv * (dpn * gain_ref[...] - xhat * mean_ref[...])).astype(BF)


def policy(model, w, inv, y, cot, x, gain, pw):
    rows, width = x.shape
    outs = y.shape[1]
    row = lambda n: pl.BlockSpec((BLOCK, n), lambda i: (i, 0))
    whole = lambda *s: pl.BlockSpec(s, lambda i: (0,) * len(s))
    params = pltpu.CompilerParams(vmem_limit_bytes=VMEM_LIMIT)
    cost = pl.CostEstimate(flops=2 * rows * width * outs, bytes_accessed=5 * 10**6, transcendentals=0)
    dy, mean, gw = pl.pallas_call(
        functools.partial(weight_kernel, model),
        out_shape=(
            jax.ShapeDtypeStruct((rows, outs), BF),
            jax.ShapeDtypeStruct((rows, 1), F32),
            jax.ShapeDtypeStruct((width, outs), BF),
        ),
        grid=(rows // BLOCK,),
        in_specs=[row(1), row(1), row(outs), row(outs), row(width), whole(1, width)],
        out_specs=(row(outs), row(1), whole(width, outs)),
        scratch_shapes=[VM((width, outs), F32)],
        compiler_params=params,
        cost_estimate=cost,
        name="weight",
    )(w, inv, y, cot, x, gain)
    dx = pl.pallas_call(
        input_kernel,
        out_shape=jax.ShapeDtypeStruct((rows, width), BF),
        grid=(rows // BLOCK,),
        in_specs=[row(1), row(1), row(outs), row(width), whole(1, width), whole(width, outs)],
        out_specs=row(width),
        compiler_params=params,
        cost_estimate=cost,
        name="input",
    )(inv, mean, dy, x, gain, pw)
    return dx, gw


def place_kernel(pieces, *refs):
    order_ref, ins, out, sem = refs[0], refs[1 : 1 + pieces], refs[1 + pieces], refs[2 + pieces]
    copies = []
    for j in range(pieces):
        width = ins[j].shape[1]
        at = pl.multiple_of(order_ref[j] * width, width)
        copies.append(pltpu.make_async_copy(ins[j], out.at[:, pl.ds(at, width)], sem.at[j]))
    pull(copies)
    for c in copies:
        c.wait()


def place_columns(order, pieces):
    n, (rows, width) = len(pieces), pieces[0].shape
    return pl.pallas_call(
        functools.partial(place_kernel, n),
        out_shape=jax.ShapeDtypeStruct((rows, n * width), pieces[0].dtype),
        in_specs=[pl.BlockSpec(memory_space=pltpu.SMEM)] + [pl.BlockSpec(memory_space=ANY)] * n,
        out_specs=pl.BlockSpec(memory_space=ANY),
        scratch_shapes=[pltpu.SemaphoreType.DMA((n,))],
        cost_estimate=pl.CostEstimate(flops=0, bytes_accessed=2 * n * rows * width * 2, transcendentals=0),
        name="place",
    )(order, *pieces)


def tp_moves(tps):
    n = tps // 2
    at = lambda x, c: (x % n) * 2 + c
    every = [(x, c) for x in range(n) for c in range(2)]
    return (
        [(at(x, c), at(x, 1 - c)) for x, c in every],
        [(at(x, c), at(x + 1 - 2 * c, c)) for x, c in every],
        [(at(x, c), at(x + 1, c)) for x, c in every],
        [(at(x, c), at(x - 1, c)) for x, c in every],
        [(at(x, c), at(x + 2, c)) for x, c in every],
    )


def ring(a, swap, step):
    go = lambda v, m: lax.ppermute(v, "tp", m)
    near = go(a, step)
    other = go(a, swap)
    near_other = go(other, step)
    opposite = go(near, step)
    far_other = go(near, swap)
    far = go(near_other, swap)
    opposite_other = go(opposite, swap)
    return [a, other, near, near_other, far_other, far, opposite, opposite_other]


def ring_order(tp, tps):
    x, c = tp // 2, tp % 2
    n = tps // 2
    at = lambda xx, cc: lax.rem(xx + n, n) * 2 + cc
    up = 1 - 2 * c
    return jnp.stack(
        [
            tp,
            at(x, 1 - c),
            at(x - up, c),
            at(x - up, 1 - c),
            at(x + up, 1 - c),
            at(x + up, c),
            at(x + 2, c),
            at(x + 2, 1 - c),
        ]
    ).astype(jnp.int32)


def double_rep(a, rep, reps):
    held = a[None]
    step = 1
    while step < reps:
        got = lax.ppermute(held, "rep", [(k, k ^ step) for k in range(reps)])
        held = jnp.concatenate([held, got], axis=0)
        step *= 2
    return held[rep ^ jnp.arange(reps, dtype=jnp.int32)]


def spread(a, axis):
    n = lax.axis_size(axis)
    return lax.all_to_all(jnp.broadcast_to(a[None], (n,) + a.shape), axis, split_axis=0, concat_axis=0, tiled=True)


def ints(a, b):
    return jnp.dot(a.astype(BF), b.astype(BF), preferred_element_type=F32).astype(jnp.int32)


def relay_lists(run_dest, rep, reps, tps):
    devices, runs = run_dest.shape
    match = (run_dest[:, :, None] == jnp.arange(devices, dtype=jnp.int32)).astype(jnp.int32)
    sends = jnp.sum(match, axis=1)
    which = jnp.sum(match * jnp.arange(runs, dtype=jnp.int32)[None, :, None], axis=1)
    at = jnp.arange(devices, dtype=jnp.int32)
    rank = ints(at[None, :] < at[:, None], sends)
    pairs = tps * tps
    blocks = sends.reshape(reps, tps, reps, tps).transpose(0, 2, 1, 3).reshape(reps * reps, pairs)
    pair = jnp.arange(pairs, dtype=jnp.int32)
    slot = ints(blocks, pair[:, None] < pair[None, :])
    most = jnp.max(jnp.sum(blocks, axis=1))
    blocks = blocks.reshape(reps, reps, pairs)
    slot = slot.reshape(reps, reps, pairs)
    local_run = (
        (jnp.arange(devices, dtype=jnp.int32) % tps)[:, None] * runs + which
    ).reshape(reps, tps, reps, tps).transpose(0, 2, 1, 3).reshape(reps, reps, pairs)
    pick = lambda a: lax.dynamic_index_in_dim(a, rep, 0, keepdims=False)
    mine, my_slot, my_run = pick(blocks), pick(slot), pick(local_run)

    def sending(turn):
        want = jnp.arange(CAP, dtype=jnp.int32) + CAP * turn
        hit = (my_slot[:, None, :] == want[None, :, None]) & (mine[:, None, :] > 0)
        return jnp.sum(jnp.where(hit, my_run[:, None, :], 0), axis=2).reshape(-1)

    take = lambda a: lax.dynamic_slice_in_dim(a, rep * tps, tps, 1)
    to_me, my_rank, from_run = take(sends), take(rank), take(which)
    slot_in = lax.dynamic_index_in_dim(slot, rep, 1, keepdims=False).reshape(devices, tps)
    hit = (my_rank[:, :, None] == jnp.arange(runs, dtype=jnp.int32)) & (to_me[:, :, None] > 0)
    get = lambda a: jnp.sum(jnp.where(hit, a[:, :, None], 0), axis=0).reshape(-1)
    got_slot = get(slot_in)
    got_rep = get(jnp.broadcast_to((at // tps)[:, None], (devices, tps)))
    got_run = get(at[:, None] * runs + from_run)
    return sending, got_rep * CAP + got_slot % CAP, got_slot // CAP, got_run, most


def relay(a, chosen, place):
    got = lax.all_to_all(a[chosen], "rep", split_axis=0, concat_axis=0, tiled=True)
    return got[place]


def per_device(
    hidden,
    ref_gain,
    ref_wq,
    ref_wkv,
    ref_wo,
    score_vec,
    lengths,
    advantage,
    dest,
    policy_norm_gain,
    pol_w,
    cotangent,
):
    tps, reps = lax.axis_size("tp"), lax.axis_size("rep")
    tp, rep = lax.axis_index("tp"), lax.axis_index("rep")
    rows, width = hidden.shape
    model = width * tps
    outs = pol_w.shape[1]
    runs_dev = dest.shape[0] // RUN
    devices = reps * tps
    swap, step, up, down, across = tp_moves(tps)
    order = ring_order(tp, tps)
    half = rows // CHUNKS

    x_parts = [ring(hidden[k * half : (k + 1) * half], swap, step) for k in range(CHUNKS)]

    share = ref_wo.shape[0] // reps
    wo_part = lax.dynamic_slice_in_dim(ref_wo, rep * share, share, 0)
    wo_part = wo_part.reshape(share, tps, width).transpose(1, 0, 2)
    cols = outs // tps
    w_rows = pol_w.shape[0]
    w_part = pol_w.reshape(w_rows, tps, cols).transpose(1, 0, 2).reshape(tps, -1, width)
    mixed = lax.all_to_all(
        jnp.concatenate([wo_part, w_part], axis=1), "tp", split_axis=0, concat_axis=0, tiled=True
    )
    wo_all = lax.all_gather(mixed[:, :share].reshape(tps * share, width), "rep", axis=0, tiled=False)
    turned = lax.ppermute(
        pol_w, ("rep", "tp"), [(t * reps + k, k * tps + t) for t in range(tps) for k in range(reps)]
    )
    small = jnp.concatenate([mixed[:, share:].reshape(-1, width), turned.reshape(-1, width)], axis=0)
    small_all = double_rep(small, rep, reps)
    w_cols = small_all[:, : small.shape[0] // 2].reshape(model, cols)
    w_cols = jnp.pad(w_cols, ((0, 0), (0, 128 - cols)))
    w_slice = small_all[:, small.shape[0] // 2 :].reshape(width, outs)

    run_dest = spread(dest.reshape(runs_dev, RUN)[:, 0], ("rep", "tp"))
    sending, place, turn_of, got_run, most = relay_lists(run_dest, rep, reps, tps)
    first = sending(0)
    x_runs = hidden.reshape(rows // RUN, RUN, width)
    x_pol = relay(x_runs, first, place)

    w_in = jnp.concatenate([ref_wq, ref_wkv.reshape(model, -1)], axis=1)
    gain_in = ref_gain.reshape(tps, 1, width)
    gain_pol = policy_norm_gain.reshape(tps, 1, width)
    vec = lax.dynamic_slice_in_dim(score_vec, tp * width, width, 0)[None]
    ends = jnp.cumsum(lengths[0])
    kvs, invs, attn_parts = [], [], []
    for k in range(CHUNKS):
        q, kv, inv = qkv(order, x_parts[k], gain_in, w_in, ref_wq.shape[1])
        kvs.append(kv)
        invs.append(inv)
        attn = attention(ends, q, jnp.concatenate(kvs, axis=0), k * half)
        attn_parts.append(ring(attn, swap, step))

    y_here = [project(order, x_parts[k], gain_pol, w_cols, invs[k], cols) for k in range(CHUNKS)]
    y_runs = jnp.concatenate(y_here, axis=0).reshape(rows // RUN, RUN, 128)
    y_pol = relay(y_runs, first, place)

    def again(state):
        turn, x_now, y_now = state
        chosen = sending(turn)
        fresh = (turn_of == turn)[:, None, None]
        return (
            turn + 1,
            jnp.where(fresh, relay(x_runs, chosen, place), x_now),
            jnp.where(fresh, relay(y_runs, chosen, place), y_now),
        )

    _, x_pol, y_pol = lax.while_loop(lambda s: s[0] * CAP < most, again, (jnp.int32(1), x_pol, y_pol))
    x_pol = x_pol.reshape(rows, width)
    y_pol = y_pol.reshape(rows, 128)
    inv_pol = y_pol[:, cols : cols + 1].astype(F32) + y_pol[:, cols + 1 : cols + 2].astype(F32)
    y_all = lax.all_gather(y_pol[:, :cols], "tp", axis=1, tiled=True)
    cot_all = lax.all_gather(cotangent, "tp", axis=0, tiled=True)

    sums = jnp.concatenate(
        [
            readout(order, attn_parts[k], wo_all, hidden[k * half : (k + 1) * half], vec)[:2]
            for k in range(CHUNKS)
        ],
        axis=1,
    )
    for move in (swap, [(t, t ^ 2) for t in range(tps)], [(t, t ^ 4) for t in range(tps)]):
        sums = sums + lax.ppermute(sums, "tp", move)
    score = sums[0] * lax.rsqrt(sums[1] / model + EPS)
    pos = jnp.arange(rows, dtype=jnp.int32)
    seg = jnp.sum((pos[:, None] >= ends[None, :]).astype(jnp.int32), axis=1)
    onehot = seg[:, None] == jnp.arange(lengths.shape[1], dtype=jnp.int32)[None, :]
    adv_tok = jnp.sum(jnp.where(onehot, advantage[0][None, :], F32(0.0)), axis=1)
    tok_weight = (adv_tok - score).astype(BF)
    w_all = spread(tok_weight, "rep").reshape(devices * runs_dev, RUN)
    w_pol = w_all[got_run].reshape(rows, 1).astype(F32)

    gain = lax.dynamic_slice_in_dim(policy_norm_gain, tp * width, width, 0)[None]
    dx, gw = policy(model, w_pol, inv_pol, y_all, cot_all, x_pol, gain, w_slice)

    parts = lax.all_to_all(gw.reshape(reps, w_rows, outs), "rep", split_axis=0, concat_axis=0, tiled=True)
    back = [(k * tps + t, t * reps + k) for t in range(tps) for k in range(reps)]
    grad_weight = lax.ppermute(jnp.sum(parts.astype(F32), axis=0), ("rep", "tp"), back)
    gain_own = lax.dynamic_slice_in_dim(policy_norm_gain, (rep * tps + tp) * w_rows, w_rows, 0)
    policy_gain_gradient = jnp.sum(grad_weight * pol_w.astype(F32), axis=1) / gain_own

    x, c = tp // 2, lax.rem(tp, 2)
    n = tps // 2
    blocks = dx.reshape(n, 2, rows // tps, width)
    keep = lax.dynamic_index_in_dim(blocks, c, 1, keepdims=False)
    give = lax.dynamic_index_in_dim(blocks, 1 - c, 1, keepdims=False)
    took = lax.ppermute(give, "tp", swap)
    pieces, places = [], []
    for shift, move in ((0, None), (1, up), (-1, down), (2, across)):
        target = lax.rem(x + shift + n, n)
        pair = [lax.dynamic_index_in_dim(v, target, 0, keepdims=False) for v in (keep, took)]
        if move is not None:
            pair = list(lax.ppermute(jnp.stack(pair), "tp", move))
        origin = lax.rem(x - shift + n, n) * 2
        pieces += pair
        places += [origin + c, origin + 1 - c]
    policy_input_gradient = place_columns(jnp.stack(places).astype(jnp.int32), pieces)
    return (policy_input_gradient, grad_weight, policy_gain_gradient)


def solution(mesh):
    return jax.shard_map(
        per_device,
        mesh=mesh,
        in_specs=(
            P("rep", "tp"),
            P(),
            P(None, "tp"),
            P(None, None, "tp"),
            P("tp", None),
            P(),
            P("rep", None),
            P("rep", None),
            P(("rep", "tp")),
            P(),
            P(("rep", "tp"), None),
            P(("rep", "tp"), None),
        ),
        out_specs=(P(("rep", "tp"), None), P(("rep", "tp"), None), P(("rep", "tp"))),
        check_vma=False,
    )
```

```python
import functools

import jax
import jax.numpy as jnp
from jax import lax
from jax.experimental import pallas as pl
from jax.experimental.pallas import tpu as pltpu
from jax.sharding import PartitionSpec as P

HD = 128
RUN = 8
CAP = 22
BLOCK = 256
PARTS = (512, 512)
DEPTH = 3
TILE = 64
EPS = 1e-6
BF = jnp.bfloat16
F32 = jnp.float32
VMEM_LIMIT = 32 * 1024 * 1024
ANY = pl.ANY
LIGHT = pl.CostEstimate(flops=1, bytes_accessed=1, transcendentals=0)
VM = pltpu.VMEM


def pull(copies):
    for c in copies:
        c.start()


def project_kernel(cols, spot_ref, x_ref, gain_ref, w_ref, *refs):
    keep_ref, give_ref, both = refs[-3:]
    half = x_ref.shape[0] // 2
    n = keep_ref.shape[0]
    for i in range(2):
        xg = (x_ref[i * half : (i + 1) * half, :].astype(F32) * gain_ref[...]).astype(BF)
        part = jnp.dot(xg, w_ref[...], preferred_element_type=F32).astype(BF)
        for t in range(2 * n):
            both[t, :, i * cols : (i + 1) * cols] = part[:, t * cols : (t + 1) * cols]
    x, c = spot_ref[0], spot_ref[1]
    for s in range(n):
        owner = lax.rem(x + s, n) * 2
        keep_ref[s] = both[owner + c]
        give_ref[s] = both[owner + 1 - c]


def project(spot, x, gain, w, tps, after):
    rows, cols = x.shape[0], w.shape[1] // tps
    shape = (tps // 2, rows // 2, 2 * cols)
    return pl.pallas_call(
        functools.partial(project_kernel, cols),
        out_shape=(jax.ShapeDtypeStruct(shape, BF),) * 2,
        in_specs=[pl.BlockSpec(memory_space=pltpu.SMEM)]
        + [pl.BlockSpec(memory_space=VM)] * 3
        + [pl.BlockSpec(memory_space=ANY)] * len(after),
        out_specs=(pl.BlockSpec(memory_space=VM),) * 2,
        scratch_shapes=[VM((tps,) + shape[1:], BF)],
        compiler_params=pltpu.CompilerParams(vmem_limit_bytes=VMEM_LIMIT),
        cost_estimate=LIGHT,
        name="project",
    )(spot, x, gain, w, *after)


def pair_kernel(keep_ref, took_ref, *out_refs):
    for s, out_ref in enumerate(out_refs):
        out_ref[...] = (keep_ref[s].astype(F32) + took_ref[s].astype(F32)).astype(BF)


def pair_sums(keep, took):
    n = keep.shape[0]
    return pl.pallas_call(
        pair_kernel,
        out_shape=(jax.ShapeDtypeStruct(keep.shape[1:], BF),) * n,
        in_specs=[pl.BlockSpec(memory_space=VM)] * 2,
        out_specs=(pl.BlockSpec(memory_space=VM),) * n,
        cost_estimate=LIGHT,
        name="pair",
    )(keep, took)


def pack_kernel(pieces, *refs):
    inv_refs, out_ref = refs[pieces:-1], refs[-1]
    scales = jnp.concatenate([r[...] for r in inv_refs], axis=0)
    total = refs[0][...].astype(F32)
    for j in range(1, pieces):
        total = total + refs[j][...].astype(F32)
    half, cols = total.shape[0], total.shape[1] // 2
    lane = lax.broadcasted_iota(jnp.int32, (half, out_ref.shape[1] - cols), 1)
    for i in range(2):
        here = slice(i * half, (i + 1) * half)
        inv = scales[here, :]
        hi = inv.astype(BF).astype(F32)
        stats = jnp.where(lane == 0, hi, jnp.where(lane == 1, inv - hi, F32(0.0)))
        y = total[:, i * cols : (i + 1) * cols] * inv
        out_ref[here, :] = jnp.concatenate([y, stats], axis=1).astype(BF)


def pack(pieces, invs):
    rows = 2 * pieces[0].shape[0]
    return pl.pallas_call(
        functools.partial(pack_kernel, len(pieces)),
        out_shape=jax.ShapeDtypeStruct((rows, 128), BF),
        in_specs=[pl.BlockSpec(memory_space=VM)] * (len(pieces) + len(invs)),
        out_specs=pl.BlockSpec(memory_space=VM),
        cost_estimate=LIGHT,
        name="pack",
    )(*pieces, *invs)


def attention_kernel(heads, first, ends_ref, q_ref, kv_ref, *refs):
    out_ref = refs[-1]
    rows = q_ref.shape[0]
    for block in range(rows // BLOCK):
        base = first + block * BLOCK
        low = max(0, base - 2 * BLOCK)
        high = base + BLOCK
        width = high - low
        row = lax.broadcasted_iota(jnp.int32, (BLOCK, 1), 0) + base
        start = jnp.zeros((BLOCK, 1), jnp.int32)
        for k in range(ends_ref.shape[0]):
            end = ends_ref[k]
            start = jnp.where(row >= end, end, start)
        col = lax.broadcasted_iota(jnp.int32, (BLOCK, width), 1) + low
        allowed = (col >= start) & (col <= row)
        keys = kv_ref[low:high, :HD]
        values = kv_ref[low:high, HD:]
        here = slice(block * BLOCK, (block + 1) * BLOCK)
        for head in range(heads):
            lanes = slice(head * HD, (head + 1) * HD)
            s = lax.dot_general(q_ref[here, lanes], keys, (((1,), (1,)), ((), ())), preferred_element_type=F32)
            s = jnp.where(allowed, s * F32(HD**-0.5), F32(-1e30))
            e = jnp.exp(s - jnp.max(s, axis=-1, keepdims=True))
            p = (e / jnp.sum(e, axis=-1, keepdims=True)).astype(BF)
            o = lax.dot_general(p, values, (((1,), (0,)), ((), ())), preferred_element_type=F32)
            out_ref[here, lanes] = o.astype(BF)


def attention(ends, q, kv, first, after):
    rows, width = q.shape
    return pl.pallas_call(
        functools.partial(attention_kernel, width // HD, first),
        out_shape=jax.ShapeDtypeStruct((rows, width), BF),
        in_specs=[
            pl.BlockSpec(memory_space=pltpu.SMEM),
            pl.BlockSpec(memory_space=VM),
            pl.BlockSpec(memory_space=VM),
        ]
        + [pl.BlockSpec(memory_space=ANY)] * len(after),
        out_specs=pl.BlockSpec(memory_space=VM),
        compiler_params=pltpu.CompilerParams(vmem_limit_bytes=VMEM_LIMIT),
        cost_estimate=LIGHT,
        name="attention",
    )(ends, q, kv, *after)


def outproj_kernel(block, at_ref, attn_ref, wo_ref, keep_ref, give_ref, a):
    x, c, n = at_ref[0], at_ref[1], a.shape[0] // (2 * block)

    @pl.when(pl.program_id(0) == 0)
    def _():
        for other in range(2):
            core = c if other == 0 else 1 - c
            for s in range(n):
                owner = lax.rem(x + s, n) * 2 + core
                here = pl.ds(pl.multiple_of(owner * block, block), block)
                a[(other * n + s) * block : (other * n + s + 1) * block, :] = attn_ref[here, :]

    out = jnp.dot(a[...], wo_ref[...], preferred_element_type=F32).astype(BF)
    keep_ref[...] = out[: n * block]
    give_ref[...] = out[n * block :]


def outproj(place, attn, wo, tps, part, parts):
    rows, depth = attn.shape[0] // parts, attn.shape[1]
    model = wo.shape[1]
    step = model // 5
    half = pl.BlockSpec((rows // 2, step), lambda i: (0, i))
    return pl.pallas_call(
        functools.partial(outproj_kernel, rows // tps),
        out_shape=(jax.ShapeDtypeStruct((rows // 2, model), BF),) * 2,
        grid=(5,),
        in_specs=[
            pl.BlockSpec(memory_space=pltpu.SMEM),
            pl.BlockSpec((rows, depth), lambda i: (part, 0)),
            pl.BlockSpec((depth, step), lambda i: (0, i)),
        ],
        out_specs=(half, half),
        scratch_shapes=[VM((rows, depth), BF)],
        compiler_params=pltpu.CompilerParams(vmem_limit_bytes=VMEM_LIMIT),
        cost_estimate=LIGHT,
        name="outproj",
    )(place, attn, wo)


def merge_kernel(block, keep_ref, took_ref, *refs):
    up_ref, down_ref, rest_ref = refs[-3:]
    half = block // 2
    add = lambda lo, hi: (keep_ref[lo:hi, :].astype(F32) + took_ref[lo:hi, :].astype(F32)).astype(BF)
    far, near_down = 2 * block, 3 * block
    up_ref[:half, :] = add(far, far + half)
    up_ref[half:, :] = add(block + half, 2 * block)
    down_ref[:half, :] = add(near_down, near_down + half)
    down_ref[half:, :] = add(far + half, far + block)
    rest_ref[:block, :] = add(0, block)
    rest_ref[block : block + half, :] = add(block, block + half)
    rest_ref[block + half :, :] = add(near_down + half, near_down + block)


def merge(keep, took, block, after):
    rows, model = keep.shape
    step = model // 2
    spec = lambda n: pl.BlockSpec((n, step), lambda i: (0, i))
    shape = lambda n: jax.ShapeDtypeStruct((n, model), BF)
    return pl.pallas_call(
        functools.partial(merge_kernel, block),
        out_shape=(shape(block), shape(block), shape(2 * block)),
        grid=(2,),
        in_specs=[spec(rows), spec(rows)] + [pl.BlockSpec(memory_space=ANY)] * len(after),
        out_specs=(spec(block), spec(block), spec(2 * block)),
        compiler_params=pltpu.CompilerParams(vmem_limit_bytes=VMEM_LIMIT),
        cost_estimate=LIGHT,
        name="merge",
    )(keep, took, *after)


def pass_kernel(block, below_ref, above_ref, rest_ref, up_ref, down_ref):
    half = block // 2
    add = lambda a, b: (a.astype(F32) + b.astype(F32)).astype(BF)
    up_ref[...] = add(rest_ref[block : block + half, :], below_ref[:half, :])
    down_ref[...] = add(rest_ref[block + half :, :], above_ref[half:, :])


def pass_on(below, above, rest):
    block, model = below.shape
    return pl.pallas_call(
        functools.partial(pass_kernel, block),
        out_shape=(jax.ShapeDtypeStruct((block // 2, model), BF),) * 2,
        in_specs=[pl.BlockSpec(memory_space=VM)] * 3,
        out_specs=(pl.BlockSpec(memory_space=VM),) * 2,
        cost_estimate=LIGHT,
        name="pass",
    )(below, above, rest)


def ring_sum(merged, up, down):
    go_up, go_down, rest = merged
    below, above = lax.ppermute(go_up, "tp", up), lax.ppermute(go_down, "tp", down)
    up2, down2 = pass_on(below, above, rest)
    return up2, (rest, below, above, lax.ppermute(up2, "tp", up), lax.ppermute(down2, "tp", down))


def score_kernel(first, order_ref, ends_ref, adv_ref, full_ref, vec_ref, *refs):
    rest_ref, below_ref, above_ref, below2_ref, above2_ref, out_ref, x, sem = refs
    rows, model = x.shape
    half = rows // 2
    own = pl.multiple_of(order_ref[0] * rows, rows)
    copy = pltpu.make_async_copy(full_ref.at[pl.ds(first + own, rows), :], x, sem)
    copy.start()
    copy.wait()
    one = jnp.zeros((rows, 128), F32)
    two = jnp.zeros((rows, 128), F32)
    for lane in range(0, model, 128):
        cols = slice(lane, lane + 128)
        get = lambda ref, lo, hi: ref[lo:hi, cols].astype(F32)
        near = jnp.concatenate(
            [
                get(below2_ref, 0, half) + get(above_ref, 0, half),
                get(below_ref, half, rows) + get(above2_ref, 0, half),
            ],
            axis=0,
        )
        total = get(x, 0, rows) + get(rest_ref, 0, rows) + near
        one = one + total * vec_ref[:, cols]
        two = two + total * total
    mean = jnp.sum(two, axis=-1, keepdims=True) * F32(1.0 / model)
    score = jnp.sum(one, axis=-1, keepdims=True) * lax.rsqrt(mean + EPS)
    row = lax.broadcasted_iota(jnp.int32, (rows, 1), 0) + own + first
    adv = jnp.full((rows, 1), adv_ref[0], F32)
    for k in range(1, ends_ref.shape[0]):
        adv = jnp.where(row >= ends_ref[k - 1], adv_ref[k], adv)
    weight = jnp.broadcast_to(adv - score, (rows, 128))
    out_ref[...] = jnp.transpose(weight)[:8, :].astype(BF).astype(F32)


def token_weights(own, ends, adv, full, vec, rest, below, above, below2, above2, first):
    rows, model = below.shape
    return pl.pallas_call(
        functools.partial(score_kernel, first),
        out_shape=jax.ShapeDtypeStruct((8, rows), F32),
        in_specs=[pl.BlockSpec(memory_space=pltpu.SMEM)] * 3
        + [pl.BlockSpec(memory_space=ANY)]
        + [pl.BlockSpec(memory_space=VM)] * 6,
        out_specs=pl.BlockSpec(memory_space=VM),
        scratch_shapes=[VM((rows, model), BF), pltpu.SemaphoreType.DMA],
        compiler_params=pltpu.CompilerParams(vmem_limit_bytes=VMEM_LIMIT),
        cost_estimate=LIGHT,
        name="score",
    )(own, ends, adv, full, vec, rest, below, above, below2, above2)


def own_weights(run_ref, all_ref, cols_of, out_ref):
    tps, runs_dev, spans = cols_of
    devices = all_ref.shape[0]
    runs = run_ref.shape[1]
    rows = out_ref.shape[0]
    run = run_ref[...]
    rep, at = lax.div(run, tps * runs_dev), lax.rem(run, tps * runs_dev) * RUN
    device, lane = jnp.zeros_like(run), jnp.zeros_like(run)
    for start, size in spans:
        share = size // tps
        here = (at >= start) & (at < start + size)
        device = jnp.where(here, rep * tps + lax.div(at - start, share), device)
        lane = jnp.where(here, start // tps + lax.rem(at - start, share), lane)
    down = lambda n, m: lax.broadcasted_iota(jnp.int32, (n, m), 0)
    across = lambda n, m: lax.broadcasted_iota(jnp.int32, (n, m), 1)
    one = lambda m: m.astype(jnp.int32).astype(F32).astype(BF)
    found = lax.dot_general(
        all_ref[...], one(down(devices, runs) == device), (((0,), (0,)), ((), ())), preferred_element_type=F32
    )
    lanes = down(found.shape[0], runs)
    found = jnp.where((lanes >= lane) & (lanes < lane + RUN), found, F32(0.0)).astype(BF)
    fold = one(down(RUN, found.shape[0]) == lax.rem(across(RUN, found.shape[0]), RUN))
    eight = jnp.dot(fold, found, preferred_element_type=F32).astype(BF)
    whose = one(lax.div(down(rows, runs), RUN) == across(rows, runs))
    wide = lax.dot_general(whose, eight, (((1,), (1,)), ((), ())), preferred_element_type=F32)
    wide = jnp.where(lax.rem(down(rows, RUN), RUN) == across(rows, RUN), wide, F32(0.0))
    out_ref[...] = jnp.sum(wide, axis=1, keepdims=True)


def weight_kernel(
    model, cols_of, run_ref, all_ref, inv_ref, y_ref, cot_ref, x_ref, gain_ref, dy_ref, mean_ref, gw_ref, acc, w
):
    i = pl.program_id(0)

    @pl.when(i == 0)
    def _():
        own_weights(run_ref, all_ref, cols_of, w)

    y = y_ref[...].astype(F32)
    here = pl.ds(pl.multiple_of(i * BLOCK, BLOCK), BLOCK)
    dy = (w[here, :] * cot_ref[...].astype(F32) + 0.5 * y).astype(BF)
    dy_ref[...] = dy
    mean_ref[...] = jnp.sum(dy.astype(F32) * y, axis=-1, keepdims=True) * F32(1.0 / model)
    pn = (x_ref[...].astype(F32) * inv_ref[...] * gain_ref[...]).astype(BF)
    part = lax.dot_general(pn, dy, (((0,), (0,)), ((), ())), preferred_element_type=F32)

    @pl.when(i == 0)
    def _():
        acc[...] = part

    @pl.when(i > 0)
    def _():
        acc[...] += part

    @pl.when(i == pl.num_programs(0) - 1)
    def _():
        gw_ref[...] = acc[...].astype(BF)


def input_kernel(spot_ref, inv_ref, mean_ref, dy_ref, x_ref, gain_ref, pw_ref, give_ref, *keep_refs):
    x, c = spot_ref[0], spot_ref[1]
    n = len(keep_refs)
    block = keep_refs[0].shape[0]
    for other in (1, 0):
        for s in range(n):
            owner = lax.rem(x + s, n) * 2 + (c if other == 0 else 1 - c)
            here = pl.ds(pl.multiple_of(owner * block, block), block)
            inv = inv_ref[here, :]
            xhat = x_ref[here, :].astype(F32) * inv
            dpn = lax.dot_general(
                dy_ref[here, :], pw_ref[...], (((1,), (1,)), ((), ())), preferred_element_type=F32
            )
            dx = (inv * (dpn * gain_ref[...] - xhat * mean_ref[here, :])).astype(BF)
            if other:
                give_ref[s] = dx
            else:
                keep_refs[s][...] = dx


def policy(spot, tps, model, cols_of, run, w_all, inv, y, cot, x, gain, pw):
    rows, width = x.shape
    outs = y.shape[1]
    row = lambda n: pl.BlockSpec((BLOCK, n), lambda i: (i, 0))
    whole = lambda *s: pl.BlockSpec(s, lambda i: (0,) * len(s))
    params = pltpu.CompilerParams(vmem_limit_bytes=VMEM_LIMIT)
    dy, mean, gw = pl.pallas_call(
        functools.partial(weight_kernel, model, cols_of),
        out_shape=(
            jax.ShapeDtypeStruct((rows, outs), BF),
            jax.ShapeDtypeStruct((rows, 1), F32),
            jax.ShapeDtypeStruct((width, outs), BF),
        ),
        grid=(rows // BLOCK,),
        in_specs=[whole(*run.shape), whole(*w_all.shape), row(1), row(outs), row(outs), row(width), whole(1, width)],
        out_specs=(row(outs), row(1), whole(width, outs)),
        scratch_shapes=[VM((width, outs), F32), VM((rows, 1), F32)],
        compiler_params=params,
        cost_estimate=LIGHT,
        name="weight",
    )(run, w_all, inv, y, cot, x, gain)
    n = tps // 2
    block = jax.ShapeDtypeStruct((rows // tps, width), BF)
    give, *keep = pl.pallas_call(
        input_kernel,
        out_shape=(jax.ShapeDtypeStruct((n, rows // tps, width), BF),) + (block,) * n,
        in_specs=[pl.BlockSpec(memory_space=pltpu.SMEM)] + [pl.BlockSpec(memory_space=VM)] * 6,
        out_specs=(pl.BlockSpec(memory_space=VM),) * (n + 1),
        compiler_params=params,
        cost_estimate=LIGHT,
        name="input",
    )(spot, inv, mean, dy, x, gain, pw)
    return give, keep, gw


def place_kernel(pieces, *refs):
    order_ref, ins, out = refs[0], refs[1 : 1 + pieces], refs[1 + pieces]
    for j in range(pieces):
        width = ins[j].shape[1]
        out[:, pl.ds(pl.multiple_of(order_ref[j] * width, width), width)] = ins[j][...]


def place_columns(order, pieces):
    n, (rows, width) = len(pieces), pieces[0].shape
    return pl.pallas_call(
        functools.partial(place_kernel, n),
        out_shape=jax.ShapeDtypeStruct((rows, n * width), pieces[0].dtype),
        in_specs=[pl.BlockSpec(memory_space=pltpu.SMEM)] + [pl.BlockSpec(memory_space=VM)] * n,
        out_specs=pl.BlockSpec(memory_space=VM),
        cost_estimate=LIGHT,
        name="place",
    )(order, *pieces)


def tp_moves(tps):
    n = tps // 2
    at = lambda x, c: (x % n) * 2 + c
    every = [(x, c) for x in range(n) for c in range(2)]
    return (
        [(at(x, c), at(x, 1 - c)) for x, c in every],
        [(at(x, c), at(x + 1, c)) for x, c in every],
        [(at(x, c), at(x - 1, c)) for x, c in every],
        [(at(x, c), at(x + 2, c)) for x, c in every],
    )


def spread(a, axis):
    n = lax.axis_size(axis)
    return lax.all_to_all(jnp.broadcast_to(a[None], (n,) + a.shape), axis, split_axis=0, concat_axis=0, tiled=True)


def flag(m):
    return m.astype(jnp.int32).astype(F32)


def small_dot(a, b, dims=(((1,), (0,)), ((), ()))):
    return lax.dot_general(a.astype(BF), b.astype(BF), dims, preferred_element_type=F32)


def grid_of(shape):
    return tuple(lax.broadcasted_iota(jnp.int32, shape, d) for d in range(2))


def send_kernel(base_ref, dest_ref, out_ref):
    tps, runs = dest_ref.shape
    reps = out_ref.shape[0]
    devices = reps * tps
    row, col = grid_of((devices, devices))
    same = row // tps == col // tps
    run, at = grid_of((tps, devices))
    sends = jnp.zeros((tps, devices), F32)
    which = jnp.zeros((tps, devices), F32)
    for k in range(runs):
        hit = flag(dest_ref[:, k : k + 1] == at)
        sends = sends + hit
        which = which + hit * k
    which = which + (run * runs).astype(F32)
    r8, c8 = grid_of((tps, tps))
    slot = small_dot(flag(c8 < r8), small_dot(sends, flag(same))) + small_dot(sends, flag(same & (row < col)))
    want = (grid_of((128, devices))[0] + base_ref[0]).astype(F32)
    found = jnp.zeros((128, devices), F32)
    for i in range(tps):
        hit = (slot[i : i + 1] == want) & (sends[i : i + 1] > 0.5)
        found = found + jnp.where(hit, which[i : i + 1], F32(0.0))
    rep, dev = grid_of((reps, devices))
    chosen = small_dot(flag(dev // tps == rep), found, (((1,), (1,)), ((), ())))
    out_ref[...] = chosen.astype(jnp.int32)


def send_lists(dest, reps, turn):
    out = pl.pallas_call(
        send_kernel,
        out_shape=jax.ShapeDtypeStruct((reps, 128), jnp.int32),
        in_specs=[pl.BlockSpec(memory_space=pltpu.SMEM), pl.BlockSpec(memory_space=VM)],
        out_specs=pl.BlockSpec(memory_space=VM),
        cost_estimate=LIGHT,
        name="send_lists",
    )((turn * CAP).astype(jnp.int32).reshape(1), dest)
    return out[:, :CAP].reshape(-1)


def get_kernel(tps, runs, rep_ref, dest_ref, out_ref):
    reps = dest_ref.shape[0]
    devices = reps * tps
    row, col = grid_of((devices, devices))
    same = row // tps == col // tps
    group, below = flag(same), flag(same & (row < col))
    at = grid_of((reps, devices))[1]
    zero = jnp.zeros((reps, devices), F32)
    sends, which = [], []
    for i in range(tps):
        a, w = zero, zero
        for k in range(runs):
            lane = i * runs + k
            hit = flag(dest_ref[:, lane : lane + 1].astype(jnp.int32) == at)
            a = a + hit
            w = w + hit * k
        sends.append(a)
        which.append(w)
    whole = functools.reduce(lambda a, b: a + b, sends)
    r16, c16 = grid_of((reps, reps))
    earlier = small_dot(flag(c16 < r16), whole)
    most = jnp.max(small_dot(whole, group))
    to_me = flag(row == rep_ref[0] * tps + col)
    rank, seen = earlier, zero
    tables = [[None] * tps for _ in range(2)]
    j = grid_of((reps, devices))[1].astype(F32)
    rep_at = grid_of((reps, devices))[0].astype(F32)
    slots, runs_of = [jnp.zeros((1, devices), F32)] * tps, [jnp.zeros((1, devices), F32)] * tps
    sources = [jnp.zeros((1, devices), F32)] * tps
    for i in range(tps):
        slot = seen + small_dot(sends[i], below)
        mine = [small_dot(v, to_me) for v in (sends[i], rank, slot, which[i])]
        for p in range(tps):
            a, r, s, w = (v[:, p : p + 1] for v in mine)
            hit = (r == j) & (a > 0.5)
            get = lambda v: jnp.sum(jnp.where(hit, v, F32(0.0)), axis=0, keepdims=True)
            slots[p] = slots[p] + get(s)
            sources[p] = sources[p] + get(rep_at)
            runs_of[p] = runs_of[p] + get((rep_at * tps + i) * runs + w)
        rank = rank + sends[i]
        seen = seen + small_dot(sends[i], group)
    for p in range(tps):
        slot = slots[p].astype(jnp.int32)
        turn = lax.div(slot, jnp.int32(CAP))
        out_ref[0, p : p + 1, :] = sources[p].astype(jnp.int32) * CAP + slot - turn * CAP
        out_ref[1, p : p + 1, :] = turn
        out_ref[2, p : p + 1, :] = runs_of[p].astype(jnp.int32)
    out_ref[3] = jnp.broadcast_to(most, (tps, devices)).astype(jnp.int32)


def get_lists(dest, rep, tps, runs):
    devices = dest.shape[0] * tps
    out = pl.pallas_call(
        functools.partial(get_kernel, tps, runs),
        out_shape=jax.ShapeDtypeStruct((4, tps, devices), jnp.int32),
        in_specs=[pl.BlockSpec(memory_space=pltpu.SMEM), pl.BlockSpec(memory_space=VM)],
        out_specs=pl.BlockSpec(memory_space=VM),
        cost_estimate=LIGHT,
        name="get_lists",
    )(rep.astype(jnp.int32).reshape(1), dest)
    tables = out[:, :, :runs].reshape(4, tps * runs)
    return tables[0], tables[1], tables[2], tables[3, 0]


def sum_kernel(parts_ref, *refs):
    total = parts_ref[0].astype(F32)
    for k in range(1, parts_ref.shape[0]):
        total = total + parts_ref[k].astype(F32)
    refs[-1][...] = total


def sum_parts(parts, after):
    return pl.pallas_call(
        sum_kernel,
        out_shape=jax.ShapeDtypeStruct(parts.shape[1:], F32),
        in_specs=[pl.BlockSpec(memory_space=VM)] + [pl.BlockSpec(memory_space=ANY)] * len(after),
        out_specs=pl.BlockSpec(memory_space=VM),
        cost_estimate=LIGHT,
        name="sum",
    )(parts, *after)


def zero_of(a, then=0):
    first = lax.dynamic_index_in_dim(a, then, 0, keepdims=False)
    return (first[(0,) * first.ndim].astype(F32) * 0.0).astype(jnp.int32)


def relay(a, chosen, place):
    got = lax.all_to_all(a[chosen], "rep", split_axis=0, concat_axis=0, tiled=True)
    return got[place]


def per_device(
    hidden,
    ref_gain,
    ref_wq,
    ref_wkv,
    ref_wo,
    score_vec,
    lengths,
    advantage,
    dest,
    policy_norm_gain,
    pol_w,
    cotangent,
):
    tps, reps = lax.axis_size("tp"), lax.axis_size("rep")
    tp, rep = lax.axis_index("tp"), lax.axis_index("rep")
    rows, width = hidden.shape
    model = width * tps
    outs = pol_w.shape[1]
    runs_dev = dest.shape[0] // RUN
    swap, up, down, across = tp_moves(tps)
    starts = [sum(PARTS[:k]) for k in range(len(PARTS))]
    spot = jnp.stack([tp // 2, lax.rem(tp, 2)]).astype(jnp.int32)
    full = lax.all_gather(hidden, "tp", axis=1, tiled=True)

    own = hidden.astype(F32)
    squares = jnp.sum(own * own, axis=1)
    run_own = jnp.pad(dest.reshape(runs_dev, RUN)[:, 0].astype(F32), (0, 128 - runs_dev))
    both = spread(jnp.concatenate([squares, run_own]), "tp")
    inv = lax.rsqrt(jnp.sum(both[:, :rows], axis=0) / model + EPS)
    run_rep = both[:, rows : rows + runs_dev].astype(jnp.int32)
    chosen = send_lists(run_rep, reps, jnp.int32(0))

    cols = outs // tps
    w_rows = pol_w.shape[0]
    turned = lax.ppermute(
        pol_w, ("rep", "tp"), [(t * reps + k, k * tps + t) for t in range(tps) for k in range(reps)]
    )
    line = jnp.pad(run_rep.reshape(1, -1).astype(BF), ((0, 7), (0, outs - tps * runs_dev)))
    spread_w = spread(jnp.concatenate([turned, line], axis=0), "rep")
    w_slice = spread_w[:, :w_rows].reshape(width, outs)
    run_all = spread_w[:, w_rows, : tps * runs_dev]

    x_runs = hidden.reshape(rows // RUN, RUN, width)
    x_sent = x_runs[chosen + zero_of(spread_w)]
    place, turn_of, got_run, most = get_lists(run_all, rep, tps, runs_dev)
    x_got = lax.all_to_all(x_sent, "rep", split_axis=0, concat_axis=0, tiled=True)

    gain = lax.dynamic_slice_in_dim(policy_norm_gain, tp * width, width, 0)[None]
    y_keep, y_give = project(spot, hidden, gain, w_slice, tps, (x_sent, place))
    y_sums = pair_sums(y_keep, lax.ppermute(y_give, "tp", swap))
    y_parts = [y_sums[0]] + [lax.ppermute(y_sums[s], "tp", m) for s, m in ((1, up), (2, across), (3, down))]
    inv_col = inv[:, None]
    y_runs = pack(y_parts, [inv_col]).reshape(rows // RUN, RUN, 128)

    xn = (full.astype(F32) * inv_col * ref_gain).astype(BF)
    q = jnp.dot(xn, ref_wq, preferred_element_type=F32).astype(BF)
    kv = jnp.dot(xn, ref_wkv.reshape(model, -1), preferred_element_type=F32).astype(BF)
    ends = jnp.cumsum(lengths[0])
    cot_all = lax.all_gather(cotangent + zero_of(full).astype(BF), "tp", axis=0, tiled=True)
    attn = attention(ends, q, kv, 0, (x_sent, y_runs, cot_all))
    mine = tp.astype(jnp.int32).reshape(1)
    parts = len(PARTS)
    held = [outproj(spot, attn, ref_wo, tps, k, parts) for k in range(parts)]
    merged = [
        merge(keep, lax.ppermute(give, "tp", swap), keep.shape[0] // 4, tuple(h[0] for h in held)) for keep, give in held
    ]
    sums = [ring_sum(m, up, down) for m in merged]
    stages = [stage for _, stage in sums]
    then = zero_of(merged[0][0]) + zero_of(merged[1][0])
    weights = [
        token_weights(mine, ends, advantage[0], full, score_vec[None], *stage, start)[:1]
        for stage, start in zip(stages, starts, strict=True)
    ]

    y_got = lax.all_to_all(
        y_runs[chosen + zero_of(x_got, then)], "rep", split_axis=0, concat_axis=0, tiled=True
    )

    def later_turns(a, held, begin):
        def again(state):
            turn, now = state
            came = relay(a, send_lists(run_rep, reps, turn), place)
            return turn + 1, jnp.where((turn_of == turn)[:, None, None], came, now)

        return lax.while_loop(lambda state: state[0] * CAP < most, again, (begin, held))[1]

    y_pol = later_turns(y_runs, y_got[place], jnp.int32(1)).reshape(rows, 128)
    last = zero_of(sums[0][0]) + zero_of(sums[1][0])
    x_pol = later_turns(x_runs, x_got[place + last], 1 + last).reshape(rows, width)
    inv_pol = y_pol[:, cols : cols + 1].astype(F32) + y_pol[:, cols + 1 : cols + 2].astype(F32)
    y_all = lax.all_gather(y_pol[:, :cols], "tp", axis=1, tiled=True)

    w_mine = jnp.concatenate(weights, axis=1).astype(BF)
    w_all = spread(w_mine.reshape(-1), ("rep", "tp"))
    cols_of = (tps, runs_dev, tuple(zip(starts, PARTS, strict=True)))

    dx_give, dx_keep, gw = policy(spot, tps, model, cols_of, got_run[None], w_all, inv_pol, y_all, cot_all, x_pol, gain, w_slice)

    parts = lax.all_to_all(gw.reshape(reps, w_rows, outs), "rep", split_axis=0, concat_axis=0, tiled=True)

    x, c = spot[0], spot[1]
    n = tps // 2
    dx_took = lax.ppermute(dx_give, "tp", swap)
    pieces, places = [], []
    for s, move in ((1, up), (3, down), (2, across), (0, None)):
        pair = [dx_keep[s], dx_took[s]]
        if move is not None:
            pair = [lax.ppermute(v, "tp", move) for v in pair]
        origin = lax.rem(x - s + n, n) * 2
        pieces += pair
        places += [origin + c, origin + 1 - c]
    places = jnp.stack(places).astype(jnp.int32)
    policy_input_gradient = place_columns(places, pieces)

    back = [(k * tps + t, t * reps + k) for t in range(tps) for k in range(reps)]
    total = sum_parts(parts, (pieces[5],))
    grad_weight = lax.ppermute(total, ("rep", "tp"), back)
    gain_own = lax.dynamic_slice_in_dim(policy_norm_gain, (rep * tps + tp) * w_rows, w_rows, 0)
    policy_gain_gradient = jnp.sum(grad_weight * pol_w.astype(F32), axis=1) / gain_own
    return (policy_input_gradient, grad_weight, policy_gain_gradient)


def solution(mesh):
    return jax.shard_map(
        per_device,
        mesh=mesh,
        in_specs=(
            P("rep", "tp"),
            P(),
            P(None, "tp"),
            P(None, None, "tp"),
            P("tp", None),
            P(),
            P("rep", None),
            P("rep", None),
            P(("rep", "tp")),
            P(),
            P(("rep", "tp"), None),
            P(("rep", "tp"), None),
        ),
        out_specs=(P(("rep", "tp"), None), P(("rep", "tp"), None), P(("rep", "tp"))),
        check_vma=False,
    )
```

```python
import functools

import jax
import jax.numpy as jnp
from jax import lax
from jax.experimental import pallas as pl
from jax.experimental.pallas import tpu as pltpu
from jax.sharding import PartitionSpec as P

HD = 128
RUN = 8
CAP = 22
BLOCK = 256
PARTS = (512, 512)
DEPTH = 3
TILE = 64
EPS = 1e-6
BF = jnp.bfloat16
F32 = jnp.float32
VMEM_LIMIT = 24 * 1024 * 1024
ANY = pl.ANY
LIGHT = pl.CostEstimate(flops=1, bytes_accessed=1, transcendentals=0)
VM = pltpu.VMEM


def pull(copies):
    for c in copies:
        c.start()


def project_kernel(cols, spot_ref, x_ref, gain_ref, w_ref, *refs):
    keep_ref, give_ref, both = refs[-3:]
    half = x_ref.shape[0] // 2
    n = keep_ref.shape[0]
    for i in range(2):
        xg = (x_ref[i * half : (i + 1) * half, :].astype(F32) * gain_ref[...]).astype(BF)
        part = jnp.dot(xg, w_ref[...], preferred_element_type=F32).astype(BF)
        for t in range(2 * n):
            both[t, :, i * cols : (i + 1) * cols] = part[:, t * cols : (t + 1) * cols]
    x, c = spot_ref[0], spot_ref[1]
    for s in range(n):
        owner = lax.rem(x + s, n) * 2
        keep_ref[s] = both[owner + c]
        give_ref[s] = both[owner + 1 - c]


def project(spot, x, gain, w, tps, after):
    rows, cols = x.shape[0], w.shape[1] // tps
    shape = (tps // 2, rows // 2, 2 * cols)
    return pl.pallas_call(
        functools.partial(project_kernel, cols),
        out_shape=(jax.ShapeDtypeStruct(shape, BF),) * 2,
        in_specs=[pl.BlockSpec(memory_space=pltpu.SMEM)]
        + [pl.BlockSpec(memory_space=VM)] * 3
        + [pl.BlockSpec(memory_space=ANY)] * len(after),
        out_specs=(pl.BlockSpec(memory_space=VM),) * 2,
        scratch_shapes=[VM((tps,) + shape[1:], BF)],
        compiler_params=pltpu.CompilerParams(vmem_limit_bytes=VMEM_LIMIT),
        cost_estimate=LIGHT,
        name="project",
    )(spot, x, gain, w, *after)


def pair_kernel(keep_ref, took_ref, *refs):
    out_refs = refs[-keep_ref.shape[0] :]
    for s, out_ref in enumerate(out_refs):
        out_ref[...] = (keep_ref[s].astype(F32) + took_ref[s].astype(F32)).astype(BF)


def pair_sums(keep, took, after):
    n = keep.shape[0]
    return pl.pallas_call(
        pair_kernel,
        out_shape=(jax.ShapeDtypeStruct(keep.shape[1:], BF),) * n,
        in_specs=[pl.BlockSpec(memory_space=VM)] * 2 + [pl.BlockSpec(memory_space=ANY)] * len(after),
        out_specs=(pl.BlockSpec(memory_space=VM),) * n,
        cost_estimate=LIGHT,
        name="pair",
    )(keep, took, *after)


def pack_kernel(pieces, scales, *refs):
    inv_refs, out_ref = refs[pieces : pieces + scales], refs[-1]
    scales = jnp.concatenate([r[...] for r in inv_refs], axis=0)
    total = refs[0][...].astype(F32)
    for j in range(1, pieces):
        total = total + refs[j][...].astype(F32)
    half, cols = total.shape[0], total.shape[1] // 2
    lane = lax.broadcasted_iota(jnp.int32, (half, out_ref.shape[1] - cols), 1)
    for i in range(2):
        here = slice(i * half, (i + 1) * half)
        inv = scales[here, :]
        hi = inv.astype(BF).astype(F32)
        stats = jnp.where(lane == 0, hi, jnp.where(lane == 1, inv - hi, F32(0.0)))
        y = total[:, i * cols : (i + 1) * cols] * inv
        out_ref[here, :] = jnp.concatenate([y, stats], axis=1).astype(BF)


def pack(pieces, invs, after):
    rows = 2 * pieces[0].shape[0]
    return pl.pallas_call(
        functools.partial(pack_kernel, len(pieces), len(invs)),
        out_shape=jax.ShapeDtypeStruct((rows, 128), BF),
        in_specs=[pl.BlockSpec(memory_space=VM)] * (len(pieces) + len(invs))
        + [pl.BlockSpec(memory_space=ANY)] * len(after),
        out_specs=pl.BlockSpec(memory_space=VM),
        cost_estimate=LIGHT,
        name="pack",
    )(*pieces, *invs, *after)


def attention_kernel(ends_ref, qkv_ref, *refs):
    out_ref = refs[-1]
    rows, wide = out_ref.shape
    q_ref = kv_ref = qkv_ref
    for block in range(rows // BLOCK):
        base = block * BLOCK
        low = max(0, base - 2 * BLOCK)
        high = base + BLOCK
        width = high - low
        row = lax.broadcasted_iota(jnp.int32, (BLOCK, 1), 0) + base
        start = jnp.zeros((BLOCK, 1), jnp.int32)
        for k in range(ends_ref.shape[0]):
            end = ends_ref[k]
            start = jnp.where(row >= end, end, start)
        col = lax.broadcasted_iota(jnp.int32, (BLOCK, width), 1) + low
        allowed = (col >= start) & (col <= row)
        keys = kv_ref[low:high, wide : wide + HD]
        values = kv_ref[low:high, wide + HD :]
        here = slice(block * BLOCK, (block + 1) * BLOCK)
        for head in range(wide // HD):
            lanes = slice(head * HD, (head + 1) * HD)
            s = lax.dot_general(q_ref[here, lanes], keys, (((1,), (1,)), ((), ())), preferred_element_type=F32)
            s = jnp.where(allowed, s * F32(HD**-0.5), F32(-1e30))
            e = jnp.exp(s - jnp.max(s, axis=-1, keepdims=True))
            p = (e / jnp.sum(e, axis=-1, keepdims=True)).astype(BF)
            o = lax.dot_general(p, values, (((1,), (0,)), ((), ())), preferred_element_type=F32)
            out_ref[here, lanes] = o.astype(BF)


def attention(ends, qkv, width, after):
    rows = qkv.shape[0]
    return pl.pallas_call(
        attention_kernel,
        out_shape=jax.ShapeDtypeStruct((rows, width), BF),
        in_specs=[pl.BlockSpec(memory_space=pltpu.SMEM), pl.BlockSpec(memory_space=VM)]
        + [pl.BlockSpec(memory_space=ANY)] * len(after),
        out_specs=pl.BlockSpec(memory_space=VM),
        compiler_params=pltpu.CompilerParams(vmem_limit_bytes=VMEM_LIMIT),
        cost_estimate=LIGHT,
        name="attention",
    )(ends, qkv, *after)


def outproj_kernel(block, at_ref, attn_ref, wo_ref, *refs):
    keep_ref, give_ref, a = refs[-3:]
    x, c, n = at_ref[0], at_ref[1], a.shape[0] // (2 * block)

    @pl.when(pl.program_id(0) == 0)
    def _():
        for other in range(2):
            core = c if other == 0 else 1 - c
            for s in range(n):
                owner = lax.rem(x + s, n) * 2 + core
                here = pl.ds(pl.multiple_of(owner * block, block), block)
                a[(other * n + s) * block : (other * n + s + 1) * block, :] = attn_ref[here, :]

    out = jnp.dot(a[...], wo_ref[...], preferred_element_type=F32).astype(BF)
    keep_ref[...] = out[: n * block]
    give_ref[...] = out[n * block :]


def outproj(place, attn, wo, tps, part, parts, after):
    rows, depth = attn.shape[0] // parts, attn.shape[1]
    model = wo.shape[1]
    step = model // 5
    half = pl.BlockSpec((rows // 2, step), lambda i: (0, i))
    return pl.pallas_call(
        functools.partial(outproj_kernel, rows // tps),
        out_shape=(jax.ShapeDtypeStruct((rows // 2, model), BF),) * 2,
        grid=(5,),
        in_specs=[
            pl.BlockSpec(memory_space=pltpu.SMEM),
            pl.BlockSpec((rows, depth), lambda i: (part, 0)),
            pl.BlockSpec((depth, step), lambda i: (0, i)),
        ]
        + [pl.BlockSpec(memory_space=ANY)] * len(after),
        out_specs=(half, half),
        scratch_shapes=[VM((rows, depth), BF)],
        compiler_params=pltpu.CompilerParams(vmem_limit_bytes=VMEM_LIMIT),
        cost_estimate=LIGHT,
        name="outproj",
    )(place, attn, wo, *after)


def merge_kernel(block, keep_ref, took_ref, *refs):
    up_ref, down_ref, rest_ref = refs[-3:]
    half = block // 2
    add = lambda lo, hi: (keep_ref[lo:hi, :].astype(F32) + took_ref[lo:hi, :].astype(F32)).astype(BF)
    far, near_down = 2 * block, 3 * block
    up_ref[:half, :] = add(far, far + half)
    up_ref[half:, :] = add(block + half, 2 * block)
    down_ref[:half, :] = add(near_down, near_down + half)
    down_ref[half:, :] = add(far + half, far + block)
    rest_ref[:block, :] = add(0, block)
    rest_ref[block : block + half, :] = add(block, block + half)
    rest_ref[block + half :, :] = add(near_down + half, near_down + block)


def merge(keep, took, block, after):
    rows, model = keep.shape
    step = model // 2
    spec = lambda n: pl.BlockSpec((n, step), lambda i: (0, i))
    shape = lambda n: jax.ShapeDtypeStruct((n, model), BF)
    return pl.pallas_call(
        functools.partial(merge_kernel, block),
        out_shape=(shape(block), shape(block), shape(2 * block)),
        grid=(2,),
        in_specs=[spec(rows), spec(rows)] + [pl.BlockSpec(memory_space=ANY)] * len(after),
        out_specs=(spec(block), spec(block), spec(2 * block)),
        compiler_params=pltpu.CompilerParams(vmem_limit_bytes=VMEM_LIMIT),
        cost_estimate=LIGHT,
        name="merge",
    )(keep, took, *after)


def pass_kernel(block, below_ref, above_ref, rest_ref, up_ref, down_ref):
    half = block // 2
    add = lambda a, b: (a.astype(F32) + b.astype(F32)).astype(BF)
    up_ref[...] = add(rest_ref[block : block + half, :], below_ref[:half, :])
    down_ref[...] = add(rest_ref[block + half :, :], above_ref[half:, :])


def pass_on(below, above, rest):
    block, model = below.shape
    return pl.pallas_call(
        functools.partial(pass_kernel, block),
        out_shape=(jax.ShapeDtypeStruct((block // 2, model), BF),) * 2,
        in_specs=[pl.BlockSpec(memory_space=VM)] * 3,
        out_specs=(pl.BlockSpec(memory_space=VM),) * 2,
        cost_estimate=LIGHT,
        name="pass",
    )(below, above, rest)


def ring_sum(merged, up, down):
    go_up, go_down, rest = merged
    below, above = lax.ppermute(go_up, "tp", up), lax.ppermute(go_down, "tp", down)
    up2, down2 = pass_on(below, above, rest)
    return up2, (rest, below, above, lax.ppermute(up2, "tp", up), lax.ppermute(down2, "tp", down))


def score_kernel(first, order_ref, ends_ref, adv_ref, x, vec_ref, *refs):
    rest_ref, below_ref, above_ref, below2_ref, above2_ref, out_ref = refs
    rows, model = x.shape
    half = rows // 2
    own = order_ref[0] * rows
    one = jnp.zeros((rows, 128), F32)
    two = jnp.zeros((rows, 128), F32)
    for lane in range(0, model, 128):
        cols = slice(lane, lane + 128)
        get = lambda ref, lo, hi: ref[lo:hi, cols].astype(F32)
        near = jnp.concatenate(
            [
                get(below2_ref, 0, half) + get(above_ref, 0, half),
                get(below_ref, half, rows) + get(above2_ref, 0, half),
            ],
            axis=0,
        )
        total = get(x, 0, rows) + get(rest_ref, 0, rows) + near
        one = one + total * vec_ref[:, cols]
        two = two + total * total
    mean = jnp.sum(two, axis=-1, keepdims=True) * F32(1.0 / model)
    score = jnp.sum(one, axis=-1, keepdims=True) * lax.rsqrt(mean + EPS)
    row = lax.broadcasted_iota(jnp.int32, (rows, 1), 0) + own + first
    adv = jnp.full((rows, 1), adv_ref[0], F32)
    for k in range(1, ends_ref.shape[0]):
        adv = jnp.where(row >= ends_ref[k - 1], adv_ref[k], adv)
    weight = jnp.broadcast_to(adv - score, (rows, 128))
    out_ref[...] = jnp.transpose(weight)[:8, :].astype(BF).astype(F32)


def token_weights(own, ends, adv, x, vec, rest, below, above, below2, above2, first):
    rows, model = below.shape
    return pl.pallas_call(
        functools.partial(score_kernel, first),
        out_shape=jax.ShapeDtypeStruct((8, rows), F32),
        in_specs=[pl.BlockSpec(memory_space=pltpu.SMEM)] * 3
        + [pl.BlockSpec(memory_space=VM)] * 7,
        out_specs=pl.BlockSpec(memory_space=VM),
        compiler_params=pltpu.CompilerParams(vmem_limit_bytes=VMEM_LIMIT),
        cost_estimate=LIGHT,
        name="score",
    )(own, ends, adv, x, vec, rest, below, above, below2, above2)


def own_weights(run_ref, all_ref, cols_of, out_ref):
    tps, runs_dev, spans = cols_of
    devices = all_ref.shape[0]
    runs = run_ref.shape[1]
    rows = out_ref.shape[0]
    run = run_ref[...]
    rep, at = lax.div(run, tps * runs_dev), lax.rem(run, tps * runs_dev) * RUN
    device, lane = jnp.zeros_like(run), jnp.zeros_like(run)
    for start, size in spans:
        share = size // tps
        here = (at >= start) & (at < start + size)
        device = jnp.where(here, rep * tps + lax.div(at - start, share), device)
        lane = jnp.where(here, start // tps + lax.rem(at - start, share), lane)
    down = lambda n, m: lax.broadcasted_iota(jnp.int32, (n, m), 0)
    across = lambda n, m: lax.broadcasted_iota(jnp.int32, (n, m), 1)
    one = lambda m: m.astype(jnp.int32).astype(F32).astype(BF)
    found = lax.dot_general(
        all_ref[...], one(down(devices, runs) == device), (((0,), (0,)), ((), ())), preferred_element_type=F32
    )
    lanes = down(found.shape[0], runs)
    found = jnp.where((lanes >= lane) & (lanes < lane + RUN), found, F32(0.0)).astype(BF)
    fold = one(down(RUN, found.shape[0]) == lax.rem(across(RUN, found.shape[0]), RUN))
    eight = jnp.dot(fold, found, preferred_element_type=F32).astype(BF)
    whose = one(lax.div(down(rows, runs), RUN) == across(rows, runs))
    wide = lax.dot_general(whose, eight, (((1,), (1,)), ((), ())), preferred_element_type=F32)
    wide = jnp.where(lax.rem(down(rows, RUN), RUN) == across(rows, RUN), wide, F32(0.0))
    out_ref[...] = jnp.sum(wide, axis=1, keepdims=True)


def weight_kernel(
    model, cols_of, run_ref, all_ref, inv_ref, y_ref, cot_ref, x_ref, gain_ref, dy_ref, mean_ref, gw_ref, acc, w
):
    i = pl.program_id(0)

    @pl.when(i == 0)
    def _():
        own_weights(run_ref, all_ref, cols_of, w)

    y = y_ref[...].astype(F32)
    here = pl.ds(pl.multiple_of(i * BLOCK, BLOCK), BLOCK)
    dy = (w[here, :] * cot_ref[...].astype(F32) + 0.5 * y).astype(BF)
    dy_ref[...] = dy
    mean_ref[...] = jnp.sum(dy.astype(F32) * y, axis=-1, keepdims=True) * F32(1.0 / model)
    pn = (x_ref[...].astype(F32) * inv_ref[...] * gain_ref[...]).astype(BF)
    part = lax.dot_general(pn, dy, (((0,), (0,)), ((), ())), preferred_element_type=F32)

    @pl.when(i == 0)
    def _():
        acc[...] = part

    @pl.when(i > 0)
    def _():
        acc[...] += part

    @pl.when(i == pl.num_programs(0) - 1)
    def _():
        gw_ref[...] = acc[...].astype(BF)


def input_kernel(spot_ref, inv_ref, mean_ref, dy_ref, x_ref, gain_ref, pw_ref, give_ref, *keep_refs):
    x, c = spot_ref[0], spot_ref[1]
    n = len(keep_refs)
    block = keep_refs[0].shape[0]
    for other in (1, 0):
        for s in range(n):
            owner = lax.rem(x + s, n) * 2 + (c if other == 0 else 1 - c)
            here = pl.ds(pl.multiple_of(owner * block, block), block)
            inv = inv_ref[here, :]
            xhat = x_ref[here, :].astype(F32) * inv
            dpn = lax.dot_general(
                dy_ref[here, :], pw_ref[...], (((1,), (1,)), ((), ())), preferred_element_type=F32
            )
            dx = (inv * (dpn * gain_ref[...] - xhat * mean_ref[here, :])).astype(BF)
            if other:
                give_ref[s] = dx
            else:
                keep_refs[s][...] = dx


def policy(spot, tps, model, cols_of, run, w_all, inv, y, cot, x, gain, pw):
    rows, width = x.shape
    outs = y.shape[1]
    row = lambda n: pl.BlockSpec((BLOCK, n), lambda i: (i, 0))
    whole = lambda *s: pl.BlockSpec(s, lambda i: (0,) * len(s))
    params = pltpu.CompilerParams(vmem_limit_bytes=VMEM_LIMIT)
    dy, mean, gw = pl.pallas_call(
        functools.partial(weight_kernel, model, cols_of),
        out_shape=(
            jax.ShapeDtypeStruct((rows, outs), BF),
            jax.ShapeDtypeStruct((rows, 1), F32),
            jax.ShapeDtypeStruct((width, outs), BF),
        ),
        grid=(rows // BLOCK,),
        in_specs=[whole(*run.shape), whole(*w_all.shape), row(1), row(outs), row(outs), row(width), whole(1, width)],
        out_specs=(row(outs), row(1), whole(width, outs)),
        scratch_shapes=[VM((width, outs), F32), VM((rows, 1), F32)],
        compiler_params=params,
        cost_estimate=LIGHT,
        name="weight",
    )(run, w_all, inv, y, cot, x, gain)
    n = tps // 2
    block = jax.ShapeDtypeStruct((rows // tps, width), BF)
    give, *keep = pl.pallas_call(
        input_kernel,
        out_shape=(jax.ShapeDtypeStruct((n, rows // tps, width), BF),) + (block,) * n,
        in_specs=[pl.BlockSpec(memory_space=pltpu.SMEM)] + [pl.BlockSpec(memory_space=VM)] * 6,
        out_specs=(pl.BlockSpec(memory_space=VM),) * (n + 1),
        compiler_params=params,
        cost_estimate=LIGHT,
        name="input",
    )(spot, inv, mean, dy, x, gain, pw)
    return give, keep, gw


def place_kernel(pieces, *refs):
    order_ref, ins, out = refs[0], refs[1 : 1 + pieces], refs[1 + pieces]
    for j in range(pieces):
        width = ins[j].shape[1]
        out[:, pl.ds(pl.multiple_of(order_ref[j] * width, width), width)] = ins[j][...]


def place_columns(order, pieces):
    n, (rows, width) = len(pieces), pieces[0].shape
    return pl.pallas_call(
        functools.partial(place_kernel, n),
        out_shape=jax.ShapeDtypeStruct((rows, n * width), pieces[0].dtype),
        in_specs=[pl.BlockSpec(memory_space=pltpu.SMEM)] + [pl.BlockSpec(memory_space=VM)] * n,
        out_specs=pl.BlockSpec(memory_space=VM),
        cost_estimate=LIGHT,
        name="place",
    )(order, *pieces)


def tp_moves(tps):
    n = tps // 2
    at = lambda x, c: (x % n) * 2 + c
    every = [(x, c) for x in range(n) for c in range(2)]
    return (
        [(at(x, c), at(x, 1 - c)) for x, c in every],
        [(at(x, c), at(x + 1, c)) for x, c in every],
        [(at(x, c), at(x - 1, c)) for x, c in every],
        [(at(x, c), at(x + 2, c)) for x, c in every],
    )


def spread(a, axis):
    n = lax.axis_size(axis)
    return lax.all_to_all(jnp.broadcast_to(a[None], (n,) + a.shape), axis, split_axis=0, concat_axis=0, tiled=True)


def flag(m):
    return m.astype(jnp.int32).astype(F32)


def small_dot(a, b, dims=(((1,), (0,)), ((), ()))):
    return lax.dot_general(a.astype(BF), b.astype(BF), dims, preferred_element_type=F32)


def grid_of(shape):
    return tuple(lax.broadcasted_iota(jnp.int32, shape, d) for d in range(2))


def send_kernel(base_ref, dest_ref, out_ref):
    tps, runs = dest_ref.shape
    reps = out_ref.shape[0]
    devices = reps * tps
    row, col = grid_of((devices, devices))
    same = row // tps == col // tps
    run, at = grid_of((tps, devices))
    sends = jnp.zeros((tps, devices), F32)
    which = jnp.zeros((tps, devices), F32)
    for k in range(runs):
        hit = flag(dest_ref[:, k : k + 1] == at)
        sends = sends + hit
        which = which + hit * k
    which = which + (run * runs).astype(F32)
    r8, c8 = grid_of((tps, tps))
    slot = small_dot(flag(c8 < r8), small_dot(sends, flag(same))) + small_dot(sends, flag(same & (row < col)))
    want = (grid_of((128, devices))[0] + base_ref[0]).astype(F32)
    found = jnp.zeros((128, devices), F32)
    for i in range(tps):
        hit = (slot[i : i + 1] == want) & (sends[i : i + 1] > 0.5)
        found = found + jnp.where(hit, which[i : i + 1], F32(0.0))
    rep, dev = grid_of((reps, devices))
    chosen = small_dot(flag(dev // tps == rep), found, (((1,), (1,)), ((), ())))
    out_ref[...] = chosen.astype(jnp.int32)


def send_lists(dest, reps, turn):
    out = pl.pallas_call(
        send_kernel,
        out_shape=jax.ShapeDtypeStruct((reps, 128), jnp.int32),
        in_specs=[pl.BlockSpec(memory_space=pltpu.SMEM), pl.BlockSpec(memory_space=VM)],
        out_specs=pl.BlockSpec(memory_space=VM),
        cost_estimate=LIGHT,
        name="send_lists",
    )((turn * CAP).astype(jnp.int32).reshape(1), dest)
    return out[:, :CAP].reshape(-1)


def get_kernel(tps, runs, rep_ref, dest_ref, *refs):
    out_ref = refs[-1]
    reps = dest_ref.shape[0]
    devices = reps * tps
    row, col = grid_of((devices, devices))
    same = row // tps == col // tps
    group, below = flag(same), flag(same & (row < col))
    at = grid_of((reps, devices))[1]
    zero = jnp.zeros((reps, devices), F32)
    sends, which = [], []
    for i in range(tps):
        a, w = zero, zero
        for k in range(runs):
            lane = i * runs + k
            hit = flag(dest_ref[:, lane : lane + 1].astype(jnp.int32) == at)
            a = a + hit
            w = w + hit * k
        sends.append(a)
        which.append(w)
    whole = functools.reduce(lambda a, b: a + b, sends)
    r16, c16 = grid_of((reps, reps))
    earlier = small_dot(flag(c16 < r16), whole)
    most = jnp.max(small_dot(whole, group))
    to_me = flag(row == rep_ref[0] * tps + col)
    rank, seen = earlier, zero
    tables = [[None] * tps for _ in range(2)]
    j = grid_of((reps, devices))[1].astype(F32)
    rep_at = grid_of((reps, devices))[0].astype(F32)
    slots, runs_of = [jnp.zeros((1, devices), F32)] * tps, [jnp.zeros((1, devices), F32)] * tps
    sources = [jnp.zeros((1, devices), F32)] * tps
    for i in range(tps):
        slot = seen + small_dot(sends[i], below)
        mine = [small_dot(v, to_me) for v in (sends[i], rank, slot, which[i])]
        for p in range(tps):
            a, r, s, w = (v[:, p : p + 1] for v in mine)
            hit = (r == j) & (a > 0.5)
            get = lambda v: jnp.sum(jnp.where(hit, v, F32(0.0)), axis=0, keepdims=True)
            slots[p] = slots[p] + get(s)
            sources[p] = sources[p] + get(rep_at)
            runs_of[p] = runs_of[p] + get((rep_at * tps + i) * runs + w)
        rank = rank + sends[i]
        seen = seen + small_dot(sends[i], group)
    for p in range(tps):
        slot = slots[p].astype(jnp.int32)
        turn = lax.div(slot, jnp.int32(CAP))
        out_ref[0, p : p + 1, :] = sources[p].astype(jnp.int32) * CAP + slot - turn * CAP
        out_ref[1, p : p + 1, :] = turn
        out_ref[2, p : p + 1, :] = runs_of[p].astype(jnp.int32)
    out_ref[3] = jnp.broadcast_to(most, (tps, devices)).astype(jnp.int32)


def get_lists(dest, rep, tps, runs, after):
    devices = dest.shape[0] * tps
    out = pl.pallas_call(
        functools.partial(get_kernel, tps, runs),
        out_shape=jax.ShapeDtypeStruct((4, tps, devices), jnp.int32),
        in_specs=[pl.BlockSpec(memory_space=pltpu.SMEM), pl.BlockSpec(memory_space=VM)]
        + [pl.BlockSpec(memory_space=ANY)] * len(after),
        out_specs=pl.BlockSpec(memory_space=VM),
        cost_estimate=LIGHT,
        name="get_lists",
    )(rep.astype(jnp.int32).reshape(1), dest, *after)
    tables = out[:, :, :runs].reshape(4, tps * runs)
    return tables[0], tables[1], tables[2], tables[3, 0]


def sum_kernel(parts_ref, *refs):
    total = parts_ref[0].astype(F32)
    for k in range(1, parts_ref.shape[0]):
        total = total + parts_ref[k].astype(F32)
    refs[-1][...] = total


def sum_parts(parts, after):
    return pl.pallas_call(
        sum_kernel,
        out_shape=jax.ShapeDtypeStruct(parts.shape[1:], F32),
        in_specs=[pl.BlockSpec(memory_space=VM)] + [pl.BlockSpec(memory_space=ANY)] * len(after),
        out_specs=pl.BlockSpec(memory_space=VM),
        cost_estimate=LIGHT,
        name="sum",
    )(parts, *after)


def zero_of(a):
    return (a[(0,) * a.ndim].astype(F32) * 0.0).astype(jnp.int32)


def relay(a, chosen, place):
    got = lax.all_to_all(a[chosen], "rep", split_axis=0, concat_axis=0, tiled=True)
    return got[place]


def per_device(
    hidden,
    ref_gain,
    ref_wq,
    ref_wkv,
    ref_wo,
    score_vec,
    lengths,
    advantage,
    dest,
    policy_norm_gain,
    pol_w,
    cotangent,
):
    tps, reps = lax.axis_size("tp"), lax.axis_size("rep")
    tp, rep = lax.axis_index("tp"), lax.axis_index("rep")
    rows, width = hidden.shape
    model = width * tps
    outs = pol_w.shape[1]
    runs_dev = dest.shape[0] // RUN
    swap, up, down, across = tp_moves(tps)
    starts = [sum(PARTS[:k]) for k in range(len(PARTS))]
    spot = jnp.stack([tp // 2, lax.rem(tp, 2)]).astype(jnp.int32)
    full = lax.all_gather(hidden, "tp", axis=1, tiled=True)

    own = hidden.astype(F32)
    squares = jnp.sum(own * own, axis=1)
    run_own = jnp.pad(dest.reshape(runs_dev, RUN)[:, 0].astype(F32), (0, 128 - runs_dev))
    both = spread(jnp.concatenate([squares, run_own]), "tp")
    inv = lax.rsqrt(jnp.sum(both[:, :rows], axis=0) / model + EPS)
    run_rep = both[:, rows : rows + runs_dev].astype(jnp.int32)
    chosen = send_lists(run_rep, reps, jnp.int32(0))

    cols = outs // tps
    w_rows = pol_w.shape[0]
    turned = lax.ppermute(
        pol_w, ("rep", "tp"), [(t * reps + k, k * tps + t) for t in range(tps) for k in range(reps)]
    )
    line = jnp.pad(run_rep.reshape(1, -1).astype(BF), ((0, 7), (0, outs - tps * runs_dev)))
    spread_w = spread(jnp.concatenate([turned, line], axis=0), "rep")
    w_slice = spread_w[:, :w_rows].reshape(width, outs)
    run_all = spread_w[:, w_rows, : tps * runs_dev]

    gain = lax.dynamic_slice_in_dim(policy_norm_gain, tp * width, width, 0)[None]
    w_in = jnp.concatenate([ref_wq, ref_wkv.reshape(model, -1)], axis=1)
    y_keep, y_give = project(spot, hidden, gain, w_slice, tps, (w_in,))
    place, turn_of, got_run, most = get_lists(run_all, rep, tps, runs_dev, (y_keep,))
    y_sums = pair_sums(y_keep, lax.ppermute(y_give, "tp", swap), (place,))
    y_parts = [y_sums[0]] + [lax.ppermute(y_sums[s], "tp", m) for s, m in ((1, up), (2, across), (3, down))]

    x_runs = hidden.reshape(rows // RUN, RUN, width)
    x_sent = x_runs[chosen + zero_of(spread_w)]
    x_got = lax.all_to_all(x_sent, "rep", split_axis=0, concat_axis=0, tiled=True)

    inv_col = inv[:, None]

    xn = (full.astype(F32) * inv_col * ref_gain).astype(BF)
    qkv = jnp.dot(xn, w_in, preferred_element_type=F32).astype(BF)
    ends = jnp.cumsum(lengths[0])
    attn = attention(ends, qkv, ref_wq.shape[1], (x_sent, *y_parts))
    mine = tp.astype(jnp.int32).reshape(1)
    parts = len(PARTS)
    cot_all = lax.all_gather(cotangent + zero_of(full).astype(BF), "tp", axis=0, tiled=True)
    held = [outproj(spot, attn, ref_wo, tps, k, parts, (cot_all,) if k else ()) for k in range(parts)]
    merged = [
        merge(keep, lax.ppermute(give, "tp", swap), keep.shape[0] // 4, tuple(h[0] for h in held)) for keep, give in held
    ]
    sums = [ring_sum(m, up, down) for m in merged]
    stages = [stage for _, stage in sums]
    y_runs = pack(y_parts, [inv_col], (x_got, stages[0][1])).reshape(rows // RUN, RUN, 128)
    weights = [
        token_weights(
            mine,
            ends,
            advantage[0],
            lax.dynamic_slice_in_dim(full, start + tp * (size // tps), size // tps, 0),
            score_vec[None],
            *stage,
            start,
        )[:1]
        for stage, start, size in zip(stages, starts, PARTS, strict=True)
    ]

    y_got = lax.all_to_all(
        y_runs[chosen], "rep", split_axis=0, concat_axis=0, tiled=True
    )

    def later_turns(a, held, begin):
        def again(state):
            turn, now = state
            came = relay(a, send_lists(run_rep, reps, turn), place)
            return turn + 1, jnp.where((turn_of == turn)[:, None, None], came, now)

        return lax.while_loop(lambda state: state[0] * CAP < most, again, (begin, held))[1]

    y_pol = later_turns(y_runs, y_got[place + zero_of(sums[-1][0])], jnp.int32(1)).reshape(rows, 128)
    x_pol = later_turns(x_runs, x_got[place], jnp.int32(1)).reshape(rows, width)
    inv_pol = y_pol[:, cols : cols + 1].astype(F32) + y_pol[:, cols + 1 : cols + 2].astype(F32)
    y_all = lax.all_gather(y_pol[:, :cols], "tp", axis=1, tiled=True)

    w_mine = jnp.concatenate(weights, axis=1).astype(BF)
    w_all = spread(w_mine.reshape(-1), ("rep", "tp"))
    cols_of = (tps, runs_dev, tuple(zip(starts, PARTS, strict=True)))

    dx_give, dx_keep, gw = policy(spot, tps, model, cols_of, got_run[None], w_all, inv_pol, y_all, cot_all, x_pol, gain, w_slice)

    parts = lax.all_to_all(gw.reshape(reps, w_rows, outs), "rep", split_axis=0, concat_axis=0, tiled=True)

    x, c = spot[0], spot[1]
    n = tps // 2
    dx_took = lax.ppermute(dx_give, "tp", swap)
    pieces, places = [], []
    for s, move in ((1, up), (3, down), (2, across), (0, None)):
        pair = [dx_keep[s], dx_took[s]]
        if move is not None:
            pair = [lax.ppermute(v, "tp", move) for v in pair]
        origin = lax.rem(x - s + n, n) * 2
        pieces += pair
        places += [origin + c, origin + 1 - c]
    places = jnp.stack(places).astype(jnp.int32)
    policy_input_gradient = place_columns(places, pieces)

    back = [(k * tps + t, t * reps + k) for t in range(tps) for k in range(reps)]
    total = sum_parts(parts, (pieces[5],))
    grad_weight = lax.ppermute(total, ("rep", "tp"), back)
    gain_own = lax.dynamic_slice_in_dim(policy_norm_gain, (rep * tps + tp) * w_rows, w_rows, 0)
    policy_gain_gradient = jnp.sum(grad_weight * pol_w.astype(F32), axis=1) / gain_own
    return (policy_input_gradient, grad_weight, policy_gain_gradient)


def solution(mesh):
    return jax.shard_map(
        per_device,
        mesh=mesh,
        in_specs=(
            P("rep", "tp"),
            P(),
            P(None, "tp"),
            P(None, None, "tp"),
            P("tp", None),
            P(),
            P("rep", None),
            P("rep", None),
            P(("rep", "tp")),
            P(),
            P(("rep", "tp"), None),
            P(("rep", "tp"), None),
        ),
        out_specs=(P(("rep", "tp"), None), P(("rep", "tp"), None), P(("rep", "tp"))),
        check_vma=False,
    )
```

```python
import functools

import jax
import jax.numpy as jnp
from jax import lax
from jax.experimental import pallas as pl
from jax.experimental.pallas import tpu as pltpu
from jax.sharding import PartitionSpec as P

HD = 128
RUN = 8
CAP = 22
BLOCK = 256
PARTS = (512, 512)
DEPTH = 3
TILE = 64
EPS = 1e-6
BF = jnp.bfloat16
F32 = jnp.float32
VMEM_LIMIT = 24 * 1024 * 1024
ANY = pl.ANY
LIGHT = pl.CostEstimate(flops=1, bytes_accessed=1, transcendentals=0)
VM = pltpu.VMEM


def pull(copies):
    for c in copies:
        c.start()


def project_kernel(cols, spot_ref, x_ref, gain_ref, w_ref, *refs):
    keep_ref, give_ref, both = refs[-3:]
    half = x_ref.shape[0] // 2
    n = keep_ref.shape[0]
    for i in range(2):
        xg = (x_ref[i * half : (i + 1) * half, :].astype(F32) * gain_ref[...]).astype(BF)
        part = jnp.dot(xg, w_ref[...], preferred_element_type=F32).astype(BF)
        for t in range(2 * n):
            both[t, :, i * cols : (i + 1) * cols] = part[:, t * cols : (t + 1) * cols]
    x, c = spot_ref[0], spot_ref[1]
    for s in range(n):
        owner = lax.rem(x + s, n) * 2
        keep_ref[s] = both[owner + c]
        give_ref[s] = both[owner + 1 - c]


def project(spot, x, gain, w, tps, after):
    rows, cols = x.shape[0], w.shape[1] // tps
    shape = (tps // 2, rows // 2, 2 * cols)
    return pl.pallas_call(
        functools.partial(project_kernel, cols),
        out_shape=(jax.ShapeDtypeStruct(shape, BF),) * 2,
        in_specs=[pl.BlockSpec(memory_space=pltpu.SMEM)]
        + [pl.BlockSpec(memory_space=VM)] * 3
        + [pl.BlockSpec(memory_space=ANY)] * len(after),
        out_specs=(pl.BlockSpec(memory_space=VM),) * 2,
        scratch_shapes=[VM((tps,) + shape[1:], BF)],
        compiler_params=pltpu.CompilerParams(vmem_limit_bytes=VMEM_LIMIT),
        cost_estimate=LIGHT,
        name="project",
    )(spot, x, gain, w, *after)


def pair_kernel(keep_ref, took_ref, *refs):
    out_refs = refs[-keep_ref.shape[0] :]
    for s, out_ref in enumerate(out_refs):
        out_ref[...] = (keep_ref[s].astype(F32) + took_ref[s].astype(F32)).astype(BF)


def pair_sums(keep, took, after):
    n = keep.shape[0]
    return pl.pallas_call(
        pair_kernel,
        out_shape=(jax.ShapeDtypeStruct(keep.shape[1:], BF),) * n,
        in_specs=[pl.BlockSpec(memory_space=VM)] * 2 + [pl.BlockSpec(memory_space=ANY)] * len(after),
        out_specs=(pl.BlockSpec(memory_space=VM),) * n,
        cost_estimate=LIGHT,
        name="pair",
    )(keep, took, *after)


def pack_kernel(pieces, scales, *refs):
    inv_refs, out_ref = refs[pieces : pieces + scales], refs[-1]
    scales = jnp.concatenate([r[...] for r in inv_refs], axis=0)
    total = refs[0][...].astype(F32)
    for j in range(1, pieces):
        total = total + refs[j][...].astype(F32)
    half, cols = total.shape[0], total.shape[1] // 2
    lane = lax.broadcasted_iota(jnp.int32, (half, out_ref.shape[1] - cols), 1)
    for i in range(2):
        here = slice(i * half, (i + 1) * half)
        inv = scales[here, :]
        hi = inv.astype(BF).astype(F32)
        stats = jnp.where(lane == 0, hi, jnp.where(lane == 1, inv - hi, F32(0.0)))
        y = total[:, i * cols : (i + 1) * cols] * inv
        out_ref[here, :] = jnp.concatenate([y, stats], axis=1).astype(BF)


def pack(pieces, invs, after):
    rows = 2 * pieces[0].shape[0]
    return pl.pallas_call(
        functools.partial(pack_kernel, len(pieces), len(invs)),
        out_shape=jax.ShapeDtypeStruct((rows, 128), BF),
        in_specs=[pl.BlockSpec(memory_space=VM)] * (len(pieces) + len(invs))
        + [pl.BlockSpec(memory_space=ANY)] * len(after),
        out_specs=pl.BlockSpec(memory_space=VM),
        cost_estimate=LIGHT,
        name="pack",
    )(*pieces, *invs, *after)


def attention_kernel(ends_ref, qkv_ref, *refs):
    out_ref = refs[-1]
    rows, wide = out_ref.shape
    q_ref = kv_ref = qkv_ref
    for block in range(rows // BLOCK):
        base = block * BLOCK
        low = max(0, base - 2 * BLOCK)
        high = base + BLOCK
        width = high - low
        row = lax.broadcasted_iota(jnp.int32, (BLOCK, 1), 0) + base
        start = jnp.zeros((BLOCK, 1), jnp.int32)
        for k in range(ends_ref.shape[0]):
            end = ends_ref[k]
            start = jnp.where(row >= end, end, start)
        col = lax.broadcasted_iota(jnp.int32, (BLOCK, width), 1) + low
        allowed = (col >= start) & (col <= row)
        keys = kv_ref[low:high, wide : wide + HD]
        values = kv_ref[low:high, wide + HD :]
        here = slice(block * BLOCK, (block + 1) * BLOCK)
        for head in range(wide // HD):
            lanes = slice(head * HD, (head + 1) * HD)
            s = lax.dot_general(q_ref[here, lanes], keys, (((1,), (1,)), ((), ())), preferred_element_type=F32)
            s = jnp.where(allowed, s * F32(HD**-0.5), F32(-1e30))
            e = jnp.exp(s - jnp.max(s, axis=-1, keepdims=True))
            p = (e / jnp.sum(e, axis=-1, keepdims=True)).astype(BF)
            o = lax.dot_general(p, values, (((1,), (0,)), ((), ())), preferred_element_type=F32)
            out_ref[here, lanes] = o.astype(BF)


def attention(ends, qkv, width, after):
    rows = qkv.shape[0]
    return pl.pallas_call(
        attention_kernel,
        out_shape=jax.ShapeDtypeStruct((rows, width), BF),
        in_specs=[pl.BlockSpec(memory_space=pltpu.SMEM), pl.BlockSpec(memory_space=VM)]
        + [pl.BlockSpec(memory_space=ANY)] * len(after),
        out_specs=pl.BlockSpec(memory_space=VM),
        compiler_params=pltpu.CompilerParams(vmem_limit_bytes=VMEM_LIMIT),
        cost_estimate=LIGHT,
        name="attention",
    )(ends, qkv, *after)


def outproj_kernel(block, at_ref, attn_ref, wo_ref, *refs):
    keep_ref, give_ref, a = refs[-3:]
    x, c, n = at_ref[0], at_ref[1], a.shape[0] // (2 * block)

    @pl.when(pl.program_id(0) == 0)
    def _():
        for other in range(2):
            core = c if other == 0 else 1 - c
            for s in range(n):
                owner = lax.rem(x + s, n) * 2 + core
                here = pl.ds(pl.multiple_of(owner * block, block), block)
                a[(other * n + s) * block : (other * n + s + 1) * block, :] = attn_ref[here, :]

    out = jnp.dot(a[...], wo_ref[...], preferred_element_type=F32).astype(BF)
    keep_ref[...] = out[: n * block]
    give_ref[...] = out[n * block :]


def outproj(place, attn, wo, tps, part, parts, after):
    rows, depth = attn.shape[0] // parts, attn.shape[1]
    model = wo.shape[1]
    step = model // 5
    half = pl.BlockSpec((rows // 2, step), lambda i: (0, i))
    return pl.pallas_call(
        functools.partial(outproj_kernel, rows // tps),
        out_shape=(jax.ShapeDtypeStruct((rows // 2, model), BF),) * 2,
        grid=(5,),
        in_specs=[
            pl.BlockSpec(memory_space=pltpu.SMEM),
            pl.BlockSpec((rows, depth), lambda i: (part, 0)),
            pl.BlockSpec((depth, step), lambda i: (0, i)),
        ]
        + [pl.BlockSpec(memory_space=ANY)] * len(after),
        out_specs=(half, half),
        scratch_shapes=[VM((rows, depth), BF)],
        compiler_params=pltpu.CompilerParams(vmem_limit_bytes=VMEM_LIMIT),
        cost_estimate=LIGHT,
        name="outproj",
    )(place, attn, wo, *after)


def merge_kernel(block, keep_ref, took_ref, *refs):
    up_ref, down_ref, rest_ref = refs[-3:]
    half = block // 2
    add = lambda lo, hi: (keep_ref[lo:hi, :].astype(F32) + took_ref[lo:hi, :].astype(F32)).astype(BF)
    far, near_down = 2 * block, 3 * block
    up_ref[:half, :] = add(far, far + half)
    up_ref[half:, :] = add(block + half, 2 * block)
    down_ref[:half, :] = add(near_down, near_down + half)
    down_ref[half:, :] = add(far + half, far + block)
    rest_ref[:block, :] = add(0, block)
    rest_ref[block : block + half, :] = add(block, block + half)
    rest_ref[block + half :, :] = add(near_down + half, near_down + block)


def merge(keep, took, block, after):
    rows, model = keep.shape
    step = model // 2
    spec = lambda n: pl.BlockSpec((n, step), lambda i: (0, i))
    shape = lambda n: jax.ShapeDtypeStruct((n, model), BF)
    return pl.pallas_call(
        functools.partial(merge_kernel, block),
        out_shape=(shape(block), shape(block), shape(2 * block)),
        grid=(2,),
        in_specs=[spec(rows), spec(rows)] + [pl.BlockSpec(memory_space=ANY)] * len(after),
        out_specs=(spec(block), spec(block), spec(2 * block)),
        compiler_params=pltpu.CompilerParams(vmem_limit_bytes=VMEM_LIMIT),
        cost_estimate=LIGHT,
        name="merge",
    )(keep, took, *after)


def pass_kernel(block, below_ref, above_ref, rest_ref, up_ref, down_ref):
    half = block // 2
    add = lambda a, b: (a.astype(F32) + b.astype(F32)).astype(BF)
    up_ref[...] = add(rest_ref[block : block + half, :], below_ref[:half, :])
    down_ref[...] = add(rest_ref[block + half :, :], above_ref[half:, :])


def pass_on(below, above, rest):
    block, model = below.shape
    return pl.pallas_call(
        functools.partial(pass_kernel, block),
        out_shape=(jax.ShapeDtypeStruct((block // 2, model), BF),) * 2,
        in_specs=[pl.BlockSpec(memory_space=VM)] * 3,
        out_specs=(pl.BlockSpec(memory_space=VM),) * 2,
        cost_estimate=LIGHT,
        name="pass",
    )(below, above, rest)


def ring_sum(merged, up, down):
    go_up, go_down, rest = merged
    below, above = lax.ppermute(go_up, "tp", up), lax.ppermute(go_down, "tp", down)
    up2, down2 = pass_on(below, above, rest)
    return up2, (rest, below, above, lax.ppermute(up2, "tp", up), lax.ppermute(down2, "tp", down))


def score_kernel(first, order_ref, ends_ref, adv_ref, x, vec_ref, *refs):
    rest_ref, below_ref, above_ref, below2_ref, above2_ref, out_ref = refs
    rows, model = x.shape
    half = rows // 2
    own = order_ref[0] * rows
    one = jnp.zeros((rows, 128), F32)
    two = jnp.zeros((rows, 128), F32)
    for lane in range(0, model, 128):
        cols = slice(lane, lane + 128)
        get = lambda ref, lo, hi: ref[lo:hi, cols].astype(F32)
        near = jnp.concatenate(
            [
                get(below2_ref, 0, half) + get(above_ref, 0, half),
                get(below_ref, half, rows) + get(above2_ref, 0, half),
            ],
            axis=0,
        )
        total = get(x, 0, rows) + get(rest_ref, 0, rows) + near
        one = one + total * vec_ref[:, cols]
        two = two + total * total
    mean = jnp.sum(two, axis=-1, keepdims=True) * F32(1.0 / model)
    score = jnp.sum(one, axis=-1, keepdims=True) * lax.rsqrt(mean + EPS)
    row = lax.broadcasted_iota(jnp.int32, (rows, 1), 0) + own + first
    adv = jnp.full((rows, 1), adv_ref[0], F32)
    for k in range(1, ends_ref.shape[0]):
        adv = jnp.where(row >= ends_ref[k - 1], adv_ref[k], adv)
    weight = jnp.broadcast_to(adv - score, (rows, 128))
    out_ref[...] = jnp.transpose(weight)[:8, :].astype(BF).astype(F32)


def token_weights(own, ends, adv, x, vec, rest, below, above, below2, above2, first):
    rows, model = below.shape
    return pl.pallas_call(
        functools.partial(score_kernel, first),
        out_shape=jax.ShapeDtypeStruct((8, rows), F32),
        in_specs=[pl.BlockSpec(memory_space=pltpu.SMEM)] * 3
        + [pl.BlockSpec(memory_space=VM)] * 7,
        out_specs=pl.BlockSpec(memory_space=VM),
        compiler_params=pltpu.CompilerParams(vmem_limit_bytes=VMEM_LIMIT),
        cost_estimate=LIGHT,
        name="score",
    )(own, ends, adv, x, vec, rest, below, above, below2, above2)


def own_weights(run_ref, all_ref, cols_of, out_ref):
    tps, runs_dev, spans = cols_of
    devices = all_ref.shape[0]
    runs = run_ref.shape[1]
    rows = out_ref.shape[0]
    run = run_ref[...]
    rep, at = lax.div(run, tps * runs_dev), lax.rem(run, tps * runs_dev) * RUN
    device, lane = jnp.zeros_like(run), jnp.zeros_like(run)
    for start, size in spans:
        share = size // tps
        here = (at >= start) & (at < start + size)
        device = jnp.where(here, rep * tps + lax.div(at - start, share), device)
        lane = jnp.where(here, start // tps + lax.rem(at - start, share), lane)
    down = lambda n, m: lax.broadcasted_iota(jnp.int32, (n, m), 0)
    across = lambda n, m: lax.broadcasted_iota(jnp.int32, (n, m), 1)
    one = lambda m: m.astype(jnp.int32).astype(F32).astype(BF)
    found = lax.dot_general(
        all_ref[...], one(down(devices, runs) == device), (((0,), (0,)), ((), ())), preferred_element_type=F32
    )
    lanes = down(found.shape[0], runs)
    found = jnp.where((lanes >= lane) & (lanes < lane + RUN), found, F32(0.0)).astype(BF)
    fold = one(down(RUN, found.shape[0]) == lax.rem(across(RUN, found.shape[0]), RUN))
    eight = jnp.dot(fold, found, preferred_element_type=F32).astype(BF)
    whose = one(lax.div(down(rows, runs), RUN) == across(rows, runs))
    wide = lax.dot_general(whose, eight, (((1,), (1,)), ((), ())), preferred_element_type=F32)
    wide = jnp.where(lax.rem(down(rows, RUN), RUN) == across(rows, RUN), wide, F32(0.0))
    out_ref[...] = jnp.sum(wide, axis=1, keepdims=True)


def weight_kernel(
    model, cols_of, run_ref, all_ref, inv_ref, y_ref, cot_ref, x_ref, gain_ref, dy_ref, mean_ref, gw_ref, acc, w
):
    i = pl.program_id(0)

    @pl.when(i == 0)
    def _():
        own_weights(run_ref, all_ref, cols_of, w)

    y = y_ref[...].astype(F32)
    here = pl.ds(pl.multiple_of(i * BLOCK, BLOCK), BLOCK)
    dy = (w[here, :] * cot_ref[...].astype(F32) + 0.5 * y).astype(BF)
    dy_ref[...] = dy
    mean_ref[...] = jnp.sum(dy.astype(F32) * y, axis=-1, keepdims=True) * F32(1.0 / model)
    pn = (x_ref[...].astype(F32) * inv_ref[...] * gain_ref[...]).astype(BF)
    part = lax.dot_general(pn, dy, (((0,), (0,)), ((), ())), preferred_element_type=F32)

    @pl.when(i == 0)
    def _():
        acc[...] = part

    @pl.when(i > 0)
    def _():
        acc[...] += part

    @pl.when(i == pl.num_programs(0) - 1)
    def _():
        gw_ref[...] = acc[...].astype(BF)


def input_kernel(spot_ref, inv_ref, mean_ref, dy_ref, x_ref, gain_ref, pw_ref, give_ref, *keep_refs):
    x, c = spot_ref[0], spot_ref[1]
    n = len(keep_refs)
    block = keep_refs[0].shape[0]
    for other in (1, 0):
        for s in range(n):
            owner = lax.rem(x + s, n) * 2 + (c if other == 0 else 1 - c)
            here = pl.ds(pl.multiple_of(owner * block, block), block)
            inv = inv_ref[here, :]
            xhat = x_ref[here, :].astype(F32) * inv
            dpn = lax.dot_general(
                dy_ref[here, :], pw_ref[...], (((1,), (1,)), ((), ())), preferred_element_type=F32
            )
            dx = (inv * (dpn * gain_ref[...] - xhat * mean_ref[here, :])).astype(BF)
            if other:
                give_ref[s] = dx
            else:
                keep_refs[s][...] = dx


def policy(spot, tps, model, cols_of, run, w_all, inv, y, cot, x, gain, pw):
    rows, width = x.shape
    outs = y.shape[1]
    row = lambda n: pl.BlockSpec((BLOCK, n), lambda i: (i, 0))
    whole = lambda *s: pl.BlockSpec(s, lambda i: (0,) * len(s))
    params = pltpu.CompilerParams(vmem_limit_bytes=VMEM_LIMIT)
    dy, mean, gw = pl.pallas_call(
        functools.partial(weight_kernel, model, cols_of),
        out_shape=(
            jax.ShapeDtypeStruct((rows, outs), BF),
            jax.ShapeDtypeStruct((rows, 1), F32),
            jax.ShapeDtypeStruct((width, outs), BF),
        ),
        grid=(rows // BLOCK,),
        in_specs=[whole(*run.shape), whole(*w_all.shape), row(1), row(outs), row(outs), row(width), whole(1, width)],
        out_specs=(row(outs), row(1), whole(width, outs)),
        scratch_shapes=[VM((width, outs), F32), VM((rows, 1), F32)],
        compiler_params=params,
        cost_estimate=LIGHT,
        name="weight",
    )(run, w_all, inv, y, cot, x, gain)
    n = tps // 2
    block = jax.ShapeDtypeStruct((rows // tps, width), BF)
    give, *keep = pl.pallas_call(
        input_kernel,
        out_shape=(jax.ShapeDtypeStruct((n, rows // tps, width), BF),) + (block,) * n,
        in_specs=[pl.BlockSpec(memory_space=pltpu.SMEM)] + [pl.BlockSpec(memory_space=VM)] * 6,
        out_specs=(pl.BlockSpec(memory_space=VM),) * (n + 1),
        compiler_params=params,
        cost_estimate=LIGHT,
        name="input",
    )(spot, inv, mean, dy, x, gain, pw)
    return give, keep, gw


def place_kernel(pieces, *refs):
    order_ref, ins, out = refs[0], refs[1 : 1 + pieces], refs[1 + pieces]
    for j in range(pieces):
        width = ins[j].shape[1]
        out[:, pl.ds(pl.multiple_of(order_ref[j] * width, width), width)] = ins[j][...]


def place_columns(order, pieces):
    n, (rows, width) = len(pieces), pieces[0].shape
    return pl.pallas_call(
        functools.partial(place_kernel, n),
        out_shape=jax.ShapeDtypeStruct((rows, n * width), pieces[0].dtype),
        in_specs=[pl.BlockSpec(memory_space=pltpu.SMEM)] + [pl.BlockSpec(memory_space=VM)] * n,
        out_specs=pl.BlockSpec(memory_space=VM),
        cost_estimate=LIGHT,
        name="place",
    )(order, *pieces)


def tp_moves(tps):
    n = tps // 2
    at = lambda x, c: (x % n) * 2 + c
    every = [(x, c) for x in range(n) for c in range(2)]
    return (
        [(at(x, c), at(x, 1 - c)) for x, c in every],
        [(at(x, c), at(x + 1, c)) for x, c in every],
        [(at(x, c), at(x - 1, c)) for x, c in every],
        [(at(x, c), at(x + 2, c)) for x, c in every],
    )


def spread(a, axis):
    n = lax.axis_size(axis)
    return lax.all_to_all(jnp.broadcast_to(a[None], (n,) + a.shape), axis, split_axis=0, concat_axis=0, tiled=True)


def flag(m):
    return m.astype(jnp.int32).astype(F32)


def small_dot(a, b, dims=(((1,), (0,)), ((), ()))):
    return lax.dot_general(a.astype(BF), b.astype(BF), dims, preferred_element_type=F32)


def grid_of(shape):
    return tuple(lax.broadcasted_iota(jnp.int32, shape, d) for d in range(2))


def send_kernel(base_ref, dest_ref, out_ref):
    tps, runs = dest_ref.shape
    reps = out_ref.shape[0]
    devices = reps * tps
    row, col = grid_of((devices, devices))
    same = row // tps == col // tps
    run, at = grid_of((tps, devices))
    sends = jnp.zeros((tps, devices), F32)
    which = jnp.zeros((tps, devices), F32)
    for k in range(runs):
        hit = flag(dest_ref[:, k : k + 1] == at)
        sends = sends + hit
        which = which + hit * k
    which = which + (run * runs).astype(F32)
    r8, c8 = grid_of((tps, tps))
    slot = small_dot(flag(c8 < r8), small_dot(sends, flag(same))) + small_dot(sends, flag(same & (row < col)))
    want = (grid_of((128, devices))[0] + base_ref[0]).astype(F32)
    found = jnp.zeros((128, devices), F32)
    for i in range(tps):
        hit = (slot[i : i + 1] == want) & (sends[i : i + 1] > 0.5)
        found = found + jnp.where(hit, which[i : i + 1], F32(0.0))
    rep, dev = grid_of((reps, devices))
    chosen = small_dot(flag(dev // tps == rep), found, (((1,), (1,)), ((), ())))
    out_ref[...] = chosen.astype(jnp.int32)


def send_lists(dest, reps, turn):
    out = pl.pallas_call(
        send_kernel,
        out_shape=jax.ShapeDtypeStruct((reps, 128), jnp.int32),
        in_specs=[pl.BlockSpec(memory_space=pltpu.SMEM), pl.BlockSpec(memory_space=VM)],
        out_specs=pl.BlockSpec(memory_space=VM),
        cost_estimate=LIGHT,
        name="send_lists",
    )((turn * CAP).astype(jnp.int32).reshape(1), dest)
    return out[:, :CAP].reshape(-1)


def get_kernel(tps, runs, rep_ref, dest_ref, *refs):
    out_ref = refs[-1]
    reps = dest_ref.shape[0]
    devices = reps * tps
    row, col = grid_of((devices, devices))
    same = row // tps == col // tps
    group, below = flag(same), flag(same & (row < col))
    at = grid_of((reps, devices))[1]
    zero = jnp.zeros((reps, devices), F32)
    sends, which = [], []
    for i in range(tps):
        a, w = zero, zero
        for k in range(runs):
            lane = i * runs + k
            hit = flag(dest_ref[:, lane : lane + 1].astype(jnp.int32) == at)
            a = a + hit
            w = w + hit * k
        sends.append(a)
        which.append(w)
    whole = functools.reduce(lambda a, b: a + b, sends)
    r16, c16 = grid_of((reps, reps))
    earlier = small_dot(flag(c16 < r16), whole)
    most = jnp.max(small_dot(whole, group))
    to_me = flag(row == rep_ref[0] * tps + col)
    rank, seen = earlier, zero
    tables = [[None] * tps for _ in range(2)]
    j = grid_of((reps, devices))[1].astype(F32)
    rep_at = grid_of((reps, devices))[0].astype(F32)
    slots, runs_of = [jnp.zeros((1, devices), F32)] * tps, [jnp.zeros((1, devices), F32)] * tps
    sources = [jnp.zeros((1, devices), F32)] * tps
    for i in range(tps):
        slot = seen + small_dot(sends[i], below)
        mine = [small_dot(v, to_me) for v in (sends[i], rank, slot, which[i])]
        for p in range(tps):
            a, r, s, w = (v[:, p : p + 1] for v in mine)
            hit = (r == j) & (a > 0.5)
            get = lambda v: jnp.sum(jnp.where(hit, v, F32(0.0)), axis=0, keepdims=True)
            slots[p] = slots[p] + get(s)
            sources[p] = sources[p] + get(rep_at)
            runs_of[p] = runs_of[p] + get((rep_at * tps + i) * runs + w)
        rank = rank + sends[i]
        seen = seen + small_dot(sends[i], group)
    for p in range(tps):
        slot = slots[p].astype(jnp.int32)
        turn = lax.div(slot, jnp.int32(CAP))
        out_ref[0, p : p + 1, :] = sources[p].astype(jnp.int32) * CAP + slot - turn * CAP
        out_ref[1, p : p + 1, :] = turn
        out_ref[2, p : p + 1, :] = runs_of[p].astype(jnp.int32)
    out_ref[3] = jnp.broadcast_to(most, (tps, devices)).astype(jnp.int32)


def get_lists(dest, rep, tps, runs, after):
    devices = dest.shape[0] * tps
    out = pl.pallas_call(
        functools.partial(get_kernel, tps, runs),
        out_shape=jax.ShapeDtypeStruct((4, tps, devices), jnp.int32),
        in_specs=[pl.BlockSpec(memory_space=pltpu.SMEM), pl.BlockSpec(memory_space=VM)]
        + [pl.BlockSpec(memory_space=ANY)] * len(after),
        out_specs=pl.BlockSpec(memory_space=VM),
        cost_estimate=LIGHT,
        name="get_lists",
    )(rep.astype(jnp.int32).reshape(1), dest, *after)
    tables = out[:, :, :runs].reshape(4, tps * runs)
    return tables[0], tables[1], tables[2], tables[3, 0]


def sum_kernel(parts_ref, *refs):
    total = parts_ref[0].astype(F32)
    for k in range(1, parts_ref.shape[0]):
        total = total + parts_ref[k].astype(F32)
    refs[-1][...] = total


def sum_parts(parts, after):
    return pl.pallas_call(
        sum_kernel,
        out_shape=jax.ShapeDtypeStruct(parts.shape[1:], F32),
        in_specs=[pl.BlockSpec(memory_space=VM)] + [pl.BlockSpec(memory_space=ANY)] * len(after),
        out_specs=pl.BlockSpec(memory_space=VM),
        cost_estimate=LIGHT,
        name="sum",
    )(parts, *after)


def zero_of(a):
    return (a[(0,) * a.ndim].astype(F32) * 0.0).astype(jnp.int32)


def relay(a, chosen, place):
    got = lax.all_to_all(a[chosen], "rep", split_axis=0, concat_axis=0, tiled=True)
    return got[place]


def per_device(
    hidden,
    ref_gain,
    ref_wq,
    ref_wkv,
    ref_wo,
    score_vec,
    lengths,
    advantage,
    dest,
    policy_norm_gain,
    pol_w,
    cotangent,
):
    tps, reps = lax.axis_size("tp"), lax.axis_size("rep")
    tp, rep = lax.axis_index("tp"), lax.axis_index("rep")
    rows, width = hidden.shape
    model = width * tps
    outs = pol_w.shape[1]
    runs_dev = dest.shape[0] // RUN
    swap, up, down, across = tp_moves(tps)
    starts = [sum(PARTS[:k]) for k in range(len(PARTS))]
    spot = jnp.stack([tp // 2, lax.rem(tp, 2)]).astype(jnp.int32)
    full = lax.all_gather(hidden, "tp", axis=1, tiled=True)

    own = hidden.astype(F32)
    squares = jnp.sum(own * own, axis=1)
    run_own = jnp.pad(dest.reshape(runs_dev, RUN)[:, 0].astype(F32), (0, 128 - runs_dev))
    both = spread(jnp.concatenate([squares, run_own]), "tp")
    inv = lax.rsqrt(jnp.sum(both[:, :rows], axis=0) / model + EPS)
    run_rep = both[:, rows : rows + runs_dev].astype(jnp.int32)
    chosen = send_lists(run_rep, reps, jnp.int32(0))

    cols = outs // tps
    w_rows = pol_w.shape[0]
    turned = lax.ppermute(
        pol_w, ("rep", "tp"), [(t * reps + k, k * tps + t) for t in range(tps) for k in range(reps)]
    )
    line = jnp.pad(run_rep.reshape(1, -1).astype(BF), ((0, 7), (0, outs - tps * runs_dev)))
    spread_w = spread(jnp.concatenate([turned, line], axis=0), "rep")
    w_slice = spread_w[:, :w_rows].reshape(width, outs)
    run_all = spread_w[:, w_rows, : tps * runs_dev]

    gain = lax.dynamic_slice_in_dim(policy_norm_gain, tp * width, width, 0)[None]
    w_in = jnp.concatenate([ref_wq, ref_wkv.reshape(model, -1)], axis=1)
    y_keep, y_give = project(spot, hidden, gain, w_slice, tps, ())
    y_sums = pair_sums(y_keep, lax.ppermute(y_give, "tp", swap), (w_in,))
    y_parts = [y_sums[0]] + [lax.ppermute(y_sums[s], "tp", m) for s, m in ((1, up), (2, across), (3, down))]

    x_runs = hidden.reshape(rows // RUN, RUN, width)
    x_sent = x_runs[chosen]
    x_got = lax.all_to_all(x_sent, "rep", split_axis=0, concat_axis=0, tiled=True)

    inv_col = inv[:, None]

    xn = (full.astype(F32) * inv_col * ref_gain).astype(BF)
    qkv = jnp.dot(xn, w_in, preferred_element_type=F32).astype(BF)
    ends = jnp.cumsum(lengths[0])
    attn = attention(ends, qkv, ref_wq.shape[1], (x_sent, *y_parts))
    mine = tp.astype(jnp.int32).reshape(1)
    parts = len(PARTS)
    cot_all = lax.all_gather(cotangent, "tp", axis=0, tiled=True)
    held = [outproj(spot, attn, ref_wo, tps, k, parts, (cot_all,) if k else ()) for k in range(parts)]
    merged = [
        merge(keep, lax.ppermute(give, "tp", swap), keep.shape[0] // 4, tuple(h[0] for h in held)) for keep, give in held
    ]
    place, turn_of, got_run, most = get_lists(run_all, rep, tps, runs_dev, (merged[-1][0],))
    sums = [ring_sum(m, up, down) for m in merged]
    stages = [stage for _, stage in sums]
    y_runs = pack(y_parts, [inv_col], (x_got, stages[0][1], place)).reshape(rows // RUN, RUN, 128)
    weights = [
        token_weights(
            mine,
            ends,
            advantage[0],
            lax.dynamic_slice_in_dim(full, start + tp * (size // tps), size // tps, 0),
            score_vec[None],
            *stage,
            start,
        )[:1]
        for stage, start, size in zip(stages, starts, PARTS, strict=True)
    ]

    y_got = lax.all_to_all(
        y_runs[chosen], "rep", split_axis=0, concat_axis=0, tiled=True
    )

    def later_turns(a, held, begin):
        def again(state):
            turn, now = state
            came = relay(a, send_lists(run_rep, reps, turn), place)
            return turn + 1, jnp.where((turn_of == turn)[:, None, None], came, now)

        return lax.while_loop(lambda state: state[0] * CAP < most, again, (begin, held))[1]

    y_pol = later_turns(y_runs, y_got[place + zero_of(sums[-1][0])], jnp.int32(1)).reshape(rows, 128)
    x_pol = later_turns(x_runs, x_got[place], jnp.int32(1)).reshape(rows, width)
    inv_pol = y_pol[:, cols : cols + 1].astype(F32) + y_pol[:, cols + 1 : cols + 2].astype(F32)
    y_all = lax.all_gather(y_pol[:, :cols], "tp", axis=1, tiled=True)

    w_mine = jnp.concatenate(weights, axis=1).astype(BF)
    w_all = spread(w_mine.reshape(-1), ("rep", "tp"))
    cols_of = (tps, runs_dev, tuple(zip(starts, PARTS, strict=True)))

    dx_give, dx_keep, gw = policy(spot, tps, model, cols_of, got_run[None], w_all, inv_pol, y_all, cot_all, x_pol, gain, w_slice)

    parts = lax.all_to_all(gw.reshape(reps, w_rows, outs), "rep", split_axis=0, concat_axis=0, tiled=True)

    x, c = spot[0], spot[1]
    n = tps // 2
    dx_took = lax.ppermute(dx_give, "tp", swap)
    pieces, places = [], []
    for s, move in ((1, up), (3, down), (2, across), (0, None)):
        pair = [dx_keep[s], dx_took[s]]
        if move is not None:
            pair = [lax.ppermute(v, "tp", move) for v in pair]
        origin = lax.rem(x - s + n, n) * 2
        pieces += pair
        places += [origin + c, origin + 1 - c]
    places = jnp.stack(places).astype(jnp.int32)
    policy_input_gradient = place_columns(places, pieces)

    back = [(k * tps + t, t * reps + k) for t in range(tps) for k in range(reps)]
    total = sum_parts(parts, (pieces[5],))
    grad_weight = lax.ppermute(total, ("rep", "tp"), back)
    gain_own = lax.dynamic_slice_in_dim(policy_norm_gain, (rep * tps + tp) * w_rows, w_rows, 0)
    policy_gain_gradient = jnp.sum(grad_weight * pol_w.astype(F32), axis=1) / gain_own
    return (policy_input_gradient, grad_weight, policy_gain_gradient)


def solution(mesh):
    return jax.shard_map(
        per_device,
        mesh=mesh,
        in_specs=(
            P("rep", "tp"),
            P(),
            P(None, "tp"),
            P(None, None, "tp"),
            P("tp", None),
            P(),
            P("rep", None),
            P("rep", None),
            P(("rep", "tp")),
            P(),
            P(("rep", "tp"), None),
            P(("rep", "tp"), None),
        ),
        out_specs=(P(("rep", "tp"), None), P(("rep", "tp"), None), P(("rep", "tp"))),
        check_vma=False,
    )
```

```python
import functools

import jax
import jax.numpy as jnp
from jax import lax
from jax.experimental import pallas as pl
from jax.experimental.pallas import tpu as pltpu
from jax.sharding import PartitionSpec as P

HD = 128
RUN = 8
CAP = 22
BLOCK = 256
PARTS = (512, 512)
DEPTH = 3
TILE = 64
EPS = 1e-6
BF = jnp.bfloat16
F32 = jnp.float32
VMEM_LIMIT = 24 * 1024 * 1024
ANY = pl.ANY
LIGHT = pl.CostEstimate(flops=1, bytes_accessed=1, transcendentals=0)
VM = pltpu.VMEM


def pull(copies):
    for c in copies:
        c.start()


def project_kernel(cols, spot_ref, x_ref, gain_ref, w_ref, *refs):
    keep_ref, give_ref, both = refs[-3:]
    half = x_ref.shape[0] // 2
    n = keep_ref.shape[0]
    for i in range(2):
        xg = (x_ref[i * half : (i + 1) * half, :].astype(F32) * gain_ref[...]).astype(BF)
        part = jnp.dot(xg, w_ref[...], preferred_element_type=F32).astype(BF)
        for t in range(2 * n):
            both[t, :, i * cols : (i + 1) * cols] = part[:, t * cols : (t + 1) * cols]
    x, c = spot_ref[0], spot_ref[1]
    for s in range(n):
        owner = lax.rem(x + s, n) * 2
        keep_ref[s] = both[owner + c]
        give_ref[s] = both[owner + 1 - c]


def project(spot, x, gain, w, tps, after):
    rows, cols = x.shape[0], w.shape[1] // tps
    shape = (tps // 2, rows // 2, 2 * cols)
    return pl.pallas_call(
        functools.partial(project_kernel, cols),
        out_shape=(jax.ShapeDtypeStruct(shape, BF),) * 2,
        in_specs=[pl.BlockSpec(memory_space=pltpu.SMEM)]
        + [pl.BlockSpec(memory_space=VM)] * 3
        + [pl.BlockSpec(memory_space=ANY)] * len(after),
        out_specs=(pl.BlockSpec(memory_space=VM),) * 2,
        scratch_shapes=[VM((tps,) + shape[1:], BF)],
        compiler_params=pltpu.CompilerParams(vmem_limit_bytes=VMEM_LIMIT),
        cost_estimate=LIGHT,
        name="project",
    )(spot, x, gain, w, *after)


def pair_kernel(keep_ref, took_ref, *refs):
    out_refs = refs[-keep_ref.shape[0] :]
    for s, out_ref in enumerate(out_refs):
        out_ref[...] = (keep_ref[s].astype(F32) + took_ref[s].astype(F32)).astype(BF)


def pair_sums(keep, took, after):
    n = keep.shape[0]
    return pl.pallas_call(
        pair_kernel,
        out_shape=(jax.ShapeDtypeStruct(keep.shape[1:], BF),) * n,
        in_specs=[pl.BlockSpec(memory_space=VM)] * 2 + [pl.BlockSpec(memory_space=ANY)] * len(after),
        out_specs=(pl.BlockSpec(memory_space=VM),) * n,
        cost_estimate=LIGHT,
        name="pair",
    )(keep, took, *after)


def pack_kernel(pieces, scales, *refs):
    inv_refs, out_ref = refs[pieces : pieces + scales], refs[-1]
    scales = jnp.concatenate([r[...] for r in inv_refs], axis=0)
    total = refs[0][...].astype(F32)
    for j in range(1, pieces):
        total = total + refs[j][...].astype(F32)
    half, cols = total.shape[0], total.shape[1] // 2
    lane = lax.broadcasted_iota(jnp.int32, (half, out_ref.shape[1] - cols), 1)
    for i in range(2):
        here = slice(i * half, (i + 1) * half)
        inv = scales[here, :]
        hi = inv.astype(BF).astype(F32)
        stats = jnp.where(lane == 0, hi, jnp.where(lane == 1, inv - hi, F32(0.0)))
        y = total[:, i * cols : (i + 1) * cols] * inv
        out_ref[here, :] = jnp.concatenate([y, stats], axis=1).astype(BF)


def pack(pieces, invs, after):
    rows = 2 * pieces[0].shape[0]
    return pl.pallas_call(
        functools.partial(pack_kernel, len(pieces), len(invs)),
        out_shape=jax.ShapeDtypeStruct((rows, 128), BF),
        in_specs=[pl.BlockSpec(memory_space=VM)] * (len(pieces) + len(invs))
        + [pl.BlockSpec(memory_space=ANY)] * len(after),
        out_specs=pl.BlockSpec(memory_space=VM),
        cost_estimate=LIGHT,
        name="pack",
    )(*pieces, *invs, *after)


def attention_kernel(ends_ref, qkv_ref, *refs):
    out_ref = refs[-1]
    rows, wide = out_ref.shape
    q_ref = kv_ref = qkv_ref
    for block in range(rows // BLOCK):
        base = block * BLOCK
        low = max(0, base - 2 * BLOCK)
        high = base + BLOCK
        width = high - low
        row = lax.broadcasted_iota(jnp.int32, (BLOCK, 1), 0) + base
        start = jnp.zeros((BLOCK, 1), jnp.int32)
        for k in range(ends_ref.shape[0]):
            end = ends_ref[k]
            start = jnp.where(row >= end, end, start)
        col = lax.broadcasted_iota(jnp.int32, (BLOCK, width), 1) + low
        allowed = (col >= start) & (col <= row)
        keys = kv_ref[low:high, wide : wide + HD]
        values = kv_ref[low:high, wide + HD :]
        here = slice(block * BLOCK, (block + 1) * BLOCK)
        for head in range(wide // HD):
            lanes = slice(head * HD, (head + 1) * HD)
            s = lax.dot_general(q_ref[here, lanes], keys, (((1,), (1,)), ((), ())), preferred_element_type=F32)
            s = jnp.where(allowed, s * F32(HD**-0.5), F32(-1e30))
            e = jnp.exp(s - jnp.max(s, axis=-1, keepdims=True))
            p = (e / jnp.sum(e, axis=-1, keepdims=True)).astype(BF)
            o = lax.dot_general(p, values, (((1,), (0,)), ((), ())), preferred_element_type=F32)
            out_ref[here, lanes] = o.astype(BF)


def attention(ends, qkv, width, after):
    rows = qkv.shape[0]
    return pl.pallas_call(
        attention_kernel,
        out_shape=jax.ShapeDtypeStruct((rows, width), BF),
        in_specs=[pl.BlockSpec(memory_space=pltpu.SMEM), pl.BlockSpec(memory_space=VM)]
        + [pl.BlockSpec(memory_space=pltpu.HBM)] * len(after),
        out_specs=pl.BlockSpec(memory_space=VM),
        compiler_params=pltpu.CompilerParams(vmem_limit_bytes=VMEM_LIMIT),
        cost_estimate=LIGHT,
        name="attention",
    )(ends, qkv, *after)


def outproj_kernel(block, at_ref, attn_ref, wo_ref, *refs):
    keep_ref, give_ref, a = refs[-3:]
    x, c, n = at_ref[0], at_ref[1], a.shape[0] // (2 * block)

    @pl.when(pl.program_id(0) == 0)
    def _():
        for other in range(2):
            core = c if other == 0 else 1 - c
            for s in range(n):
                owner = lax.rem(x + s, n) * 2 + core
                here = pl.ds(pl.multiple_of(owner * block, block), block)
                a[(other * n + s) * block : (other * n + s + 1) * block, :] = attn_ref[here, :]

    out = jnp.dot(a[...], wo_ref[...], preferred_element_type=F32).astype(BF)
    keep_ref[...] = out[: n * block]
    give_ref[...] = out[n * block :]


def outproj(place, attn, wo, tps, part, parts, after):
    rows, depth = attn.shape[0] // parts, attn.shape[1]
    model = wo.shape[1]
    step = model // 5
    half = pl.BlockSpec((rows // 2, step), lambda i: (0, i))
    return pl.pallas_call(
        functools.partial(outproj_kernel, rows // tps),
        out_shape=(jax.ShapeDtypeStruct((rows // 2, model), BF),) * 2,
        grid=(5,),
        in_specs=[
            pl.BlockSpec(memory_space=pltpu.SMEM),
            pl.BlockSpec((rows, depth), lambda i: (part, 0)),
            pl.BlockSpec((depth, step), lambda i: (0, i)),
        ]
        + [pl.BlockSpec(memory_space=pltpu.HBM)] * len(after),
        out_specs=(half, half),
        scratch_shapes=[VM((rows, depth), BF)],
        compiler_params=pltpu.CompilerParams(vmem_limit_bytes=56 * 1024 * 1024),
        cost_estimate=LIGHT,
        name="outproj",
    )(place, attn, wo, *after)


def merge_kernel(block, keep_ref, took_ref, *refs):
    up_ref, down_ref, rest_ref = refs[-3:]
    half = block // 2
    add = lambda lo, hi: (keep_ref[lo:hi, :].astype(F32) + took_ref[lo:hi, :].astype(F32)).astype(BF)
    far, near_down = 2 * block, 3 * block
    up_ref[:half, :] = add(far, far + half)
    up_ref[half:, :] = add(block + half, 2 * block)
    down_ref[:half, :] = add(near_down, near_down + half)
    down_ref[half:, :] = add(far + half, far + block)
    rest_ref[:block, :] = add(0, block)
    rest_ref[block : block + half, :] = add(block, block + half)
    rest_ref[block + half :, :] = add(near_down + half, near_down + block)


def merge(keep, took, block, after):
    rows, model = keep.shape
    step = model // 2
    spec = lambda n: pl.BlockSpec((n, step), lambda i: (0, i))
    shape = lambda n: jax.ShapeDtypeStruct((n, model), BF)
    return pl.pallas_call(
        functools.partial(merge_kernel, block),
        out_shape=(shape(block), shape(block), shape(2 * block)),
        grid=(2,),
        in_specs=[spec(rows), spec(rows)] + [pl.BlockSpec(memory_space=ANY)] * len(after),
        out_specs=(spec(block), spec(block), spec(2 * block)),
        compiler_params=pltpu.CompilerParams(vmem_limit_bytes=VMEM_LIMIT),
        cost_estimate=LIGHT,
        name="merge",
    )(keep, took, *after)


def pass_kernel(block, below_ref, above_ref, rest_ref, up_ref, down_ref):
    half = block // 2
    add = lambda a, b: (a.astype(F32) + b.astype(F32)).astype(BF)
    up_ref[...] = add(rest_ref[block : block + half, :], below_ref[:half, :])
    down_ref[...] = add(rest_ref[block + half :, :], above_ref[half:, :])


def pass_on(below, above, rest):
    block, model = below.shape
    return pl.pallas_call(
        functools.partial(pass_kernel, block),
        out_shape=(jax.ShapeDtypeStruct((block // 2, model), BF),) * 2,
        in_specs=[pl.BlockSpec(memory_space=VM)] * 3,
        out_specs=(pl.BlockSpec(memory_space=VM),) * 2,
        cost_estimate=LIGHT,
        name="pass",
    )(below, above, rest)


def ring_sum(merged, up, down):
    go_up, go_down, rest = merged
    below, above = lax.ppermute(go_up, "tp", up), lax.ppermute(go_down, "tp", down)
    up2, down2 = pass_on(below, above, rest)
    return up2, (rest, below, above, lax.ppermute(up2, "tp", up), lax.ppermute(down2, "tp", down))


def score_kernel(first, order_ref, ends_ref, adv_ref, x, vec_ref, *refs):
    rest_ref, below_ref, above_ref, below2_ref, above2_ref, out_ref = refs
    rows, model = x.shape
    half = rows // 2
    own = order_ref[0] * rows
    one = jnp.zeros((rows, 128), F32)
    two = jnp.zeros((rows, 128), F32)
    for lane in range(0, model, 128):
        cols = slice(lane, lane + 128)
        get = lambda ref, lo, hi: ref[lo:hi, cols].astype(F32)
        near = jnp.concatenate(
            [
                get(below2_ref, 0, half) + get(above_ref, 0, half),
                get(below_ref, half, rows) + get(above2_ref, 0, half),
            ],
            axis=0,
        )
        total = get(x, 0, rows) + get(rest_ref, 0, rows) + near
        one = one + total * vec_ref[:, cols]
        two = two + total * total
    mean = jnp.sum(two, axis=-1, keepdims=True) * F32(1.0 / model)
    score = jnp.sum(one, axis=-1, keepdims=True) * lax.rsqrt(mean + EPS)
    row = lax.broadcasted_iota(jnp.int32, (rows, 1), 0) + own + first
    adv = jnp.full((rows, 1), adv_ref[0], F32)
    for k in range(1, ends_ref.shape[0]):
        adv = jnp.where(row >= ends_ref[k - 1], adv_ref[k], adv)
    weight = jnp.broadcast_to(adv - score, (rows, 128))
    out_ref[...] = jnp.transpose(weight)[:8, :].astype(BF).astype(F32)


def token_weights(own, ends, adv, x, vec, rest, below, above, below2, above2, first):
    rows, model = below.shape
    return pl.pallas_call(
        functools.partial(score_kernel, first),
        out_shape=jax.ShapeDtypeStruct((8, rows), F32),
        in_specs=[pl.BlockSpec(memory_space=pltpu.SMEM)] * 3
        + [pl.BlockSpec(memory_space=VM)] * 7,
        out_specs=pl.BlockSpec(memory_space=VM),
        compiler_params=pltpu.CompilerParams(vmem_limit_bytes=VMEM_LIMIT),
        cost_estimate=LIGHT,
        name="score",
    )(own, ends, adv, x, vec, rest, below, above, below2, above2)


def own_weights(run_ref, all_ref, cols_of, out_ref):
    tps, runs_dev, spans = cols_of
    devices = all_ref.shape[0]
    runs = run_ref.shape[1]
    rows = out_ref.shape[0]
    run = run_ref[...]
    rep, at = lax.div(run, tps * runs_dev), lax.rem(run, tps * runs_dev) * RUN
    device, lane = jnp.zeros_like(run), jnp.zeros_like(run)
    for start, size in spans:
        share = size // tps
        here = (at >= start) & (at < start + size)
        device = jnp.where(here, rep * tps + lax.div(at - start, share), device)
        lane = jnp.where(here, start // tps + lax.rem(at - start, share), lane)
    down = lambda n, m: lax.broadcasted_iota(jnp.int32, (n, m), 0)
    across = lambda n, m: lax.broadcasted_iota(jnp.int32, (n, m), 1)
    one = lambda m: m.astype(jnp.int32).astype(F32).astype(BF)
    found = lax.dot_general(
        all_ref[...], one(down(devices, runs) == device), (((0,), (0,)), ((), ())), preferred_element_type=F32
    )
    lanes = down(found.shape[0], runs)
    found = jnp.where((lanes >= lane) & (lanes < lane + RUN), found, F32(0.0)).astype(BF)
    fold = one(down(RUN, found.shape[0]) == lax.rem(across(RUN, found.shape[0]), RUN))
    eight = jnp.dot(fold, found, preferred_element_type=F32).astype(BF)
    whose = one(lax.div(down(rows, runs), RUN) == across(rows, runs))
    wide = lax.dot_general(whose, eight, (((1,), (1,)), ((), ())), preferred_element_type=F32)
    wide = jnp.where(lax.rem(down(rows, RUN), RUN) == across(rows, RUN), wide, F32(0.0))
    out_ref[...] = jnp.sum(wide, axis=1, keepdims=True)


def weight_kernel(
    model, cols_of, run_ref, all_ref, inv_ref, y_ref, cot_ref, x_ref, gain_ref, dy_ref, mean_ref, gw_ref, acc, w
):
    i = pl.program_id(0)

    @pl.when(i == 0)
    def _():
        own_weights(run_ref, all_ref, cols_of, w)

    y = y_ref[...].astype(F32)
    here = pl.ds(pl.multiple_of(i * BLOCK, BLOCK), BLOCK)
    dy = (w[here, :] * cot_ref[...].astype(F32) + 0.5 * y).astype(BF)
    dy_ref[...] = dy
    mean_ref[...] = jnp.sum(dy.astype(F32) * y, axis=-1, keepdims=True) * F32(1.0 / model)
    pn = (x_ref[...].astype(F32) * inv_ref[...] * gain_ref[...]).astype(BF)
    part = lax.dot_general(pn, dy, (((0,), (0,)), ((), ())), preferred_element_type=F32)

    @pl.when(i == 0)
    def _():
        acc[...] = part

    @pl.when(i > 0)
    def _():
        acc[...] += part

    @pl.when(i == pl.num_programs(0) - 1)
    def _():
        gw_ref[...] = acc[...].astype(BF)


def input_kernel(spot_ref, inv_ref, mean_ref, dy_ref, x_ref, gain_ref, pw_ref, give_ref, *keep_refs):
    x, c = spot_ref[0], spot_ref[1]
    n = len(keep_refs)
    block = keep_refs[0].shape[0]
    for other in (1, 0):
        for s in range(n):
            owner = lax.rem(x + s, n) * 2 + (c if other == 0 else 1 - c)
            here = pl.ds(pl.multiple_of(owner * block, block), block)
            inv = inv_ref[here, :]
            xhat = x_ref[here, :].astype(F32) * inv
            dpn = lax.dot_general(
                dy_ref[here, :], pw_ref[...], (((1,), (1,)), ((), ())), preferred_element_type=F32
            )
            dx = (inv * (dpn * gain_ref[...] - xhat * mean_ref[here, :])).astype(BF)
            if other:
                give_ref[s] = dx
            else:
                keep_refs[s][...] = dx


def policy(spot, tps, model, cols_of, run, w_all, inv, y, cot, x, gain, pw):
    rows, width = x.shape
    outs = y.shape[1]
    row = lambda n: pl.BlockSpec((BLOCK, n), lambda i: (i, 0))
    whole = lambda *s: pl.BlockSpec(s, lambda i: (0,) * len(s))
    params = pltpu.CompilerParams(vmem_limit_bytes=VMEM_LIMIT)
    dy, mean, gw = pl.pallas_call(
        functools.partial(weight_kernel, model, cols_of),
        out_shape=(
            jax.ShapeDtypeStruct((rows, outs), BF),
            jax.ShapeDtypeStruct((rows, 1), F32),
            jax.ShapeDtypeStruct((width, outs), BF),
        ),
        grid=(rows // BLOCK,),
        in_specs=[whole(*run.shape), whole(*w_all.shape), row(1), row(outs), row(outs), row(width), whole(1, width)],
        out_specs=(row(outs), row(1), whole(width, outs)),
        scratch_shapes=[VM((width, outs), F32), VM((rows, 1), F32)],
        compiler_params=params,
        cost_estimate=LIGHT,
        name="weight",
    )(run, w_all, inv, y, cot, x, gain)
    n = tps // 2
    block = jax.ShapeDtypeStruct((rows // tps, width), BF)
    give, *keep = pl.pallas_call(
        input_kernel,
        out_shape=(jax.ShapeDtypeStruct((n, rows // tps, width), BF),) + (block,) * n,
        in_specs=[pl.BlockSpec(memory_space=pltpu.SMEM)] + [pl.BlockSpec(memory_space=VM)] * 6,
        out_specs=(pl.BlockSpec(memory_space=VM),) * (n + 1),
        compiler_params=params,
        cost_estimate=LIGHT,
        name="input",
    )(spot, inv, mean, dy, x, gain, pw)
    return give, keep, gw


def place_kernel(pieces, *refs):
    order_ref, ins, out = refs[0], refs[1 : 1 + pieces], refs[1 + pieces]
    for j in range(pieces):
        width = ins[j].shape[1]
        out[:, pl.ds(pl.multiple_of(order_ref[j] * width, width), width)] = ins[j][...]


def place_columns(order, pieces):
    n, (rows, width) = len(pieces), pieces[0].shape
    return pl.pallas_call(
        functools.partial(place_kernel, n),
        out_shape=jax.ShapeDtypeStruct((rows, n * width), pieces[0].dtype),
        in_specs=[pl.BlockSpec(memory_space=pltpu.SMEM)] + [pl.BlockSpec(memory_space=VM)] * n,
        out_specs=pl.BlockSpec(memory_space=VM),
        cost_estimate=LIGHT,
        name="place",
    )(order, *pieces)


def tp_moves(tps):
    n = tps // 2
    at = lambda x, c: (x % n) * 2 + c
    every = [(x, c) for x in range(n) for c in range(2)]
    return (
        [(at(x, c), at(x, 1 - c)) for x, c in every],
        [(at(x, c), at(x + 1, c)) for x, c in every],
        [(at(x, c), at(x - 1, c)) for x, c in every],
        [(at(x, c), at(x + 2, c)) for x, c in every],
    )


def spread(a, axis):
    n = lax.axis_size(axis)
    return lax.all_to_all(jnp.broadcast_to(a[None], (n,) + a.shape), axis, split_axis=0, concat_axis=0, tiled=True)


def flag(m):
    return m.astype(jnp.int32).astype(F32)


def small_dot(a, b, dims=(((1,), (0,)), ((), ()))):
    return lax.dot_general(a.astype(BF), b.astype(BF), dims, preferred_element_type=F32)


def grid_of(shape):
    return tuple(lax.broadcasted_iota(jnp.int32, shape, d) for d in range(2))


def send_kernel(base_ref, dest_ref, out_ref):
    tps, runs = dest_ref.shape
    reps = out_ref.shape[0]
    devices = reps * tps
    row, col = grid_of((devices, devices))
    same = row // tps == col // tps
    run, at = grid_of((tps, devices))
    sends = jnp.zeros((tps, devices), F32)
    which = jnp.zeros((tps, devices), F32)
    for k in range(runs):
        hit = flag(dest_ref[:, k : k + 1] == at)
        sends = sends + hit
        which = which + hit * k
    which = which + (run * runs).astype(F32)
    r8, c8 = grid_of((tps, tps))
    slot = small_dot(flag(c8 < r8), small_dot(sends, flag(same))) + small_dot(sends, flag(same & (row < col)))
    want = (grid_of((128, devices))[0] + base_ref[0]).astype(F32)
    found = jnp.zeros((128, devices), F32)
    for i in range(tps):
        hit = (slot[i : i + 1] == want) & (sends[i : i + 1] > 0.5)
        found = found + jnp.where(hit, which[i : i + 1], F32(0.0))
    rep, dev = grid_of((reps, devices))
    chosen = small_dot(flag(dev // tps == rep), found, (((1,), (1,)), ((), ())))
    out_ref[...] = chosen.astype(jnp.int32)


def send_lists(dest, reps, turn):
    out = pl.pallas_call(
        send_kernel,
        out_shape=jax.ShapeDtypeStruct((reps, 128), jnp.int32),
        in_specs=[pl.BlockSpec(memory_space=pltpu.SMEM), pl.BlockSpec(memory_space=VM)],
        out_specs=pl.BlockSpec(memory_space=VM),
        cost_estimate=LIGHT,
        name="send_lists",
    )((turn * CAP).astype(jnp.int32).reshape(1), dest)
    return out[:, :CAP].reshape(-1)


def get_kernel(tps, runs, rep_ref, dest_ref, *refs):
    out_ref = refs[-1]
    reps = dest_ref.shape[0]
    devices = reps * tps
    row, col = grid_of((devices, devices))
    same = row // tps == col // tps
    group, below = flag(same), flag(same & (row < col))
    at = grid_of((reps, devices))[1]
    zero = jnp.zeros((reps, devices), F32)
    sends, which = [], []
    for i in range(tps):
        a, w = zero, zero
        for k in range(runs):
            lane = i * runs + k
            hit = flag(dest_ref[:, lane : lane + 1].astype(jnp.int32) == at)
            a = a + hit
            w = w + hit * k
        sends.append(a)
        which.append(w)
    whole = functools.reduce(lambda a, b: a + b, sends)
    r16, c16 = grid_of((reps, reps))
    earlier = small_dot(flag(c16 < r16), whole)
    most = jnp.max(small_dot(whole, group))
    to_me = flag(row == rep_ref[0] * tps + col)
    rank, seen = earlier, zero
    tables = [[None] * tps for _ in range(2)]
    j = grid_of((reps, devices))[1].astype(F32)
    rep_at = grid_of((reps, devices))[0].astype(F32)
    slots, runs_of = [jnp.zeros((1, devices), F32)] * tps, [jnp.zeros((1, devices), F32)] * tps
    sources = [jnp.zeros((1, devices), F32)] * tps
    for i in range(tps):
        slot = seen + small_dot(sends[i], below)
        mine = [small_dot(v, to_me) for v in (sends[i], rank, slot, which[i])]
        for p in range(tps):
            a, r, s, w = (v[:, p : p + 1] for v in mine)
            hit = (r == j) & (a > 0.5)
            get = lambda v: jnp.sum(jnp.where(hit, v, F32(0.0)), axis=0, keepdims=True)
            slots[p] = slots[p] + get(s)
            sources[p] = sources[p] + get(rep_at)
            runs_of[p] = runs_of[p] + get((rep_at * tps + i) * runs + w)
        rank = rank + sends[i]
        seen = seen + small_dot(sends[i], group)
    for p in range(tps):
        slot = slots[p].astype(jnp.int32)
        turn = lax.div(slot, jnp.int32(CAP))
        out_ref[0, p : p + 1, :] = sources[p].astype(jnp.int32) * CAP + slot - turn * CAP
        out_ref[1, p : p + 1, :] = turn
        out_ref[2, p : p + 1, :] = runs_of[p].astype(jnp.int32)
    out_ref[3] = jnp.broadcast_to(most, (tps, devices)).astype(jnp.int32)


def get_lists(dest, rep, tps, runs, after):
    devices = dest.shape[0] * tps
    out = pl.pallas_call(
        functools.partial(get_kernel, tps, runs),
        out_shape=jax.ShapeDtypeStruct((4, tps, devices), jnp.int32),
        in_specs=[pl.BlockSpec(memory_space=pltpu.SMEM), pl.BlockSpec(memory_space=VM)]
        + [pl.BlockSpec(memory_space=ANY)] * len(after),
        out_specs=pl.BlockSpec(memory_space=VM),
        cost_estimate=LIGHT,
        name="get_lists",
    )(rep.astype(jnp.int32).reshape(1), dest, *after)
    tables = out[:, :, :runs].reshape(4, tps * runs)
    return tables[0], tables[1], tables[2], tables[3, 0]


def sum_kernel(parts_ref, *refs):
    total = parts_ref[0].astype(F32)
    for k in range(1, parts_ref.shape[0]):
        total = total + parts_ref[k].astype(F32)
    refs[-1][...] = total


def sum_parts(parts, after):
    return pl.pallas_call(
        sum_kernel,
        out_shape=jax.ShapeDtypeStruct(parts.shape[1:], F32),
        in_specs=[pl.BlockSpec(memory_space=VM)] + [pl.BlockSpec(memory_space=ANY)] * len(after),
        out_specs=pl.BlockSpec(memory_space=VM),
        cost_estimate=LIGHT,
        name="sum",
    )(parts, *after)


def zero_of(a):
    return (a[(0,) * a.ndim].astype(F32) * 0.0).astype(jnp.int32)


def relay(a, chosen, place):
    got = lax.all_to_all(a[chosen], "rep", split_axis=0, concat_axis=0, tiled=True)
    return got[place]


def per_device(
    hidden,
    ref_gain,
    ref_wq,
    ref_wkv,
    ref_wo,
    score_vec,
    lengths,
    advantage,
    dest,
    policy_norm_gain,
    pol_w,
    cotangent,
):
    tps, reps = lax.axis_size("tp"), lax.axis_size("rep")
    tp, rep = lax.axis_index("tp"), lax.axis_index("rep")
    rows, width = hidden.shape
    model = width * tps
    outs = pol_w.shape[1]
    runs_dev = dest.shape[0] // RUN
    swap, up, down, across = tp_moves(tps)
    starts = [sum(PARTS[:k]) for k in range(len(PARTS))]
    spot = jnp.stack([tp // 2, lax.rem(tp, 2)]).astype(jnp.int32)
    full = lax.all_gather(hidden, "tp", axis=1, tiled=True)

    own = hidden.astype(F32)
    squares = jnp.sum(own * own, axis=1)
    run_own = jnp.pad(dest.reshape(runs_dev, RUN)[:, 0].astype(F32), (0, 128 - runs_dev))
    both = spread(jnp.concatenate([squares, run_own]), "tp")
    inv = lax.rsqrt(jnp.sum(both[:, :rows], axis=0) / model + EPS)
    run_rep = both[:, rows : rows + runs_dev].astype(jnp.int32)
    chosen = send_lists(run_rep, reps, jnp.int32(0))

    cols = outs // tps
    w_rows = pol_w.shape[0]
    turned = lax.ppermute(
        pol_w, ("rep", "tp"), [(t * reps + k, k * tps + t) for t in range(tps) for k in range(reps)]
    )
    line = jnp.pad(run_rep.reshape(1, -1).astype(BF), ((0, 7), (0, outs - tps * runs_dev)))
    spread_w = spread(jnp.concatenate([turned, line], axis=0), "rep")
    w_slice = spread_w[:, :w_rows].reshape(width, outs)
    run_all = spread_w[:, w_rows, : tps * runs_dev]

    gain = lax.dynamic_slice_in_dim(policy_norm_gain, tp * width, width, 0)[None]
    w_in = jnp.concatenate([ref_wq, ref_wkv.reshape(model, -1)], axis=1)
    y_keep, y_give = project(spot, hidden, gain, w_slice, tps, ())
    y_sums = pair_sums(y_keep, lax.ppermute(y_give, "tp", swap), (w_in,))
    y_parts = [y_sums[0]] + [lax.ppermute(y_sums[s], "tp", m) for s, m in ((1, up), (2, across), (3, down))]

    x_runs = hidden.reshape(rows // RUN, RUN, width)
    x_sent = x_runs[chosen]
    x_got = lax.all_to_all(x_sent, "rep", split_axis=0, concat_axis=0, tiled=True)

    inv_col = inv[:, None]

    xn = (full.astype(F32) * inv_col * ref_gain).astype(BF)
    qkv = jnp.dot(xn, w_in, preferred_element_type=F32).astype(BF)
    ends = jnp.cumsum(lengths[0])
    attn = attention(ends, qkv, ref_wq.shape[1], (x_sent, *y_parts))
    mine = tp.astype(jnp.int32).reshape(1)
    parts = len(PARTS)
    cot_all = lax.all_gather(cotangent, "tp", axis=0, tiled=True)
    held = [outproj(spot, attn, ref_wo, tps, k, parts, (cot_all,) if k else ()) for k in range(parts)]
    merged = [
        merge(keep, lax.ppermute(give, "tp", swap), keep.shape[0] // 4, tuple(h[0] for h in held)) for keep, give in held
    ]
    place, turn_of, got_run, most = get_lists(run_all, rep, tps, runs_dev, (merged[-1][0],))
    sums = [ring_sum(m, up, down) for m in merged]
    stages = [stage for _, stage in sums]
    y_runs = pack(y_parts, [inv_col], (x_got, stages[0][1], place)).reshape(rows // RUN, RUN, 128)
    weights = [
        token_weights(
            mine,
            ends,
            advantage[0],
            lax.dynamic_slice_in_dim(full, start + tp * (size // tps), size // tps, 0),
            score_vec[None],
            *stage,
            start,
        )[:1]
        for stage, start, size in zip(stages, starts, PARTS, strict=True)
    ]

    y_got = lax.all_to_all(
        y_runs[chosen], "rep", split_axis=0, concat_axis=0, tiled=True
    )

    def later_turns(a, held, begin):
        def again(state):
            turn, now = state
            came = relay(a, send_lists(run_rep, reps, turn), place)
            return turn + 1, jnp.where((turn_of == turn)[:, None, None], came, now)

        return lax.while_loop(lambda state: state[0] * CAP < most, again, (begin, held))[1]

    y_pol = later_turns(y_runs, y_got[place + zero_of(sums[-1][0])], jnp.int32(1)).reshape(rows, 128)
    x_pol = later_turns(x_runs, x_got[place], jnp.int32(1)).reshape(rows, width)
    inv_pol = y_pol[:, cols : cols + 1].astype(F32) + y_pol[:, cols + 1 : cols + 2].astype(F32)
    y_all = lax.all_gather(y_pol[:, :cols], "tp", axis=1, tiled=True)

    w_mine = jnp.concatenate(weights, axis=1).astype(BF)
    w_all = spread(w_mine.reshape(-1), ("rep", "tp"))
    cols_of = (tps, runs_dev, tuple(zip(starts, PARTS, strict=True)))

    dx_give, dx_keep, gw = policy(spot, tps, model, cols_of, got_run[None], w_all, inv_pol, y_all, cot_all, x_pol, gain, w_slice)

    parts = lax.all_to_all(gw.reshape(reps, w_rows, outs), "rep", split_axis=0, concat_axis=0, tiled=True)

    x, c = spot[0], spot[1]
    n = tps // 2
    dx_took = lax.ppermute(dx_give, "tp", swap)
    pieces, places = [], []
    for s, move in ((1, up), (3, down), (2, across), (0, None)):
        pair = [dx_keep[s], dx_took[s]]
        if move is not None:
            pair = [lax.ppermute(v, "tp", move) for v in pair]
        origin = lax.rem(x - s + n, n) * 2
        pieces += pair
        places += [origin + c, origin + 1 - c]
    places = jnp.stack(places).astype(jnp.int32)
    policy_input_gradient = place_columns(places, pieces)

    back = [(k * tps + t, t * reps + k) for t in range(tps) for k in range(reps)]
    total = sum_parts(parts, (pieces[5],))
    grad_weight = lax.ppermute(total, ("rep", "tp"), back)
    gain_own = lax.dynamic_slice_in_dim(policy_norm_gain, (rep * tps + tp) * w_rows, w_rows, 0)
    policy_gain_gradient = jnp.sum(grad_weight * pol_w.astype(F32), axis=1) / gain_own
    return (policy_input_gradient, grad_weight, policy_gain_gradient)


def solution(mesh):
    return jax.shard_map(
        per_device,
        mesh=mesh,
        in_specs=(
            P("rep", "tp"),
            P(),
            P(None, "tp"),
            P(None, None, "tp"),
            P("tp", None),
            P(),
            P("rep", None),
            P("rep", None),
            P(("rep", "tp")),
            P(),
            P(("rep", "tp"), None),
            P(("rep", "tp"), None),
        ),
        out_specs=(P(("rep", "tp"), None), P(("rep", "tp"), None), P(("rep", "tp"))),
        check_vma=False,
    )
```

```python
import functools

import jax
import jax.numpy as jnp
from jax import lax
from jax.experimental import pallas as pl
from jax.experimental.pallas import tpu as pltpu
from jax.sharding import PartitionSpec as P

HD = 128
RUN = 8
CAP = 22
BLOCK = 256
PARTS = (512, 512)
DEPTH = 3
TILE = 64
EPS = 1e-6
BF = jnp.bfloat16
F32 = jnp.float32
VMEM_LIMIT = 24 * 1024 * 1024
ANY = pl.ANY
LIGHT = pl.CostEstimate(flops=1, bytes_accessed=1, transcendentals=0)
VM = pltpu.VMEM


def pull(copies):
    for c in copies:
        c.start()


def project_kernel(cols, spot_ref, x_ref, gain_ref, w_ref, *refs):
    keep_ref, give_ref, both = refs[-3:]
    half = x_ref.shape[0] // 2
    n = keep_ref.shape[0]
    for i in range(2):
        xg = (x_ref[i * half : (i + 1) * half, :].astype(F32) * gain_ref[...]).astype(BF)
        part = jnp.dot(xg, w_ref[...], preferred_element_type=F32).astype(BF)
        for t in range(2 * n):
            both[t, :, i * cols : (i + 1) * cols] = part[:, t * cols : (t + 1) * cols]
    x, c = spot_ref[0], spot_ref[1]
    for s in range(n):
        owner = lax.rem(x + s, n) * 2
        keep_ref[s] = both[owner + c]
        give_ref[s] = both[owner + 1 - c]


def project(spot, x, gain, w, tps, after):
    rows, cols = x.shape[0], w.shape[1] // tps
    shape = (tps // 2, rows // 2, 2 * cols)
    return pl.pallas_call(
        functools.partial(project_kernel, cols),
        out_shape=(jax.ShapeDtypeStruct(shape, BF),) * 2,
        in_specs=[pl.BlockSpec(memory_space=pltpu.SMEM)]
        + [pl.BlockSpec(memory_space=VM)] * 3
        + [pl.BlockSpec(memory_space=ANY)] * len(after),
        out_specs=(pl.BlockSpec(memory_space=VM),) * 2,
        scratch_shapes=[VM((tps,) + shape[1:], BF)],
        compiler_params=pltpu.CompilerParams(vmem_limit_bytes=VMEM_LIMIT),
        cost_estimate=LIGHT,
        name="project",
    )(spot, x, gain, w, *after)


def pair_kernel(keep_ref, took_ref, *refs):
    out_refs = refs[-keep_ref.shape[0] :]
    for s, out_ref in enumerate(out_refs):
        out_ref[...] = (keep_ref[s].astype(F32) + took_ref[s].astype(F32)).astype(BF)


def pair_sums(keep, took, after):
    n = keep.shape[0]
    return pl.pallas_call(
        pair_kernel,
        out_shape=(jax.ShapeDtypeStruct(keep.shape[1:], BF),) * n,
        in_specs=[pl.BlockSpec(memory_space=VM)] * 2 + [pl.BlockSpec(memory_space=ANY)] * len(after),
        out_specs=(pl.BlockSpec(memory_space=VM),) * n,
        cost_estimate=LIGHT,
        name="pair",
    )(keep, took, *after)


def pack_kernel(pieces, scales, *refs):
    inv_refs, out_ref = refs[pieces : pieces + scales], refs[-1]
    scales = jnp.concatenate([r[...] for r in inv_refs], axis=0)
    total = refs[0][...].astype(F32)
    for j in range(1, pieces):
        total = total + refs[j][...].astype(F32)
    half, cols = total.shape[0], total.shape[1] // 2
    lane = lax.broadcasted_iota(jnp.int32, (half, out_ref.shape[1] - cols), 1)
    for i in range(2):
        here = slice(i * half, (i + 1) * half)
        inv = scales[here, :]
        hi = inv.astype(BF).astype(F32)
        stats = jnp.where(lane == 0, hi, jnp.where(lane == 1, inv - hi, F32(0.0)))
        y = total[:, i * cols : (i + 1) * cols] * inv
        out_ref[here, :] = jnp.concatenate([y, stats], axis=1).astype(BF)


def pack(pieces, invs, after):
    rows = 2 * pieces[0].shape[0]
    return pl.pallas_call(
        functools.partial(pack_kernel, len(pieces), len(invs)),
        out_shape=jax.ShapeDtypeStruct((rows, 128), BF),
        in_specs=[pl.BlockSpec(memory_space=VM)] * (len(pieces) + len(invs))
        + [pl.BlockSpec(memory_space=ANY)] * len(after),
        out_specs=pl.BlockSpec(memory_space=VM),
        cost_estimate=LIGHT,
        name="pack",
    )(*pieces, *invs, *after)


def attention_kernel(ends_ref, qkv_ref, *refs):
    out_ref = refs[-1]
    rows, wide = out_ref.shape
    q_ref = kv_ref = qkv_ref
    for block in range(rows // BLOCK):
        base = block * BLOCK
        low = max(0, base - 2 * BLOCK)
        high = base + BLOCK
        width = high - low
        row = lax.broadcasted_iota(jnp.int32, (BLOCK, 1), 0) + base
        start = jnp.zeros((BLOCK, 1), jnp.int32)
        for k in range(ends_ref.shape[0]):
            end = ends_ref[k]
            start = jnp.where(row >= end, end, start)
        col = lax.broadcasted_iota(jnp.int32, (BLOCK, width), 1) + low
        allowed = (col >= start) & (col <= row)
        keys = kv_ref[low:high, wide : wide + HD]
        values = kv_ref[low:high, wide + HD :]
        here = slice(block * BLOCK, (block + 1) * BLOCK)
        for head in range(wide // HD):
            lanes = slice(head * HD, (head + 1) * HD)
            s = lax.dot_general(q_ref[here, lanes], keys, (((1,), (1,)), ((), ())), preferred_element_type=F32)
            s = jnp.where(allowed, s * F32(HD**-0.5), F32(-1e30))
            e = jnp.exp(s - jnp.max(s, axis=-1, keepdims=True))
            p = (e / jnp.sum(e, axis=-1, keepdims=True)).astype(BF)
            o = lax.dot_general(p, values, (((1,), (0,)), ((), ())), preferred_element_type=F32)
            out_ref[here, lanes] = o.astype(BF)


def attention(ends, qkv, width, after):
    rows = qkv.shape[0]
    return pl.pallas_call(
        attention_kernel,
        out_shape=jax.ShapeDtypeStruct((rows, width), BF),
        in_specs=[pl.BlockSpec(memory_space=pltpu.SMEM), pl.BlockSpec(memory_space=VM)]
        + [pl.BlockSpec(memory_space=pltpu.HBM)] * len(after),
        out_specs=pl.BlockSpec(memory_space=VM),
        compiler_params=pltpu.CompilerParams(vmem_limit_bytes=VMEM_LIMIT),
        cost_estimate=LIGHT,
        name="attention",
    )(ends, qkv, *after)


def outproj_kernel(block, at_ref, attn_ref, wo_ref, *refs):
    keep_ref, give_ref, a = refs[-3:]
    x, c, n = at_ref[0], at_ref[1], a.shape[0] // (2 * block)

    @pl.when(pl.program_id(0) == 0)
    def _():
        for other in range(2):
            core = c if other == 0 else 1 - c
            for s in range(n):
                owner = lax.rem(x + s, n) * 2 + core
                here = pl.ds(pl.multiple_of(owner * block, block), block)
                a[(other * n + s) * block : (other * n + s + 1) * block, :] = attn_ref[here, :]

    out = jnp.dot(a[...], wo_ref[...], preferred_element_type=F32).astype(BF)
    keep_ref[...] = out[: n * block]
    give_ref[...] = out[n * block :]


def outproj(place, attn, wo, tps, part, parts, after):
    rows, depth = attn.shape[0] // parts, attn.shape[1]
    model = wo.shape[1]
    step = model // 5
    half = pl.BlockSpec((rows // 2, step), lambda i: (0, i))
    return pl.pallas_call(
        functools.partial(outproj_kernel, rows // tps),
        out_shape=(jax.ShapeDtypeStruct((rows // 2, model), BF),) * 2,
        grid=(5,),
        in_specs=[
            pl.BlockSpec(memory_space=pltpu.SMEM),
            pl.BlockSpec((rows, depth), lambda i: (part, 0)),
            pl.BlockSpec((depth, step), lambda i: (0, i)),
        ]
        + [pl.BlockSpec(memory_space=pltpu.HBM)] * len(after),
        out_specs=(half, half),
        scratch_shapes=[VM((rows, depth), BF)],
        compiler_params=pltpu.CompilerParams(vmem_limit_bytes=56 * 1024 * 1024),
        cost_estimate=LIGHT,
        name="outproj",
    )(place, attn, wo, *after)


def merge_kernel(block, keep_ref, took_ref, *refs):
    up_ref, down_ref, rest_ref = refs[-3:]
    half = block // 2
    add = lambda lo, hi: (keep_ref[lo:hi, :].astype(F32) + took_ref[lo:hi, :].astype(F32)).astype(BF)
    far, near_down = 2 * block, 3 * block
    up_ref[:half, :] = add(far, far + half)
    up_ref[half:, :] = add(block + half, 2 * block)
    down_ref[:half, :] = add(near_down, near_down + half)
    down_ref[half:, :] = add(far + half, far + block)
    rest_ref[:block, :] = add(0, block)
    rest_ref[block : block + half, :] = add(block, block + half)
    rest_ref[block + half :, :] = add(near_down + half, near_down + block)


def merge(keep, took, block, after):
    rows, model = keep.shape
    step = model // 2
    spec = lambda n: pl.BlockSpec((n, step), lambda i: (0, i))
    shape = lambda n: jax.ShapeDtypeStruct((n, model), BF)
    return pl.pallas_call(
        functools.partial(merge_kernel, block),
        out_shape=(shape(block), shape(block), shape(2 * block)),
        grid=(2,),
        in_specs=[spec(rows), spec(rows)] + [pl.BlockSpec(memory_space=ANY)] * len(after),
        out_specs=(spec(block), spec(block), spec(2 * block)),
        compiler_params=pltpu.CompilerParams(vmem_limit_bytes=VMEM_LIMIT),
        cost_estimate=LIGHT,
        name="merge",
    )(keep, took, *after)


def pass_kernel(block, below_ref, above_ref, rest_ref, up_ref, down_ref):
    half = block // 2
    add = lambda a, b: (a.astype(F32) + b.astype(F32)).astype(BF)
    up_ref[...] = add(rest_ref[block : block + half, :], below_ref[:half, :])
    down_ref[...] = add(rest_ref[block + half :, :], above_ref[half:, :])


def pass_on(below, above, rest):
    block, model = below.shape
    return pl.pallas_call(
        functools.partial(pass_kernel, block),
        out_shape=(jax.ShapeDtypeStruct((block // 2, model), BF),) * 2,
        in_specs=[pl.BlockSpec(memory_space=VM)] * 3,
        out_specs=(pl.BlockSpec(memory_space=VM),) * 2,
        cost_estimate=LIGHT,
        name="pass",
    )(below, above, rest)


def ring_sum(merged, up, down):
    go_up, go_down, rest = merged
    below, above = lax.ppermute(go_up, "tp", up), lax.ppermute(go_down, "tp", down)
    up2, down2 = pass_on(below, above, rest)
    return up2, (rest, below, above, lax.ppermute(up2, "tp", up), lax.ppermute(down2, "tp", down))


def score_kernel(first, order_ref, ends_ref, adv_ref, x, vec_ref, *refs):
    rest_ref, below_ref, above_ref, below2_ref, above2_ref, out_ref = refs
    rows, model = x.shape
    half = rows // 2
    own = order_ref[0] * rows
    one = jnp.zeros((rows, 128), F32)
    two = jnp.zeros((rows, 128), F32)
    for lane in range(0, model, 128):
        cols = slice(lane, lane + 128)
        get = lambda ref, lo, hi: ref[lo:hi, cols].astype(F32)
        near = jnp.concatenate(
            [
                get(below2_ref, 0, half) + get(above_ref, 0, half),
                get(below_ref, half, rows) + get(above2_ref, 0, half),
            ],
            axis=0,
        )
        total = get(x, 0, rows) + get(rest_ref, 0, rows) + near
        one = one + total * vec_ref[:, cols]
        two = two + total * total
    mean = jnp.sum(two, axis=-1, keepdims=True) * F32(1.0 / model)
    score = jnp.sum(one, axis=-1, keepdims=True) * lax.rsqrt(mean + EPS)
    row = lax.broadcasted_iota(jnp.int32, (rows, 1), 0) + own + first
    adv = jnp.full((rows, 1), adv_ref[0], F32)
    for k in range(1, ends_ref.shape[0]):
        adv = jnp.where(row >= ends_ref[k - 1], adv_ref[k], adv)
    weight = jnp.broadcast_to(adv - score, (rows, 128))
    out_ref[...] = jnp.transpose(weight)[:8, :].astype(BF).astype(F32)


def token_weights(own, ends, adv, x, vec, rest, below, above, below2, above2, first):
    rows, model = below.shape
    return pl.pallas_call(
        functools.partial(score_kernel, first),
        out_shape=jax.ShapeDtypeStruct((8, rows), F32),
        in_specs=[pl.BlockSpec(memory_space=pltpu.SMEM)] * 3
        + [pl.BlockSpec(memory_space=VM)] * 7,
        out_specs=pl.BlockSpec(memory_space=VM),
        compiler_params=pltpu.CompilerParams(vmem_limit_bytes=VMEM_LIMIT),
        cost_estimate=LIGHT,
        name="score",
    )(own, ends, adv, x, vec, rest, below, above, below2, above2)


def own_weights(run_ref, all_ref, cols_of, out_ref):
    tps, runs_dev, spans = cols_of
    devices = all_ref.shape[0]
    runs = run_ref.shape[1]
    rows = out_ref.shape[0]
    run = run_ref[...]
    rep, at = lax.div(run, tps * runs_dev), lax.rem(run, tps * runs_dev) * RUN
    device, lane = jnp.zeros_like(run), jnp.zeros_like(run)
    for start, size in spans:
        share = size // tps
        here = (at >= start) & (at < start + size)
        device = jnp.where(here, rep * tps + lax.div(at - start, share), device)
        lane = jnp.where(here, start // tps + lax.rem(at - start, share), lane)
    down = lambda n, m: lax.broadcasted_iota(jnp.int32, (n, m), 0)
    across = lambda n, m: lax.broadcasted_iota(jnp.int32, (n, m), 1)
    one = lambda m: m.astype(jnp.int32).astype(F32).astype(BF)
    found = lax.dot_general(
        all_ref[...], one(down(devices, runs) == device), (((0,), (0,)), ((), ())), preferred_element_type=F32
    )
    lanes = down(found.shape[0], runs)
    found = jnp.where((lanes >= lane) & (lanes < lane + RUN), found, F32(0.0)).astype(BF)
    fold = one(down(RUN, found.shape[0]) == lax.rem(across(RUN, found.shape[0]), RUN))
    eight = jnp.dot(fold, found, preferred_element_type=F32).astype(BF)
    whose = one(lax.div(down(rows, runs), RUN) == across(rows, runs))
    wide = lax.dot_general(whose, eight, (((1,), (1,)), ((), ())), preferred_element_type=F32)
    wide = jnp.where(lax.rem(down(rows, RUN), RUN) == across(rows, RUN), wide, F32(0.0))
    out_ref[...] = jnp.sum(wide, axis=1, keepdims=True)


def weight_kernel(
    model, cols_of, run_ref, all_ref, inv_ref, y_ref, cot_ref, x_ref, gain_ref, dy_ref, mean_ref, gw_ref, acc, w
):
    i = pl.program_id(0)

    @pl.when(i == 0)
    def _():
        own_weights(run_ref, all_ref, cols_of, w)

    y = y_ref[...].astype(F32)
    here = pl.ds(pl.multiple_of(i * BLOCK, BLOCK), BLOCK)
    dy = (w[here, :] * cot_ref[...].astype(F32) + 0.5 * y).astype(BF)
    dy_ref[...] = dy
    mean_ref[...] = jnp.sum(dy.astype(F32) * y, axis=-1, keepdims=True) * F32(1.0 / model)
    pn = (x_ref[...].astype(F32) * inv_ref[...] * gain_ref[...]).astype(BF)
    part = lax.dot_general(pn, dy, (((0,), (0,)), ((), ())), preferred_element_type=F32)

    @pl.when(i == 0)
    def _():
        acc[...] = part

    @pl.when(i > 0)
    def _():
        acc[...] += part

    @pl.when(i == pl.num_programs(0) - 1)
    def _():
        gw_ref[...] = acc[...].astype(BF)


def input_kernel(spot_ref, inv_ref, mean_ref, dy_ref, x_ref, gain_ref, pw_ref, give_ref, *keep_refs):
    x, c = spot_ref[0], spot_ref[1]
    n = len(keep_refs)
    block = keep_refs[0].shape[0]
    for other in (1, 0):
        for s in range(n):
            owner = lax.rem(x + s, n) * 2 + (c if other == 0 else 1 - c)
            here = pl.ds(pl.multiple_of(owner * block, block), block)
            inv = inv_ref[here, :]
            xhat = x_ref[here, :].astype(F32) * inv
            dpn = lax.dot_general(
                dy_ref[here, :], pw_ref[...], (((1,), (1,)), ((), ())), preferred_element_type=F32
            )
            dx = (inv * (dpn * gain_ref[...] - xhat * mean_ref[here, :])).astype(BF)
            if other:
                give_ref[s] = dx
            else:
                keep_refs[s][...] = dx


def policy(spot, tps, model, cols_of, run, w_all, inv, y, cot, x, gain, pw):
    rows, width = x.shape
    outs = y.shape[1]
    row = lambda n: pl.BlockSpec((BLOCK, n), lambda i: (i, 0))
    whole = lambda *s: pl.BlockSpec(s, lambda i: (0,) * len(s))
    params = pltpu.CompilerParams(vmem_limit_bytes=56 * 1024 * 1024)
    dy, mean, gw = pl.pallas_call(
        functools.partial(weight_kernel, model, cols_of),
        out_shape=(
            jax.ShapeDtypeStruct((rows, outs), BF),
            jax.ShapeDtypeStruct((rows, 1), F32),
            jax.ShapeDtypeStruct((width, outs), BF),
        ),
        grid=(rows // BLOCK,),
        in_specs=[whole(*run.shape), whole(*w_all.shape), row(1), row(outs), row(outs), row(width), whole(1, width)],
        out_specs=(row(outs), row(1), whole(width, outs)),
        scratch_shapes=[VM((width, outs), F32), VM((rows, 1), F32)],
        compiler_params=params,
        cost_estimate=LIGHT,
        name="weight",
    )(run, w_all, inv, y, cot, x, gain)
    n = tps // 2
    block = jax.ShapeDtypeStruct((rows // tps, width), BF)
    give, *keep = pl.pallas_call(
        input_kernel,
        out_shape=(jax.ShapeDtypeStruct((n, rows // tps, width), BF),) + (block,) * n,
        in_specs=[pl.BlockSpec(memory_space=pltpu.SMEM)] + [pl.BlockSpec(memory_space=VM)] * 6,
        out_specs=(pl.BlockSpec(memory_space=VM),) * (n + 1),
        compiler_params=params,
        cost_estimate=LIGHT,
        name="input",
    )(spot, inv, mean, dy, x, gain, pw)
    return give, keep, gw


def place_kernel(pieces, *refs):
    order_ref, ins, out = refs[0], refs[1 : 1 + pieces], refs[1 + pieces]
    for j in range(pieces):
        width = ins[j].shape[1]
        out[:, pl.ds(pl.multiple_of(order_ref[j] * width, width), width)] = ins[j][...]


def place_columns(order, pieces):
    n, (rows, width) = len(pieces), pieces[0].shape
    return pl.pallas_call(
        functools.partial(place_kernel, n),
        out_shape=jax.ShapeDtypeStruct((rows, n * width), pieces[0].dtype),
        in_specs=[pl.BlockSpec(memory_space=pltpu.SMEM)] + [pl.BlockSpec(memory_space=VM)] * n,
        out_specs=pl.BlockSpec(memory_space=VM),
        cost_estimate=LIGHT,
        name="place",
    )(order, *pieces)


def tp_moves(tps):
    n = tps // 2
    at = lambda x, c: (x % n) * 2 + c
    every = [(x, c) for x in range(n) for c in range(2)]
    return (
        [(at(x, c), at(x, 1 - c)) for x, c in every],
        [(at(x, c), at(x + 1, c)) for x, c in every],
        [(at(x, c), at(x - 1, c)) for x, c in every],
        [(at(x, c), at(x + 2, c)) for x, c in every],
    )


def spread(a, axis):
    n = lax.axis_size(axis)
    return lax.all_to_all(jnp.broadcast_to(a[None], (n,) + a.shape), axis, split_axis=0, concat_axis=0, tiled=True)


def flag(m):
    return m.astype(jnp.int32).astype(F32)


def small_dot(a, b, dims=(((1,), (0,)), ((), ()))):
    return lax.dot_general(a.astype(BF), b.astype(BF), dims, preferred_element_type=F32)


def grid_of(shape):
    return tuple(lax.broadcasted_iota(jnp.int32, shape, d) for d in range(2))


def send_kernel(base_ref, dest_ref, out_ref):
    tps, runs = dest_ref.shape
    reps = out_ref.shape[0]
    devices = reps * tps
    row, col = grid_of((devices, devices))
    same = row // tps == col // tps
    run, at = grid_of((tps, devices))
    sends = jnp.zeros((tps, devices), F32)
    which = jnp.zeros((tps, devices), F32)
    for k in range(runs):
        hit = flag(dest_ref[:, k : k + 1] == at)
        sends = sends + hit
        which = which + hit * k
    which = which + (run * runs).astype(F32)
    r8, c8 = grid_of((tps, tps))
    slot = small_dot(flag(c8 < r8), small_dot(sends, flag(same))) + small_dot(sends, flag(same & (row < col)))
    want = (grid_of((128, devices))[0] + base_ref[0]).astype(F32)
    found = jnp.zeros((128, devices), F32)
    for i in range(tps):
        hit = (slot[i : i + 1] == want) & (sends[i : i + 1] > 0.5)
        found = found + jnp.where(hit, which[i : i + 1], F32(0.0))
    rep, dev = grid_of((reps, devices))
    chosen = small_dot(flag(dev // tps == rep), found, (((1,), (1,)), ((), ())))
    out_ref[...] = chosen.astype(jnp.int32)


def send_lists(dest, reps, turn):
    out = pl.pallas_call(
        send_kernel,
        out_shape=jax.ShapeDtypeStruct((reps, 128), jnp.int32),
        in_specs=[pl.BlockSpec(memory_space=pltpu.SMEM), pl.BlockSpec(memory_space=VM)],
        out_specs=pl.BlockSpec(memory_space=VM),
        cost_estimate=LIGHT,
        name="send_lists",
    )((turn * CAP).astype(jnp.int32).reshape(1), dest)
    return out[:, :CAP].reshape(-1)


def get_kernel(tps, runs, rep_ref, dest_ref, *refs):
    out_ref = refs[-1]
    reps = dest_ref.shape[0]
    devices = reps * tps
    row, col = grid_of((devices, devices))
    same = row // tps == col // tps
    group, below = flag(same), flag(same & (row < col))
    at = grid_of((reps, devices))[1]
    zero = jnp.zeros((reps, devices), F32)
    sends, which = [], []
    for i in range(tps):
        a, w = zero, zero
        for k in range(runs):
            lane = i * runs + k
            hit = flag(dest_ref[:, lane : lane + 1].astype(jnp.int32) == at)
            a = a + hit
            w = w + hit * k
        sends.append(a)
        which.append(w)
    whole = functools.reduce(lambda a, b: a + b, sends)
    r16, c16 = grid_of((reps, reps))
    earlier = small_dot(flag(c16 < r16), whole)
    most = jnp.max(small_dot(whole, group))
    to_me = flag(row == rep_ref[0] * tps + col)
    rank, seen = earlier, zero
    tables = [[None] * tps for _ in range(2)]
    j = grid_of((reps, devices))[1].astype(F32)
    rep_at = grid_of((reps, devices))[0].astype(F32)
    slots, runs_of = [jnp.zeros((1, devices), F32)] * tps, [jnp.zeros((1, devices), F32)] * tps
    sources = [jnp.zeros((1, devices), F32)] * tps
    for i in range(tps):
        slot = seen + small_dot(sends[i], below)
        mine = [small_dot(v, to_me) for v in (sends[i], rank, slot, which[i])]
        for p in range(tps):
            a, r, s, w = (v[:, p : p + 1] for v in mine)
            hit = (r == j) & (a > 0.5)
            get = lambda v: jnp.sum(jnp.where(hit, v, F32(0.0)), axis=0, keepdims=True)
            slots[p] = slots[p] + get(s)
            sources[p] = sources[p] + get(rep_at)
            runs_of[p] = runs_of[p] + get((rep_at * tps + i) * runs + w)
        rank = rank + sends[i]
        seen = seen + small_dot(sends[i], group)
    for p in range(tps):
        slot = slots[p].astype(jnp.int32)
        turn = lax.div(slot, jnp.int32(CAP))
        out_ref[0, p : p + 1, :] = sources[p].astype(jnp.int32) * CAP + slot - turn * CAP
        out_ref[1, p : p + 1, :] = turn
        out_ref[2, p : p + 1, :] = runs_of[p].astype(jnp.int32)
    out_ref[3] = jnp.broadcast_to(most, (tps, devices)).astype(jnp.int32)


def get_lists(dest, rep, tps, runs, after):
    devices = dest.shape[0] * tps
    out = pl.pallas_call(
        functools.partial(get_kernel, tps, runs),
        out_shape=jax.ShapeDtypeStruct((4, tps, devices), jnp.int32),
        in_specs=[pl.BlockSpec(memory_space=pltpu.SMEM), pl.BlockSpec(memory_space=VM)]
        + [pl.BlockSpec(memory_space=ANY)] * len(after),
        out_specs=pl.BlockSpec(memory_space=VM),
        cost_estimate=LIGHT,
        name="get_lists",
    )(rep.astype(jnp.int32).reshape(1), dest, *after)
    tables = out[:, :, :runs].reshape(4, tps * runs)
    return tables[0], tables[1], tables[2], tables[3, 0]


def sum_kernel(parts_ref, *refs):
    total = parts_ref[0].astype(F32)
    for k in range(1, parts_ref.shape[0]):
        total = total + parts_ref[k].astype(F32)
    refs[-1][...] = total


def sum_parts(parts, after):
    return pl.pallas_call(
        sum_kernel,
        out_shape=jax.ShapeDtypeStruct(parts.shape[1:], F32),
        in_specs=[pl.BlockSpec(memory_space=VM)] + [pl.BlockSpec(memory_space=ANY)] * len(after),
        out_specs=pl.BlockSpec(memory_space=VM),
        cost_estimate=LIGHT,
        name="sum",
    )(parts, *after)


def zero_of(a):
    return (a[(0,) * a.ndim].astype(F32) * 0.0).astype(jnp.int32)


def relay(a, chosen, place):
    got = lax.all_to_all(a[chosen], "rep", split_axis=0, concat_axis=0, tiled=True)
    return got[place]


def per_device(
    hidden,
    ref_gain,
    ref_wq,
    ref_wkv,
    ref_wo,
    score_vec,
    lengths,
    advantage,
    dest,
    policy_norm_gain,
    pol_w,
    cotangent,
):
    tps, reps = lax.axis_size("tp"), lax.axis_size("rep")
    tp, rep = lax.axis_index("tp"), lax.axis_index("rep")
    rows, width = hidden.shape
    model = width * tps
    outs = pol_w.shape[1]
    runs_dev = dest.shape[0] // RUN
    swap, up, down, across = tp_moves(tps)
    starts = [sum(PARTS[:k]) for k in range(len(PARTS))]
    spot = jnp.stack([tp // 2, lax.rem(tp, 2)]).astype(jnp.int32)
    full = lax.all_gather(hidden, "tp", axis=1, tiled=True)

    own = hidden.astype(F32)
    squares = jnp.sum(own * own, axis=1)
    run_own = jnp.pad(dest.reshape(runs_dev, RUN)[:, 0].astype(F32), (0, 128 - runs_dev))
    both = spread(jnp.concatenate([squares, run_own]), "tp")
    inv = lax.rsqrt(jnp.sum(both[:, :rows], axis=0) / model + EPS)
    run_rep = both[:, rows : rows + runs_dev].astype(jnp.int32)
    chosen = send_lists(run_rep, reps, jnp.int32(0))

    cols = outs // tps
    w_rows = pol_w.shape[0]
    turned = lax.ppermute(
        pol_w, ("rep", "tp"), [(t * reps + k, k * tps + t) for t in range(tps) for k in range(reps)]
    )
    line = jnp.pad(run_rep.reshape(1, -1).astype(BF), ((0, 7), (0, outs - tps * runs_dev)))
    spread_w = spread(jnp.concatenate([turned, line], axis=0), "rep")
    w_slice = spread_w[:, :w_rows].reshape(width, outs)
    run_all = spread_w[:, w_rows, : tps * runs_dev]

    gain = lax.dynamic_slice_in_dim(policy_norm_gain, tp * width, width, 0)[None]
    w_in = jnp.concatenate([ref_wq, ref_wkv.reshape(model, -1)], axis=1)
    y_keep, y_give = project(spot, hidden, gain, w_slice, tps, ())
    y_sums = pair_sums(y_keep, lax.ppermute(y_give, "tp", swap), (w_in,))
    y_parts = [y_sums[0]] + [lax.ppermute(y_sums[s], "tp", m) for s, m in ((1, up), (2, across), (3, down))]

    x_runs = hidden.reshape(rows // RUN, RUN, width)
    x_sent = x_runs[chosen]
    x_got = lax.all_to_all(x_sent, "rep", split_axis=0, concat_axis=0, tiled=True)

    inv_col = inv[:, None]

    xn = (full.astype(F32) * inv_col * ref_gain).astype(BF)
    qkv = jnp.dot(xn, w_in, preferred_element_type=F32).astype(BF)
    ends = jnp.cumsum(lengths[0])
    attn = attention(ends, qkv, ref_wq.shape[1], (x_sent, *y_parts))
    mine = tp.astype(jnp.int32).reshape(1)
    parts = len(PARTS)
    cot_all = lax.all_gather(cotangent, "tp", axis=0, tiled=True)
    held = [outproj(spot, attn, ref_wo, tps, k, parts, (cot_all,) if k else ()) for k in range(parts)]
    merged = [
        merge(keep, lax.ppermute(give, "tp", swap), keep.shape[0] // 4, tuple(h[0] for h in held)) for keep, give in held
    ]
    place, turn_of, got_run, most = get_lists(run_all, rep, tps, runs_dev, (merged[-1][0],))
    sums = [ring_sum(m, up, down) for m in merged]
    stages = [stage for _, stage in sums]
    y_runs = pack(y_parts, [inv_col], (x_got, stages[0][1], place)).reshape(rows // RUN, RUN, 128)
    weights = [
        token_weights(
            mine,
            ends,
            advantage[0],
            lax.dynamic_slice_in_dim(full, start + tp * (size // tps), size // tps, 0),
            score_vec[None],
            *stage,
            start,
        )[:1]
        for stage, start, size in zip(stages, starts, PARTS, strict=True)
    ]

    y_got = lax.all_to_all(
        y_runs[chosen], "rep", split_axis=0, concat_axis=0, tiled=True
    )

    def later_turns(a, held, begin):
        def again(state):
            turn, now = state
            came = relay(a, send_lists(run_rep, reps, turn), place)
            return turn + 1, jnp.where((turn_of == turn)[:, None, None], came, now)

        return lax.while_loop(lambda state: state[0] * CAP < most, again, (begin, held))[1]

    y_pol = later_turns(y_runs, y_got[place + zero_of(sums[-1][0])], jnp.int32(1)).reshape(rows, 128)
    x_pol = later_turns(x_runs, x_got[place], jnp.int32(1)).reshape(rows, width)
    inv_pol = y_pol[:, cols : cols + 1].astype(F32) + y_pol[:, cols + 1 : cols + 2].astype(F32)
    y_all = lax.all_gather(y_pol[:, :cols], "tp", axis=1, tiled=True)

    w_mine = jnp.concatenate(weights, axis=1).astype(BF)
    w_all = spread(w_mine.reshape(-1), ("rep", "tp"))
    cols_of = (tps, runs_dev, tuple(zip(starts, PARTS, strict=True)))

    dx_give, dx_keep, gw = policy(spot, tps, model, cols_of, got_run[None], w_all, inv_pol, y_all, cot_all, x_pol, gain, w_slice)

    parts = lax.all_to_all(gw.reshape(reps, w_rows, outs), "rep", split_axis=0, concat_axis=0, tiled=True)

    x, c = spot[0], spot[1]
    n = tps // 2
    dx_took = lax.ppermute(dx_give, "tp", swap)
    pieces, places = [], []
    for s, move in ((1, up), (3, down), (2, across), (0, None)):
        pair = [dx_keep[s], dx_took[s]]
        if move is not None:
            pair = [lax.ppermute(v, "tp", move) for v in pair]
        origin = lax.rem(x - s + n, n) * 2
        pieces += pair
        places += [origin + c, origin + 1 - c]
    places = jnp.stack(places).astype(jnp.int32)
    policy_input_gradient = place_columns(places, pieces)

    back = [(k * tps + t, t * reps + k) for t in range(tps) for k in range(reps)]
    total = sum_parts(parts, (pieces[5],))
    grad_weight = lax.ppermute(total, ("rep", "tp"), back)
    gain_own = lax.dynamic_slice_in_dim(policy_norm_gain, (rep * tps + tp) * w_rows, w_rows, 0)
    policy_gain_gradient = jnp.sum(grad_weight * pol_w.astype(F32), axis=1) / gain_own
    return (policy_input_gradient, grad_weight, policy_gain_gradient)


def solution(mesh):
    return jax.shard_map(
        per_device,
        mesh=mesh,
        in_specs=(
            P("rep", "tp"),
            P(),
            P(None, "tp"),
            P(None, None, "tp"),
            P("tp", None),
            P(),
            P("rep", None),
            P("rep", None),
            P(("rep", "tp")),
            P(),
            P(("rep", "tp"), None),
            P(("rep", "tp"), None),
        ),
        out_specs=(P(("rep", "tp"), None), P(("rep", "tp"), None), P(("rep", "tp"))),
        check_vma=False,
    )
```
